512 devices in a mesh: dp: 32 (over z_hi, x, y), expert: 16 (over z_lo, core).
Axes of the slice: x: 4, y: 4, z: 16 (z_hi: 2, z_lo: 8; z = z_hi * 8 + z_lo), core: 2. Of those that a mesh axis runs over, the one named last changes fastest.
Arguments:
- frames: bfloat16 [12288, 1024], P('dp'), may hold values from -6 to 6
- norm_gain: float32 [1024], replicated, may hold values from 0.1 to 1.9
- router: float32 [1024, 32], replicated, may hold values from -0.1875 to 0.1875
- routes: int32 [12288, 2], P('dp'), may hold values from 0 to 31, all different within a row; in each aligned block of 384 rows (0 to 383, 384 to 767, ...) at most 32 rows name the same one
- w_in: bfloat16 [32, 1024, 4096], P('dp', None, 'expert'), may hold values from -0.25 to 0.25
- w_out: bfloat16 [32, 4096, 1024], P('dp', 'expert'), may hold values from -0.125 to 0.125
- cotangent: bfloat16 [12288, 1024], P('dp', 'expert'), may hold values from -6 to 6
Outputs:
- mixed_out: bfloat16 [12288, 1024], P('dp', 'expert')
- d_frames: bfloat16 [12288, 1024], P('dp', 'expert')
- d_gain: float32 [1024], P('expert')
- d_router: float32 [1024, 32], replicated
- grad_in: bfloat16 [32, 1024, 4096], P('dp', None, 'expert')
- grad_out: bfloat16 [32, 4096, 1024], P('dp', 'expert')
The draws below stay inside these ranges and needn't reach their ends.
Inputs may be any that keep to these rules, and one draw needn't show every extreme that they name: `routes`: each row names 2 different experts; among the rows of one device no expert is named more than 32 times, a bound that some block reaches.
All inputs are finite; a program needn't handle non-finite values.
Results may differ from the reference program's by a relative error of at most 0.023.
Values may be sent and summed in bfloat16 or wider, within the bound.
A program may use at most 64 MiB of HBM per device.

```python
import math
import jax
import jax.numpy as jnp
import numpy as np
from jax import lax

D = 1024
FF = 4096
TOPK = 2
TOK_DEV = 384
EXPERTS = 32
CAP = 32
TOKENS = 12288
N_DP = 32
N_EXPERT = 16


def raised(array, rng, source, target, shards_of, factor):
    owner, partner = [(jnp.arange(array.shape[dim]) // (array.shape[dim] // shards_of)).reshape([-1 if axis == dim else 1 for axis in range(array.ndim)]) for dim in (source, target)]
    chosen = jax.random.permutation(rng, shards_of)[partner]
    strong = (owner == chosen) | (owner == (partner + shards_of // 2) % shards_of)
    return jnp.where(strong, factor * array, array)


def level_of(own_key, shape, cuts, least, high):
    def one(dim, blocks):
        draws = jax.random.uniform(jax.random.fold_in(jax.random.fold_in(own_key, 6), dim), (blocks,), jnp.float32, least / len(cuts), high / len(cuts))
        return jnp.repeat(jnp.exp(draws), shape[dim] // blocks).reshape((-1,) + (1,) * (len(shape) - dim - 1))

    loudness = one(*cuts[0])
    for cut in cuts[1:]:
        loudness = loudness * one(*cut)
    return loudness


def routed_block(own_key, own, number, rows, amount, top, bound, slope):
    ranking = jax.random.permutation(own_key, amount)
    heavy_load, usual = portions_of(amount, rows * top, bound, slope, True), portions_of(amount, rows * top, bound, slope, False)
    places = jnp.arange(amount)

    def named(lengths, turn):
        used = int((lengths > 0).sum())
        fixed = max(1, used // 4)
        shifted = fixed + (places - fixed + turn * (used - fixed)) % max(1, amount - fixed)
        return jnp.zeros((amount,), jnp.int32).at[ranking[jnp.where(places < fixed, places, shifted)]].set(jnp.asarray(lengths, jnp.int32))

    lengths = jnp.where(number % 4 == 0, named(heavy_load, number // 4), named(usual, number - number // 4 - 1))
    mixed = jax.random.permutation(jax.random.fold_in(own, 3), amount)
    source_of, sink = mixed[0:amount // 2 * 2:2], mixed[1:amount // 2 * 2:2]
    room = jnp.minimum(lengths[source_of] - 1, bound - lengths[sink]) // 2
    room = jnp.where((source_of == ranking[0]) | (sink == ranking[0]) | (lengths[sink] == 0), 0, jnp.maximum(room, 0))
    shifted = jax.random.randint(jax.random.fold_in(own, 4), (amount // 2,), 0, 1 << 20) % (room + 1)
    lengths = lengths.at[source_of].add(-shifted).at[sink].add(shifted)
    items = jnp.searchsorted(jnp.cumsum(lengths), jnp.arange(rows * top), side="right").astype(jnp.int32)
    table = items.reshape(top, rows).T
    table = table[jax.random.permutation(jax.random.fold_in(own, 1), rows)]
    turn = jax.random.randint(jax.random.fold_in(own, 2), (rows, 1), 0, top)
    return jnp.take_along_axis(table, (jnp.arange(top)[None, :] + turn) % top, axis=1)


def portions_of(count, total, reach, lean, full):
    portions = [(1 << 20) // math.isqrt(grade ** lean) + 1 for grade in range(1, count + 1)]
    largest = reach if full else min(reach, max(-(-total // count), total * portions[0] // sum(portions)))
    least = 1 if total - largest >= count - 1 else 0
    holding, surplus = [largest] + [least] * (count - 1), total - largest - least * (count - 1)
    while surplus > 0:
        movable = [i for i in range(1, count) if holding[i] < largest] or [i for i in range(1, count) if holding[i] < reach]
        pool, remaining = sum([portions[i] for i in movable]), surplus
        for i in movable:
            addition = min(reach - holding[i], max(1, remaining * portions[i] // pool), surplus)
            holding[i] = holding[i] + addition
            surplus = surplus - addition
    return np.array(holding)


def scatter_about(rng, dims, deviation, reach, cuts=(), kind=jnp.bfloat16):
    level = level_of(rng, dims, cuts, -0.22, 0.18) if cuts else 1.0
    drawn = jax.random.normal(rng, dims, jnp.float32) * deviation * level
    return jnp.minimum(jnp.maximum(drawn, -reach), reach).astype(kind)


def heavy_noise(stream_key, extent, spread, limit, cuts, heavy, kind=jnp.bfloat16):
    result = spread * jax.random.normal(stream_key, extent, jnp.float32)
    if cuts:
        result = result * level_of(stream_key, extent, cuts, -0.22, 0.18)
    return jnp.clip(raised(result, jax.random.fold_in(stream_key, 3), *heavy), -limit, limit).astype(kind)


def setup_inputs(seed: int = 0) -> dict:
    key_list = jax.random.split(jax.random.key(seed), 8)
    frames = scatter_about(key_list[0], (TOKENS, D), 1.0, 6.0, ((0, 32),))
    norm_gain = jnp.clip(1.0 + 0.18 * jax.random.normal(key_list[1], (D,), jnp.float32), 0.1, 1.9)
    router = scatter_about(key_list[2], (D, EXPERTS), D ** -0.5, 0.1875, (), jnp.float32)
    routes_keys = jax.random.split(jax.random.fold_in(key_list[3], 1), TOKENS // TOK_DEV)
    routes_turns = jax.random.permutation(jax.random.fold_in(key_list[3], 3), TOKENS // TOK_DEV)
    routes = jax.vmap(lambda own, number: routed_block(jax.random.fold_in(key_list[3], 2), own, number, TOK_DEV, EXPERTS, TOPK, CAP, 2))(routes_keys, routes_turns).reshape((TOKENS, TOPK))
    w_in = heavy_noise(key_list[4], (EXPERTS, D, FF), D ** -0.5, 0.25, ((0, 32), (2, 16)), (2, 1, 16, 2.0))
    w_out = heavy_noise(key_list[5], (EXPERTS, FF, D), FF ** -0.5, 0.125, ((0, 32), (1, 16)), (1, 2, 16, 2.0))
    cotangent = scatter_about(key_list[6], (TOKENS, D), 1.0, 6.0, ((0, 32), (1, 16)))
    return {"frames": frames, "norm_gain": norm_gain, "router": router, "routes": routes, "w_in": w_in, "w_out": w_out, "cotangent": cotangent}


epsilon = 1e-05

def silu_slope(hidden):
    sigmoid_h = jax.nn.sigmoid(hidden)
    return sigmoid_h * (1.0 + hidden * (1.0 - sigmoid_h))

def round_trip(values):
    rounded = lax.optimization_barrier(values.astype(jnp.bfloat16))
    return rounded.astype(jnp.float32)

def reference(frames, norm_gain, router, routes, w_in, w_out, cotangent):
    values = frames.astype(jnp.float32)
    centred = values - lax.optimization_barrier(jnp.mean(values, axis=1, keepdims=True))
    inverse = lax.rsqrt(lax.optimization_barrier(jnp.mean(centred * centred, axis=1, keepdims=True)) + epsilon)
    scaled = centred * inverse
    normed = (scaled * norm_gain).astype(jnp.bfloat16)
    logits = jnp.dot(normed.astype(jnp.float32), router, precision=lax.Precision.HIGHEST)
    gate_values = jax.nn.sigmoid(jnp.take_along_axis(logits, routes, axis=1))
    blocks = routes.reshape(N_DP, TOK_DEV * TOPK)
    onehot = (blocks[:, :, None] == jnp.arange(EXPERTS, dtype=jnp.int32)[None, None, :]).astype(jnp.int32)
    slot_ids = lax.optimization_barrier(jnp.sum((jnp.cumsum(onehot, axis=1) - onehot) * onehot, axis=2)).reshape(TOKENS, TOPK)
    source = (jnp.arange(TOKENS, dtype=jnp.int32) // TOK_DEV)[:, None]
    position = (routes * (N_DP * CAP) + source * CAP + slot_ids).reshape(TOKENS * TOPK).astype(jnp.int32)
    total_rows = EXPERTS * N_DP * CAP
    dispatched = jnp.zeros((total_rows, D), jnp.bfloat16).at[position].set(jnp.repeat(normed, TOPK, axis=0))
    cot_values = cotangent.astype(jnp.float32)
    grad_rows = (0.5 * gate_values[:, :, None] * cot_values[:, None, :]).astype(jnp.bfloat16)
    grad_buffer = jnp.zeros((total_rows, D), jnp.bfloat16).at[position].set(grad_rows.reshape(TOKENS * TOPK, D))
    unit_width = FF // N_EXPERT

    def per_expert(operands):
        arrived, incoming, weight_in, weight_out = operands
        hidden = jnp.dot(arrived, weight_in, preferred_element_type=jnp.float32)
        active = jax.nn.silu(hidden).astype(jnp.bfloat16)
        block_terms = jnp.einsum('rbf,bfd->brd', active.reshape(-1, N_EXPERT, unit_width).astype(jnp.float32), weight_out.reshape(N_EXPERT, unit_width, D).astype(jnp.float32))
        produced = lax.optimization_barrier(jnp.sum(round_trip(block_terms), axis=0)).astype(jnp.bfloat16)
        upstream = jnp.dot(incoming, weight_out.T, preferred_element_type=jnp.float32)
        d_hidden = (upstream * silu_slope(hidden)).astype(jnp.bfloat16)
        grad_out = jnp.dot(active.T, incoming, preferred_element_type=jnp.float32).astype(jnp.bfloat16)
        grad_in = jnp.dot(arrived.T, d_hidden, preferred_element_type=jnp.float32).astype(jnp.bfloat16)
        back_terms = jnp.einsum('rbf,dbf->brd', d_hidden.reshape(-1, N_EXPERT, unit_width).astype(jnp.float32), weight_in.reshape(D, N_EXPERT, unit_width).astype(jnp.float32))
        returned = lax.optimization_barrier(jnp.sum(round_trip(back_terms), axis=0)).astype(jnp.bfloat16)
        return (produced, returned, grad_in, grad_out)
    produced, returned, grad_in, grad_out = lax.map(per_expert, (dispatched.reshape(EXPERTS, N_DP * CAP, D), grad_buffer.reshape(EXPERTS, N_DP * CAP, D), w_in, w_out))
    picked = produced.reshape(total_rows, D)[position].reshape(TOKENS, TOPK, D).astype(jnp.float32)
    mixed_out = (values + 0.5 * lax.optimization_barrier(jnp.sum(gate_values[:, :, None] * picked, axis=1))).astype(jnp.bfloat16)
    d_moe = lax.optimization_barrier(jnp.sum(returned.reshape(total_rows, D)[position].reshape(TOKENS, TOPK, D).astype(jnp.float32), axis=1))
    d_gate = 0.5 * lax.optimization_barrier(jnp.sum(cot_values[:, None, :] * picked, axis=2))
    d_chosen = d_gate * gate_values * (1.0 - gate_values)
    selector = (routes[:, :, None] == jnp.arange(EXPERTS, dtype=jnp.int32)[None, None, :]).astype(jnp.float32)
    d_logits = lax.optimization_barrier(jnp.sum(selector * d_chosen[:, :, None], axis=1))
    d_normed = d_moe + jnp.dot(d_logits, router.T, precision=lax.Precision.HIGHEST)
    d_router = jnp.dot(normed.astype(jnp.float32).T, d_logits, precision=lax.Precision.HIGHEST) / TOK_DEV
    d_gain = lax.optimization_barrier(jnp.sum(d_normed * scaled, axis=0)) / TOK_DEV
    d_scaled = d_normed * norm_gain
    d_frames = cot_values + inverse * (d_scaled - lax.optimization_barrier(jnp.mean(d_scaled, axis=1, keepdims=True)) - scaled * lax.optimization_barrier(jnp.mean(d_scaled * scaled, axis=1, keepdims=True)))
    return (mixed_out, d_frames.astype(jnp.bfloat16), d_gain, d_router, grad_in, grad_out)
```

```python
import functools

import jax
import jax.numpy as jnp
from jax import lax
from jax.experimental import pallas as pl
from jax.experimental.pallas import tpu as pltpu
from jax.sharding import PartitionSpec as P

EPS = 1e-05
F32 = jnp.float32
BF16 = jnp.bfloat16
MESH = pl.DeviceIdType.MESH
NN = (((1,), (0,)), ((), ()))
NT = (((1,), (1,)), ((), ()))


def dot(a, b, dims=NN):
    return lax.dot_general(a, b, dims, preferred_element_type=F32)


def loop(lo, hi, body):
    def step(i, carry):
        body(i)
        return carry

    lax.fori_loop(lo, hi, step, 0)


def kernel(
    dims,
    frames,
    gain,
    routerT,
    routesT,
    w_in,
    w_out,
    cot,
    mixed,
    dfr,
    vout,
    gin,
    gout,
    rt,
    nb,
    cotb,
    sibcot,
    stats,
    p0t,
    p1t,
    pcomb,
    send_n,
    send_c,
    rows_a,
    rows_c,
    ga_t,
    d_t,
    prodb,
    retb,
    sib_p,
    sib_r,
    got_p,
    got_r,
    part,
    ring,
    scal,
    vw,
    sibvw,
    vz,
    vp,
    tail,
    sib_s,
    sib_q,
    rt_sem,
    nrm_s,
    nrm_q,
    cot_r,
    cot_l,
    cot_q,
    xy_s,
    xy_q,
    rs_s,
    rs_q,
    sc_s,
    sc_q,
    vz_s,
    vz_q,
):
    X, Y, ZL = dims
    NP = X * Y
    NZ = 2 * ZL
    T, D = frames.shape
    SL = send_n.shape[0]
    CAP = SL // NP
    E = routerT.shape[0]
    W = 128
    dp = lax.axis_index("dp")
    ex = lax.axis_index("expert")
    p = lax.rem(dp, NP)
    zh = dp // NP
    zl = ex // 2
    c = lax.rem(ex, 2)
    z = zh * ZL + zl
    x = p // Y
    y = lax.rem(p, Y)
    r = lax.rem(z + NZ - ZL * c, NZ)
    own = r < ZL
    sib_id = (dp, zl * 2 + 1 - c)

    def z_id(to):
        return ((to // ZL) * NP + p, lax.rem(to, ZL) * 2 + c)

    right = z_id(lax.rem(z + 1, NZ))
    left = z_id(lax.rem(z + NZ - 1, NZ))

    def plane(k, sign):
        px = lax.rem(x + X + sign * (k // Y), X)
        py = lax.rem(y + Y + sign * lax.rem(k, Y), Y)
        return px * Y + py

    def plane_id(k):
        return (zh * NP + plane(k, 1), ex)

    def remote(src, dst, ssem, rsem, to):
        return pltpu.make_async_remote_copy(
            src_ref=src, dst_ref=dst, send_sem=ssem, recv_sem=rsem, device_id=to, device_id_type=MESH
        )

    def sib(src, dst, i):
        return remote(src, dst, sib_s.at[i], sib_q.at[i], sib_id)

    barrier = pltpu.get_barrier_semaphore()

    def greet(to):
        pl.semaphore_signal(barrier, inc=1, device_id=to, device_id_type=MESH)

    greet(sib_id)
    loop(1, NP, lambda k: greet(plane_id(k)))
    loop(1, NZ, lambda k: greet(z_id(lax.rem(z + k, NZ))))

    @pl.when(own)
    def _():
        step = T // 8

        def norm(i):
            at = pl.ds(pl.multiple_of(i * step, step), step)
            values = frames[at, :].astype(F32)
            mean = jnp.mean(values, axis=1, keepdims=True)
            centred = values - mean
            inverse = lax.rsqrt(jnp.mean(centred * centred, axis=1, keepdims=True) + EPS)
            normed = (centred * inverse * gain[...]).astype(BF16)
            for s in range(ZL):
                nb[s, at, :] = normed[:, s * W : (s + 1) * W]
            stats[0, at, :] = jnp.broadcast_to(mean, (step, W))
            stats[1, at, :] = jnp.broadcast_to(inverse, (step, W))

        loop(0, 8, norm)
        rt[...] = routesT[...]

    pl.semaphore_wait(barrier, NP + NZ - 1)

    cot_copy = sib(cot, sibcot, 0)
    rt_copy = remote(rt, rt, rt_sem.at[0], rt_sem.at[1], z_id(lax.rem(z + ZL, NZ)))

    def nrm(s, to):
        return remote(nb.at[s], nb.at[s], nrm_s.at[s], nrm_q.at[s], to)

    def cot_piece(s, sems, to):
        return remote(cotb.at[s], cotb.at[s], sems.at[s], cot_q.at[s], to)

    def cot_step(j, run):
        piece = lax.rem(r + NZ - j, NZ)

        @pl.when(piece < ZL)
        def _():
            s = lax.rem(piece, ZL)
            if run:
                pl.when(j >= 1)(lambda: cot_piece(s, cot_r, right).wait_recv())
            pl.when(j < ZL)(
                lambda: cot_piece(s, cot_r, right).start()
                if run
                else cot_piece(s, cot_r, right).wait_send()
            )

        other = lax.rem(r + j, NZ)

        @pl.when((other < ZL) & (j < ZL))
        def _():
            s = lax.rem(other, ZL)
            if run:
                pl.when(j >= 1)(lambda: cot_piece(s, cot_l, left).wait_recv())
            pl.when(j < ZL - 1)(
                lambda: cot_piece(s, cot_l, left).start()
                if run
                else cot_piece(s, cot_l, left).wait_send()
            )

    def positions():
        r0 = rt[0:1, :].astype(F32)
        r1 = rt[1:2, :].astype(F32)
        lanes = lax.broadcasted_iota(jnp.int32, (E, T), 0).astype(F32)
        e0 = jnp.where(lanes == r0, 1.0, 0.0)
        e1 = jnp.where(lanes == r1, 1.0, 0.0)
        before = lax.broadcasted_iota(jnp.int32, (T, T), 0) < lax.broadcasted_iota(
            jnp.int32, (T, T), 1
        )
        counts = dot((e0 + e1).astype(BF16), jnp.where(before, 1.0, 0.0).astype(BF16))
        base = (zh * NP).astype(F32)
        for rk, ek, pt, first in ((r0, e0, p0t, True), (r1, e1, p1t, False)):
            slot = jnp.sum(ek * counts, axis=0, keepdims=True)
            pos = (rk - base) * CAP + slot
            posc = jnp.transpose(jnp.broadcast_to(pos, (W, T)))
            for b in range(SL // W):
                down = (lax.broadcasted_iota(jnp.int32, (W, T), 0) + b * W).astype(F32)
                pt[b * W : (b + 1) * W, :] = jnp.where(down == pos, 1.0, 0.0).astype(BF16)
                across = (lax.broadcasted_iota(jnp.int32, (T, W), 1) + b * W).astype(F32)
                hit = jnp.where(across == posc, 1.0, 0.0).astype(BF16)
                if first:
                    pcomb[:, b * W : (b + 1) * W] = hit
                else:
                    pcomb[:, b * W : (b + 1) * W] += hit

    def xy(a, src, dst, at, k):
        return remote(
            src.at[pl.ds(pl.multiple_of(plane(k, 1) * CAP, CAP), CAP)],
            dst.at[pl.ds(pl.multiple_of(at + p * CAP, CAP), CAP)],
            xy_s.at[a, k],
            xy_q.at[a, k],
            plane_id(k),
        )

    def xy_arrival(a, dst, at, k):
        here = dst.at[pl.ds(pl.multiple_of(at + plane(k, -1) * CAP, CAP), CAP)]
        return remote(here, here, xy_s.at[a, k], xy_q.at[a, k], plane_id(k))

    def dispatch(a, pieces, send, dst):
        pt = p0t[...] + p1t[...]

        def one(s):
            send[:, pl.ds(pl.multiple_of(s * W, W), W)] = dot(pt, pieces[s]).astype(BF16)

        loop(0, ZL, one)
        loop(1, NP, lambda k: xy(a, send, dst, c * SL, k).start())
        mine = pl.ds(pl.multiple_of(p * CAP, CAP), CAP)
        dst[pl.ds(pl.multiple_of(c * SL + p * CAP, CAP), CAP), :] = send[mine, :]

    @pl.when(own)
    def _():
        rt_copy.start()
        pl.when(r == ZL - 1)(lambda: loop(0, ZL, lambda s: nrm(s, right).start()))
        pl.when(r == 0)(lambda: loop(0, ZL, lambda s: nrm(s, left).start()))
        cot_copy.wait_recv()
        one, two = cot[...], sibcot[...]

        @pl.when(c == 0)
        def _():
            cotb[r, :, :] = jnp.concatenate([one, two], axis=1)

        @pl.when(c == 1)
        def _():
            cotb[r, :, :] = jnp.concatenate([two, one], axis=1)

        cot_step(0, True)
        positions()
        dispatch(0, nb, send_n, rows_a)
        loop(1, ZL + 1, lambda j: cot_step(j, True))

    @pl.when(jnp.logical_not(own))
    def _():
        cot_copy.start()
        rt_copy.wait_recv()
        positions()

        def step(i):
            near = r < ZL + ZL // 2

            @pl.when(near)
            def _():
                nrm(i, right).wait_recv()
                pl.when(r < ZL + ZL // 2 - 1)(lambda: nrm(i, right).start())

            @pl.when(jnp.logical_not(near))
            def _():
                nrm(i, left).wait_recv()
                pl.when(r > ZL + ZL // 2)(lambda: nrm(i, left).start())

            cot_step(i + 1, True)

        loop(0, ZL, step)
        dispatch(0, nb, send_n, rows_a)

    dispatch(1, cotb, send_c, rows_c)

    half = pl.ds(pl.multiple_of(c * SL, SL), SL)
    a_copy = sib(rows_a.at[half], rows_a.at[half], 1)
    c_copy = sib(rows_c.at[half], rows_c.at[half], 2)
    loop(1, NP, lambda k: xy_arrival(0, rows_a, c * SL, k).wait_recv())
    a_copy.start()
    loop(1, NP, lambda k: xy_arrival(1, rows_c, c * SL, k).wait_recv())
    c_copy.start()

    gain_hi = gain[...].astype(BF16)
    gain_lo = (gain[...] - gain_hi.astype(F32)).astype(BF16)
    weight_in = w_in[...]
    weight_out = w_out[...]
    gw = (
        dot(jnp.broadcast_to(gain_hi, (16, D)), weight_in)
        + dot(jnp.broadcast_to(gain_lo, (16, D)), weight_in)
    )[0:1, :]
    router_row = routerT[pl.ds(dp, 1), :]
    router_hi = router_row.astype(BF16)
    router_lo = (router_row - router_hi.astype(F32)).astype(BF16)
    router_hi = jnp.broadcast_to(router_hi, (16, D))
    router_lo = jnp.broadcast_to(router_lo, (16, D))
    vw[...] = jnp.zeros_like(vw)
    RT = 128
    lane = lax.broadcasted_iota(jnp.int32, (RT, W), 1)

    def expert_tile(i):
        at = pl.ds(pl.multiple_of(i * RT, RT), RT)
        arrived = rows_a[at, :]
        cots = rows_c[at, :]
        hidden = dot(arrived, weight_in)
        logit = dot(arrived, router_hi, NT) + dot(arrived, router_lo, NT)
        gate = jax.nn.sigmoid(logit[:, 0:1])
        sig = jax.nn.sigmoid(hidden)
        active = hidden * sig
        up = dot(cots, weight_out, NT) * (0.5 * gate)
        ga = active.astype(BF16).astype(F32) * (0.5 * gate)
        dh = up * (sig * (1.0 + hidden * (1.0 - sig)))
        dh_b = dh.astype(BF16)
        ga_b = ga.astype(BF16)
        ga_t[:, at] = jnp.transpose(ga).astype(BF16)
        d_t[:, at] = jnp.transpose(dh).astype(BF16)
        dgg = jnp.sum(up * active, axis=1, keepdims=True)
        s1 = jnp.sum(dh * gw, axis=1, keepdims=True)
        s2 = jnp.sum(dh * hidden, axis=1, keepdims=True)
        prodb[at, :] = dot(ga_b, weight_out).astype(BF16)
        back = dot(dh_b, weight_in, NT)
        retb[at, 0:D] = back.astype(BF16)
        retb[at, D : D + W] = jnp.where(
            lane == 0, dgg, jnp.where(lane == 1, s1, jnp.where(lane == 2, s2, 0.0))
        ).astype(BF16)
        wide = arrived.astype(F32)
        v = jnp.sum(wide * (dgg * (1.0 - gate)), axis=0, keepdims=True)
        w = jnp.sum(wide * back, axis=0, keepdims=True)
        for b in range(D // W):
            vw[0, b : b + 1, :] += v[:, b * W : (b + 1) * W]
            vw[1, b : b + 1, :] += w[:, b * W : (b + 1) * W]

    tiles = SL // RT
    away = pl.ds(pl.multiple_of((1 - c) * SL, SL), SL)
    p_copy = sib(prodb.at[away], sib_p, 3)
    r_copy = sib(retb.at[away], sib_r, 4)
    sib(rows_a.at[away], rows_a.at[away], 1).wait_recv()
    sib(rows_c.at[away], rows_c.at[away], 2).wait_recv()
    loop(0, tiles, lambda i: expert_tile((1 - c) * tiles + i))
    p_copy.start()
    r_copy.start()
    loop(0, tiles, lambda i: expert_tile(c * tiles + i))
    v_copy = sib(vw.at[1 - c], sibvw, 5)
    v_copy.start()

    def pair_sum(i):
        at = pl.ds(pl.multiple_of(i * RT, RT), RT)
        mine = pl.ds(pl.multiple_of(c * SL + i * RT, RT), RT)
        prodb[mine, :] = (prodb[mine, :].astype(F32) + sib_p[at, :].astype(F32)).astype(BF16)

    def pair_sum_r(i):
        at = pl.ds(pl.multiple_of(i * RT, RT), RT)
        mine = pl.ds(pl.multiple_of(c * SL + i * RT, RT), RT)
        retb[mine, :] = (retb[mine, :].astype(F32) + sib_r[at, :].astype(F32)).astype(BF16)

    def give(a, src, dst, k):
        return remote(
            src.at[pl.ds(pl.multiple_of(c * SL + plane(k, 1) * CAP, CAP), CAP)],
            dst.at[pl.ds(pl.multiple_of(p * CAP, CAP), CAP)],
            xy_s.at[a, k],
            xy_q.at[a, k],
            plane_id(k),
        )

    mine_rows = pl.ds(pl.multiple_of(c * SL + p * CAP, CAP), CAP)
    here_rows = pl.ds(pl.multiple_of(p * CAP, CAP), CAP)
    r_copy.wait_recv()
    loop(0, tiles, pair_sum_r)
    loop(1, NP, lambda k: give(3, retb, got_r, k).start())
    got_r[here_rows, :] = retb[mine_rows, :]
    p_copy.wait_recv()
    loop(0, tiles, pair_sum)
    loop(1, NP, lambda k: give(2, prodb, got_p, k).start())
    got_p[here_rows, :] = prodb[mine_rows, :]

    v_copy.wait_recv()
    vz[z, :, :] = vw[c, :, :] + sibvw[...]

    def v_send(k):
        return remote(vz.at[z], vz.at[z], vz_s.at[0, k], vz_q.at[0, k], z_id(lax.rem(z + k, NZ)))

    def v_arrival(k):
        here = vz.at[lax.rem(z + NZ - k, NZ)]
        return remote(here, here, vz_s.at[0, k], vz_q.at[0, k], z_id(lax.rem(z + k, NZ)))

    loop(1, NZ, lambda k: v_send(k).start())

    def grads(i):
        at = pl.ds(pl.multiple_of(i * W, W), W)
        gout[:, at] = dot(ga_t[...], rows_c[:, at]).astype(BF16)
        gin[at, :] = jnp.transpose(dot(d_t[...], rows_a[:, at])).astype(BF16)

    loop(0, D // W, grads)

    loop(1, NZ, lambda k: v_arrival(k).wait_recv())
    vp[p, 0, :, :] = jnp.sum(vz[0:ZL], axis=0)
    vp[p, 1, :, :] = jnp.sum(vz[ZL:NZ], axis=0)

    def vp_send(k):
        return remote(vp.at[p], vp.at[p], vz_s.at[1, k], vz_q.at[1, k], plane_id(k))

    def vp_arrival(k):
        here = vp.at[plane(k, -1)]
        return remote(here, here, vz_s.at[1, k], vz_q.at[1, k], plane_id(k))

    loop(1, NP, lambda k: vp_send(k).start())

    def ring_copy(a, d, s):
        src = part.at[a, d, s]
        return remote(
            src, ring.at[a, d, s], rs_s.at[a, d, s], rs_q.at[a, d, s], right if d == 0 else left
        )

    def combine(a, got):
        def one(s):
            at = pl.ds(pl.multiple_of(s * W, W), W)
            value = dot(pcomb[...], got[:, at]).astype(BF16)
            part[a, 0, s, :, :] = value
            part[a, 1, s, :, :] = value

        loop(0, ZL, one)

    def ring_step(a, j, run):
        to_r = lax.rem(r + ZL - j, NZ)

        @pl.when(to_r < ZL)
        def _():
            s = lax.rem(to_r, ZL)
            if run:

                @pl.when(j >= 1)
                def _():
                    ring_copy(a, 0, s).wait_recv()
                    part[a, 0, s, :, :] = (
                        part[a, 0, s, :, :].astype(F32) + ring[a, 0, s, :, :].astype(F32)
                    ).astype(BF16)

                ring_copy(a, 0, s).start()
            else:
                ring_copy(a, 0, s).wait_send()

        to_l = lax.rem(r + NZ - ZL + 1 + j, NZ)

        @pl.when((to_l < ZL) & (j < ZL - 1))
        def _():
            s = lax.rem(to_l, ZL)
            if run:

                @pl.when(j >= 1)
                def _():
                    ring_copy(a, 1, s).wait_recv()
                    part[a, 1, s, :, :] = (
                        part[a, 1, s, :, :].astype(F32) + ring[a, 1, s, :, :].astype(F32)
                    ).astype(BF16)

                ring_copy(a, 1, s).start()
            else:
                ring_copy(a, 1, s).wait_send()

    loop(1, NP, lambda k: xy_arrival(3, got_r, 0, k).wait_recv())
    combine(1, got_r)
    extra = jnp.transpose(got_r[:, D : D + W].astype(F32)).astype(BF16)
    t0 = dot(extra, p0t[...])
    t1 = dot(extra, p1t[...])
    scal[z, 0:1, :] = t0[0:1, :]
    scal[z, 1:2, :] = t1[0:1, :]
    scal[z, 2:4, :] = t0[1:3, :] + t1[1:3, :]
    scal[z, 4:8, :] = jnp.zeros((4, T), F32)

    def sc_copy(s):
        to = lax.rem(s + ZL * c, NZ)
        return remote(scal.at[z], scal.at[z], sc_s.at[s], sc_q.at[z], z_id(to))

    def sc_arrival(k):
        here = scal.at[k]
        return remote(here, here, sc_s.at[0], sc_q.at[k], right)

    loop(0, ZL, lambda s: pl.when(s != r)(lambda: sc_copy(s).start()))
    ring_step(1, 0, True)
    loop(1, NP, lambda k: xy_arrival(2, got_p, 0, k).wait_recv())
    combine(0, got_p)
    ring_step(0, 0, True)

    def both(j):
        ring_step(1, j, True)
        ring_step(0, j, True)

    loop(1, ZL, both)

    loop(1, NP, lambda k: vp_arrival(k).wait_recv())
    vp_copy = sib(vp, vout.at[c], 6)
    vp_copy.start()
    vout[c, :, :, :, :] = vp[...]

    t_copy = sib(tail, tail, 7)

    @pl.when(own)
    def _():
        s = lax.rem(r, ZL)
        cols = pl.ds(pl.multiple_of(zl * W, W), W)
        router_all = routerT[...]
        router_h = router_all.astype(BF16)
        router_l = (router_all - router_h.astype(F32)).astype(BF16)
        logits = jnp.zeros((E, T), F32)
        for b in range(ZL):
            at = slice(b * W, (b + 1) * W)
            logits += dot(router_h[:, at], nb[b], NT) + dot(router_l[:, at], nb[b], NT)
        r0 = rt[0:1, :].astype(F32)
        r1 = rt[1:2, :].astype(F32)
        ids = lax.broadcasted_iota(jnp.int32, (E, T), 0).astype(F32)
        rg = jnp.sum(router_all * gain[...], axis=1, keepdims=True)

        def sc_wait(k):
            pl.when(k != z)(lambda: sc_arrival(k).wait_recv())

        loop(0, NZ, sc_wait)
        total = jnp.sum(scal[...], axis=0)
        dl = jnp.where(ids == r0, total[0:1, :], 0.0) + jnp.where(ids == r1, total[1:2, :], 0.0)
        dl = dl * (1.0 - jax.nn.sigmoid(logits))
        sum_1 = total[2:3, :] + jnp.sum(dl * rg, axis=0, keepdims=True)
        sum_2 = total[3:4, :] + jnp.sum(dl * logits, axis=0, keepdims=True)
        sum_1 = jnp.transpose(jnp.broadcast_to(sum_1, (W, T))) * (1.0 / D)
        sum_2 = jnp.transpose(jnp.broadcast_to(sum_2, (W, T))) * (1.0 / D)
        dl_c = jnp.transpose(jnp.concatenate([dl, jnp.zeros((W - E, T), F32)], axis=0))
        router_cols = jnp.concatenate([routerT[:, cols], jnp.zeros((W - E, W), F32)], axis=0)
        second = dot(dl_c.astype(BF16), router_cols.astype(BF16))
        values = frames[:, cols].astype(F32)
        inverse = stats[1]
        scaled = (values - stats[0]) * inverse

        def arrived_sum(a):
            ring_copy(a, 0, s).wait_recv()
            ring_copy(a, 1, s).wait_recv()
            return (
                part[a, 0, s, :, :].astype(F32)
                + ring[a, 0, s, :, :].astype(F32)
                + ring[a, 1, s, :, :].astype(F32)
            )

        d_scaled = (arrived_sum(1) + second) * gain[:, cols]
        result = cotb[s, :, :].astype(F32) + inverse * (d_scaled - sum_1 - scaled * sum_2)
        tail[1, :, :] = result.astype(BF16)
        tail[0, :, :] = (values + arrived_sum(0)).astype(BF16)
        t_copy.start()

    pl.when(jnp.logical_not(own))(lambda: t_copy.wait_recv())

    @pl.when(c == 0)
    def _():
        mixed[...] = tail[0, :, 0 : W // 2]
        dfr[...] = tail[1, :, 0 : W // 2]

    @pl.when(c == 1)
    def _():
        mixed[...] = tail[0, :, W // 2 : W]
        dfr[...] = tail[1, :, W // 2 : W]

    @pl.when(own)
    def _():
        t_copy.wait_send()
        rt_copy.wait_send()
        pl.when(r == ZL - 1)(lambda: loop(0, ZL, lambda s: nrm(s, right).wait_send()))
        pl.when(r == 0)(lambda: loop(0, ZL, lambda s: nrm(s, left).wait_send()))

    @pl.when(jnp.logical_not(own))
    def _():
        cot_copy.wait_send()
        pl.when(r < ZL + ZL // 2 - 1)(lambda: loop(0, ZL, lambda s: nrm(s, right).wait_send()))
        pl.when(r > ZL + ZL // 2)(lambda: loop(0, ZL, lambda s: nrm(s, left).wait_send()))

    loop(0, ZL + 1, lambda j: cot_step(j, False))

    def last_xy(k):
        xy(0, send_n, rows_a, c * SL, k).wait_send()
        xy(1, send_c, rows_c, c * SL, k).wait_send()
        give(3, retb, got_r, k).wait_send()
        give(2, prodb, got_p, k).wait_send()
        vp_send(k).wait_send()

    loop(1, NP, last_xy)
    loop(1, NZ, lambda k: v_send(k).wait_send())
    loop(0, ZL, lambda s: pl.when(s != r)(lambda: sc_copy(s).wait_send()))

    def last_ring(j):
        ring_step(0, j, False)
        ring_step(1, j, False)

    loop(0, ZL, last_ring)
    sib(vp, vout.at[1 - c], 6).wait_recv()
    for copy in (a_copy, c_copy, p_copy, r_copy, v_copy, vp_copy):
        copy.wait_send()


def shards(dims, frames, norm_gain, router, routes, w_in, w_out, cotangent):
    X, Y, ZL = dims
    NP, NZ, W = X * Y, 2 * ZL, 128
    T, D = frames.shape
    E = router.shape[1]
    CAP = 4 * routes.shape[1] * T // (3 * E)
    SL = NP * CAP
    HS = w_in.shape[2]
    vmem = pl.BlockSpec(memory_space=pltpu.VMEM)
    dma = pltpu.SemaphoreType.DMA
    mixed, dfr, sums, gin, gout = pl.pallas_call(
        functools.partial(kernel, dims),
        out_shape=[
            jax.ShapeDtypeStruct((T, W // 2), BF16),
            jax.ShapeDtypeStruct((T, W // 2), BF16),
            jax.ShapeDtypeStruct((2, NP, 2, D // W, W), F32),
            jax.ShapeDtypeStruct((D, HS), BF16),
            jax.ShapeDtypeStruct((HS, D), BF16),
        ],
        in_specs=[vmem] * 7,
        out_specs=[vmem] * 5,
        scratch_shapes=[
            pltpu.VMEM((8, T), jnp.int32),
            pltpu.VMEM((ZL, T, W), BF16),
            pltpu.VMEM((ZL, T, W), BF16),
            pltpu.VMEM((T, W // 2), BF16),
            pltpu.VMEM((2, T, W), F32),
            pltpu.VMEM((SL, T), BF16),
            pltpu.VMEM((SL, T), BF16),
            pltpu.VMEM((T, SL), BF16),
            pltpu.VMEM((SL, D), BF16),
            pltpu.VMEM((SL, D), BF16),
            pltpu.VMEM((2 * SL, D), BF16),
            pltpu.VMEM((2 * SL, D), BF16),
            pltpu.VMEM((HS, 2 * SL), BF16),
            pltpu.VMEM((HS, 2 * SL), BF16),
            pltpu.VMEM((2 * SL, D), BF16),
            pltpu.VMEM((2 * SL, D + W), BF16),
            pltpu.VMEM((SL, D), BF16),
            pltpu.VMEM((SL, D + W), BF16),
            pltpu.VMEM((SL, D), BF16),
            pltpu.VMEM((SL, D + W), BF16),
            pltpu.VMEM((2, 2, ZL, T, W), BF16),
            pltpu.VMEM((2, 2, ZL, T, W), BF16),
            pltpu.VMEM((NZ, 8, T), F32),
            pltpu.VMEM((2, D // W, W), F32),
            pltpu.VMEM((D // W, W), F32),
            pltpu.VMEM((NZ, D // W, W), F32),
            pltpu.VMEM((NP, 2, D // W, W), F32),
            pltpu.VMEM((2, T, W), BF16),
            dma((8,)),
            dma((8,)),
            dma((2,)),
            dma((ZL,)),
            dma((ZL,)),
            dma((ZL,)),
            dma((ZL,)),
            dma((ZL,)),
            dma((4, NP)),
            dma((4, NP)),
            dma((2, 2, ZL)),
            dma((2, 2, ZL)),
            dma((ZL,)),
            dma((NZ,)),
            dma((2, max(NP, NZ))),
            dma((2, max(NP, NZ))),
        ],
        compiler_params=pltpu.CompilerParams(
            collective_id=0, has_side_effects=True, vmem_limit_bytes=56 * 1024 * 1024
        ),
        name="experts",
    )(
        frames,
        norm_gain.reshape(1, D),
        router.T,
        jnp.pad(routes.T, ((0, 8 - routes.shape[1]), (0, 0))),
        w_in.reshape(D, HS),
        w_out.reshape(HS, D),
        cotangent,
    )
    column = lax.axis_index("expert")
    router_sum = sums[0].transpose(1, 0, 2, 3).reshape(E, D)
    d_router = router_sum.T * (1.0 / T)
    gain_sum = jnp.sum(sums[1, :, 0] + sums[1, :, 1], axis=0).reshape(D) * (1.0 / T)
    d_gain = (gain_sum + jnp.sum(router * d_router, axis=1)) / norm_gain
    d_gain = lax.dynamic_slice_in_dim(d_gain, column * (W // 2), W // 2, 0)
    return mixed, dfr, d_gain, d_router, gin.reshape(1, D, HS), gout.reshape(1, HS, D)


def plan(mesh):
    dp, ex = mesh.shape["dp"], mesh.shape["expert"]
    side = 4 if dp == 32 else 2
    return side, dp // 2 // side, ex // 2


def solution(mesh):
    placed = (
        P("dp", None),
        P(),
        P(),
        P("dp", None),
        P("dp", None, "expert"),
        P("dp", "expert", None),
        P("dp", "expert"),
    )
    return jax.shard_map(
        functools.partial(shards, plan(mesh)),
        mesh=mesh,
        in_specs=placed,
        out_specs=(
            P("dp", "expert"),
            P("dp", "expert"),
            P("expert"),
            P(),
            P("dp", None, "expert"),
            P("dp", "expert", None),
        ),
        check_vma=False,
    )
```

```python
import functools

import jax
import jax.numpy as jnp
from jax import lax
from jax.experimental import pallas as pl
from jax.experimental.pallas import tpu as pltpu
from jax.sharding import PartitionSpec as P

EPS = 1e-05
F32 = jnp.float32
BF16 = jnp.bfloat16
MESH = pl.DeviceIdType.MESH
NN = (((1,), (0,)), ((), ()))
NT = (((1,), (1,)), ((), ()))


def dot(a, b, dims=NN):
    return lax.dot_general(a, b, dims, preferred_element_type=F32)


def loop(lo, hi, body):
    def step(i, carry):
        body(i)
        return carry

    lax.fori_loop(lo, hi, step, 0)


PARENT = {1: 0, 2: 0, 3: 2, 4: 0, 5: 4, 6: 4, 7: 6, 8: 6}
LAST = {1: 0, 2: 1, 4: 2}


def kernel(
    dims,
    frames,
    gain,
    routerT,
    routesT,
    w_in,
    w_out,
    cot,
    mixed,
    dfr,
    vout,
    gin,
    gout,
    rt,
    nb,
    cotb,
    sibcot,
    stats,
    p0t,
    p1t,
    pcomb,
    send_n,
    send_c,
    rows_a,
    rows_c,
    hid,
    gates,
    ga_t,
    d_t,
    prodb,
    retb,
    sib_p,
    sib_r,
    got_p,
    got_r,
    part,
    relay,
    fin,
    scal,
    vw,
    sibvw,
    vz,
    vp,
    tail,
    sib_s,
    sib_q,
    rt_sem,
    nrm_s,
    nrm_q,
    cot_s0,
    cot_s1,
    cot_q,
    xy_s,
    xy_q,
    up_s,
    relay_q,
    fin_q,
    sc_s,
    sc_q,
    vz_s,
    vz_q,
):
    X, Y, ZL = dims
    NP = X * Y
    NZ = 2 * ZL
    T, D = frames.shape
    SL = send_n.shape[0]
    CAP = SL // NP
    E = routerT.shape[0]
    W = 128
    reach = (ZL, ZL - 1)
    dp = lax.axis_index("dp")
    ex = lax.axis_index("expert")
    p = lax.rem(dp, NP)
    zh = dp // NP
    zl = ex // 2
    c = lax.rem(ex, 2)
    z = zh * ZL + zl
    x = p // Y
    y = lax.rem(p, Y)
    r = lax.rem(z + NZ - ZL * c, NZ)
    own = r < ZL
    sib_id = (dp, zl * 2 + 1 - c)

    def z_id(to):
        return ((to // ZL) * NP + p, lax.rem(to, ZL) * 2 + c)

    def z_at(way, hops):
        return z_id(lax.rem(z + (hops if way == 0 else NZ - hops), NZ))

    right = z_at(0, 1)
    left = z_at(1, 1)

    def plane(k, sign):
        px = lax.rem(x + X + sign * (k // Y), X)
        py = lax.rem(y + Y + sign * lax.rem(k, Y), Y)
        return px * Y + py

    def plane_id(k):
        return (zh * NP + plane(k, 1), ex)

    def remote(src, dst, ssem, rsem, to):
        return pltpu.make_async_remote_copy(
            src_ref=src, dst_ref=dst, send_sem=ssem, recv_sem=rsem, device_id=to, device_id_type=MESH
        )

    def sib(src, dst, i):
        return remote(src, dst, sib_s.at[i], sib_q.at[i], sib_id)

    barrier = pltpu.get_barrier_semaphore()

    def greet(to):
        pl.semaphore_signal(barrier, inc=1, device_id=to, device_id_type=MESH)

    greet(sib_id)
    loop(1, NP, lambda k: greet(plane_id(k)))
    loop(1, NZ, lambda k: greet(z_id(lax.rem(z + k, NZ))))

    @pl.when(own)
    def _():
        step = T // 8

        def norm(i):
            at = pl.ds(pl.multiple_of(i * step, step), step)
            values = frames[at, :].astype(F32)
            mean = jnp.mean(values, axis=1, keepdims=True)
            centred = values - mean
            inverse = lax.rsqrt(jnp.mean(centred * centred, axis=1, keepdims=True) + EPS)
            normed = (centred * inverse * gain[...]).astype(BF16)
            for s in range(ZL):
                nb[s, at, :] = normed[:, s * W : (s + 1) * W]
            stats[0, at, :] = jnp.broadcast_to(mean, (step, W))
            stats[1, at, :] = jnp.broadcast_to(inverse, (step, W))

        loop(0, 8, norm)
        rt[...] = routesT[...]

    pl.semaphore_wait(barrier, NP + NZ - 1)

    cot_copy = sib(cot, sibcot, 0)
    rt_copy = remote(rt, rt, rt_sem.at[0], rt_sem.at[1], z_id(lax.rem(z + ZL, NZ)))

    def nrm(s, to):
        return remote(nb.at[s], nb.at[s], nrm_s.at[s], nrm_q.at[s], to)

    def cot_copy_to(s, sem, way, hops):
        return remote(cotb.at[s], cotb.at[s], sem, cot_q.at[s], z_at(way, hops))

    def cot_source(act):
        s = lax.rem(r, ZL)
        for d in (4, 2, 1):
            for way in (0, 1):
                if d <= reach[way]:
                    act(cot_copy_to(s, cot_s0.at[way * 3 + LAST[d]], way, d))

    def cot_relay(d, act, wait=True):
        for way in (0, 1):
            if d > reach[way]:
                continue
            piece = lax.rem(r + (NZ - d if way == 0 else d), NZ)

            @pl.when(piece < ZL)
            def _():
                s = lax.rem(piece, ZL)
                if wait:
                    cot_copy_to(s, cot_s1.at[s, 0], way, 1).wait_recv()
                for far in (d + 2, d + 1):
                    if far <= reach[way] and PARENT[far] == d:
                        act(cot_copy_to(s, cot_s1.at[s, far - d - 1], way, far - d))

    def start(copy):
        copy.start()

    def sent(copy):
        copy.wait_send()

    def positions():
        r0 = rt[0:1, :].astype(F32)
        r1 = rt[1:2, :].astype(F32)
        lanes = lax.broadcasted_iota(jnp.int32, (E, T), 0).astype(F32)
        e0 = jnp.where(lanes == r0, 1.0, 0.0)
        e1 = jnp.where(lanes == r1, 1.0, 0.0)
        before = lax.broadcasted_iota(jnp.int32, (T, T), 0) < lax.broadcasted_iota(
            jnp.int32, (T, T), 1
        )
        counts = dot((e0 + e1).astype(BF16), jnp.where(before, 1.0, 0.0).astype(BF16))
        base = (zh * NP).astype(F32)
        for rk, ek, pt, first in ((r0, e0, p0t, True), (r1, e1, p1t, False)):
            slot = jnp.sum(ek * counts, axis=0, keepdims=True)
            pos = (rk - base) * CAP + slot
            posc = jnp.transpose(jnp.broadcast_to(pos, (W, T)))
            for b in range(SL // W):
                down = (lax.broadcasted_iota(jnp.int32, (W, T), 0) + b * W).astype(F32)
                pt[b * W : (b + 1) * W, :] = jnp.where(down == pos, 1.0, 0.0).astype(BF16)
                across = (lax.broadcasted_iota(jnp.int32, (T, W), 1) + b * W).astype(F32)
                hit = jnp.where(across == posc, 1.0, 0.0).astype(BF16)
                if first:
                    pcomb[:, b * W : (b + 1) * W] = hit
                else:
                    pcomb[:, b * W : (b + 1) * W] += hit

    def xy(a, src, dst, at, k):
        return remote(
            src.at[pl.ds(pl.multiple_of(plane(k, 1) * CAP, CAP), CAP)],
            dst.at[pl.ds(pl.multiple_of(at + p * CAP, CAP), CAP)],
            xy_s.at[a, k],
            xy_q.at[a, k],
            plane_id(k),
        )

    def xy_arrival(a, dst, at, k):
        here = dst.at[pl.ds(pl.multiple_of(at + plane(k, -1) * CAP, CAP), CAP)]
        return remote(here, here, xy_s.at[a, k], xy_q.at[a, k], plane_id(k))

    def dispatch(a, pieces, send, dst):
        pt = p0t[...] + p1t[...]

        def one(s):
            send[:, pl.ds(pl.multiple_of(s * W, W), W)] = dot(pt, pieces[s]).astype(BF16)

        loop(0, ZL, one)
        loop(1, NP, lambda k: xy(a, send, dst, c * SL, k).start())
        mine = pl.ds(pl.multiple_of(p * CAP, CAP), CAP)
        dst[pl.ds(pl.multiple_of(c * SL + p * CAP, CAP), CAP), :] = send[mine, :]

    @pl.when(own)
    def _():
        rt_copy.start()
        pl.when(r == ZL - 1)(lambda: loop(0, ZL, lambda s: nrm(s, right).start()))
        pl.when(r == 0)(lambda: loop(0, ZL, lambda s: nrm(s, left).start()))
        cot_copy.wait_recv()
        one, two = cot[...], sibcot[...]

        @pl.when(c == 0)
        def _():
            cotb[r, :, :] = jnp.concatenate([one, two], axis=1)

        @pl.when(c == 1)
        def _():
            cotb[r, :, :] = jnp.concatenate([two, one], axis=1)

        cot_source(start)
        positions()
        dispatch(0, nb, send_n, rows_a)
        for d in (2, 4, 6):
            cot_relay(d, start)

    @pl.when(jnp.logical_not(own))
    def _():
        cot_copy.start()
        rt_copy.wait_recv()
        positions()

        def step(i):
            near = r < ZL + ZL // 2

            @pl.when(near)
            def _():
                nrm(i, right).wait_recv()
                pl.when(r < ZL + ZL // 2 - 1)(lambda: nrm(i, right).start())

            @pl.when(jnp.logical_not(near))
            def _():
                nrm(i, left).wait_recv()
                pl.when(r > ZL + ZL // 2)(lambda: nrm(i, left).start())

        loop(0, ZL // 2, step)
        cot_relay(2, start)
        cot_relay(4, start)
        loop(ZL // 2, ZL, step)
        cot_relay(6, start)
        dispatch(0, nb, send_n, rows_a)

    for d in (1, 3, 5, 7, 8):
        cot_relay(d, start)
    dispatch(1, cotb, send_c, rows_c)

    half = pl.ds(pl.multiple_of(c * SL, SL), SL)
    away = pl.ds(pl.multiple_of((1 - c) * SL, SL), SL)
    RT = 128
    tiles = SL // RT
    mine_rows = pl.ds(pl.multiple_of(c * SL + p * CAP, CAP), CAP)
    here_rows = pl.ds(pl.multiple_of(p * CAP, CAP), CAP)

    a_copy = sib(rows_a.at[half], rows_a.at[half], 1)
    loop(1, NP, lambda k: xy_arrival(0, rows_a, c * SL, k).wait_recv())
    a_copy.start()
    weight_in = w_in[...]
    weight_out = w_out[...]
    router_row = routerT[pl.ds(dp, 1), :]
    router_hi = router_row.astype(BF16)
    router_lo = (router_row - router_hi.astype(F32)).astype(BF16)
    router_hi = jnp.broadcast_to(router_hi, (16, D))
    router_lo = jnp.broadcast_to(router_lo, (16, D))

    def forward(i):
        at = pl.ds(pl.multiple_of(i * RT, RT), RT)
        arrived = rows_a[at, :]
        hidden = dot(arrived, weight_in)
        logit = dot(arrived, router_hi, NT) + dot(arrived, router_lo, NT)
        gate = jax.nn.sigmoid(logit[:, 0:1])
        active = hidden * jax.nn.sigmoid(hidden)
        ga = active.astype(BF16).astype(F32) * (0.5 * gate)
        hid[at, :] = hidden
        gates[at, :] = jnp.broadcast_to(gate, (RT, W))
        ga_t[:, at] = jnp.transpose(ga).astype(BF16)
        prodb[at, :] = dot(ga.astype(BF16), weight_out).astype(BF16)

    def pair_sum(buf, other, i):
        at = pl.ds(pl.multiple_of(i * RT, RT), RT)
        mine = pl.ds(pl.multiple_of(c * SL + i * RT, RT), RT)
        buf[mine, :] = (buf[mine, :].astype(F32) + other[at, :].astype(F32)).astype(BF16)

    def give(a, h, src, dst, k):
        wide = src.shape[1]
        cut = wide - D // 2
        cols = pl.ds(0, cut) if h == 0 else pl.ds(cut, D // 2)
        return remote(
            src.at[pl.ds(pl.multiple_of(c * SL + plane(k, 1) * CAP, CAP), CAP), cols],
            dst.at[here_rows, cols],
            xy_s.at[2 + 2 * a + h, k],
            xy_q.at[2 + 2 * a + h, k],
            plane_id(k),
        )

    def give_arrival(a, h, dst, k):
        wide = dst.shape[1]
        cut = wide - D // 2
        cols = pl.ds(0, cut) if h == 0 else pl.ds(cut, D // 2)
        here = dst.at[pl.ds(pl.multiple_of(plane(k, -1) * CAP, CAP), CAP), cols]
        return remote(here, here, xy_s.at[2 + 2 * a + h, k], xy_q.at[2 + 2 * a + h, k], plane_id(k))

    p_copy = sib(prodb.at[away], sib_p, 3)
    sib(rows_a.at[away], rows_a.at[away], 1).wait_recv()
    loop(0, tiles, lambda i: forward((1 - c) * tiles + i))
    p_copy.start()
    loop(0, tiles, lambda i: forward(c * tiles + i))
    p_copy.wait_recv()
    loop(0, tiles, lambda i: pair_sum(prodb, sib_p, i))
    for h in (0, 1):
        loop(1, NP, lambda k: give(0, h, prodb, got_p, k).start())
    got_p[here_rows, :] = prodb[mine_rows, :]

    c_copy = sib(rows_c.at[half], rows_c.at[half], 2)
    loop(1, NP, lambda k: xy_arrival(1, rows_c, c * SL, k).wait_recv())
    c_copy.start()
    gain_hi = gain[...].astype(BF16)
    gain_lo = (gain[...] - gain_hi.astype(F32)).astype(BF16)
    gw = (
        dot(jnp.broadcast_to(gain_hi, (16, D)), weight_in)
        + dot(jnp.broadcast_to(gain_lo, (16, D)), weight_in)
    )[0:1, :]
    vw[...] = jnp.zeros_like(vw)
    lane = lax.broadcasted_iota(jnp.int32, (RT, W), 1)

    def backward(i):
        at = pl.ds(pl.multiple_of(i * RT, RT), RT)
        hidden = hid[at, :]
        gate = gates[at, 0:1]
        sig = jax.nn.sigmoid(hidden)
        up = dot(rows_c[at, :], weight_out, NT) * (0.5 * gate)
        dh = up * (sig * (1.0 + hidden * (1.0 - sig)))
        d_t[:, at] = jnp.transpose(dh).astype(BF16)
        dgg = jnp.sum(up * (hidden * sig), axis=1, keepdims=True)
        s1 = jnp.sum(dh * gw, axis=1, keepdims=True)
        s2 = jnp.sum(dh * hidden, axis=1, keepdims=True)
        back = dot(dh.astype(BF16), weight_in, NT)
        retb[at, W : W + D] = back.astype(BF16)
        retb[at, 0:W] = jnp.where(
            lane == 0, dgg, jnp.where(lane == 1, s1, jnp.where(lane == 2, s2, 0.0))
        ).astype(BF16)
        wide = rows_a[at, :].astype(F32)
        v = jnp.sum(wide * (dgg * (1.0 - gate)), axis=0, keepdims=True)
        w = jnp.sum(wide * back, axis=0, keepdims=True)
        for b in range(D // W):
            vw[0, b : b + 1, :] += v[:, b * W : (b + 1) * W]
            vw[1, b : b + 1, :] += w[:, b * W : (b + 1) * W]

    r_copy = sib(retb.at[away], sib_r, 4)
    sib(rows_c.at[away], rows_c.at[away], 2).wait_recv()
    loop(0, tiles, lambda i: backward((1 - c) * tiles + i))
    r_copy.start()
    loop(0, tiles, lambda i: backward(c * tiles + i))
    v_copy = sib(vw.at[1 - c], sibvw, 5)
    v_copy.start()
    r_copy.wait_recv()
    loop(0, tiles, lambda i: pair_sum(retb, sib_r, i))
    for h in (0, 1):
        loop(1, NP, lambda k: give(1, h, retb, got_r, k).start())
    got_r[here_rows, :] = retb[mine_rows, :]

    v_copy.wait_recv()
    vz[z, :, :] = vw[c, :, :] + sibvw[...]

    def v_send(k):
        return remote(vz.at[z], vz.at[z], vz_s.at[0, k], vz_q.at[0, k], z_id(lax.rem(z + k, NZ)))

    def v_arrival(k):
        here = vz.at[lax.rem(z + NZ - k, NZ)]
        return remote(here, here, vz_s.at[0, k], vz_q.at[0, k], z_id(lax.rem(z + k, NZ)))

    loop(1, NZ, lambda k: v_send(k).start())

    def up(a, d, lo, hi, act, run=True):
        for way in (0, 1):
            if d > reach[way]:
                continue
            to = lax.rem(r + (d if way == 0 else NZ - d), NZ)

            @pl.when((to >= lo) & (to < hi))
            def _():
                s = lax.rem(to, ZL)
                pd = PARENT[d]
                if pd == 0:
                    dst, sem = fin.at[a, way * 3 + LAST[d]], fin_q.at[a, way * 3 + LAST[d]]
                else:
                    dst, sem = relay.at[a, s, 1 - d % 2], relay_q.at[a, s, 1 - d % 2]
                if run:
                    kids = [k for k in (d + 1, d + 2) if k <= reach[way] and PARENT[k] == d]
                    total = None
                    for kid in kids:
                        q = 1 - kid % 2
                        landed = relay.at[a, s, q]
                        remote(landed, landed, up_s.at[a, s], relay_q.at[a, s, q], right).wait_recv()
                        if total is None:
                            total = part[a, s, :, :].astype(F32)
                        total = total + relay[a, s, q, :, :].astype(F32)
                    if kids:
                        part[a, s, :, :] = total.astype(BF16)
                act(remote(part.at[a, s], dst, up_s.at[a, s], sem, z_at(way, d - pd)))

    def combine(a, h, got):
        first = h * (ZL // 2)
        off = got.shape[1] - D

        def one(i):
            s = first + i
            at = pl.ds(pl.multiple_of(off + s * W, W), W)
            part[a, s, :, :] = dot(pcomb[...], got[:, at]).astype(BF16)

        loop(1, NP, lambda k: give_arrival(a, h, got, k).wait_recv())
        loop(0, ZL // 2, one)
        for d in (7, 8, 5, 3, 1):
            up(a, d, first, first + ZL // 2, start)

    def relays(a, ds, lo, hi):
        for d in ds:
            up(a, d, lo, hi, start)

    combine(0, 0, got_p)
    combine(0, 1, got_p)

    def grads(i):
        at = pl.ds(pl.multiple_of(i * W, W), W)
        gout[:, at] = dot(ga_t[...], rows_c[:, at]).astype(BF16)
        gin[at, :] = jnp.transpose(dot(d_t[...], rows_a[:, at])).astype(BF16)

    loop(0, D // W // 2, grads)
    relays(0, (6, 2), 0, ZL)
    loop(D // W // 2, D // W, grads)
    relays(0, (4,), 0, ZL)

    loop(1, NZ, lambda k: v_arrival(k).wait_recv())
    vp[p, 0, :, :] = jnp.sum(vz[0:ZL], axis=0)
    vp[p, 1, :, :] = jnp.sum(vz[ZL:NZ], axis=0)

    def vp_send(k):
        return remote(vp.at[p], vp.at[p], vz_s.at[1, k], vz_q.at[1, k], plane_id(k))

    def vp_arrival(k):
        here = vp.at[plane(k, -1)]
        return remote(here, here, vz_s.at[1, k], vz_q.at[1, k], plane_id(k))

    loop(1, NP, lambda k: vp_send(k).start())

    combine(1, 0, got_r)
    extra = jnp.transpose(got_r[:, 0:W].astype(F32)).astype(BF16)
    t0 = dot(extra, p0t[...])
    t1 = dot(extra, p1t[...])
    scal[z, 0:1, :] = t0[0:1, :]
    scal[z, 1:2, :] = t1[0:1, :]
    scal[z, 2:4, :] = t0[1:3, :] + t1[1:3, :]
    scal[z, 4:8, :] = jnp.zeros((4, T), F32)

    def sc_copy(s):
        to = lax.rem(s + ZL * c, NZ)
        return remote(scal.at[z], scal.at[z], sc_s.at[s], sc_q.at[z], z_id(to))

    def sc_arrival(k):
        here = scal.at[k]
        return remote(here, here, sc_s.at[0], sc_q.at[k], right)

    loop(0, ZL, lambda s: pl.when(s != r)(lambda: sc_copy(s).start()))
    relays(1, (6, 2), 0, ZL // 2)
    combine(1, 1, got_r)
    relays(1, (4,), 0, ZL // 2)
    relays(1, (6, 2, 4), ZL // 2, ZL)

    loop(1, NP, lambda k: vp_arrival(k).wait_recv())
    vp_copy = sib(vp, vout.at[c], 6)
    vp_copy.start()
    vout[c, :, :, :, :] = vp[...]

    t_copy = sib(tail, tail, 7)

    @pl.when(own)
    def _():
        s = lax.rem(r, ZL)
        cols = pl.ds(pl.multiple_of(zl * W, W), W)
        router_all = routerT[...]
        router_h = router_all.astype(BF16)
        router_l = (router_all - router_h.astype(F32)).astype(BF16)
        logits = jnp.zeros((E, T), F32)
        for b in range(ZL):
            at = slice(b * W, (b + 1) * W)
            logits += dot(router_h[:, at], nb[b], NT) + dot(router_l[:, at], nb[b], NT)
        r0 = rt[0:1, :].astype(F32)
        r1 = rt[1:2, :].astype(F32)
        ids = lax.broadcasted_iota(jnp.int32, (E, T), 0).astype(F32)
        rg = jnp.sum(router_all * gain[...], axis=1, keepdims=True)

        def sc_wait(k):
            pl.when(k != z)(lambda: sc_arrival(k).wait_recv())

        loop(0, NZ, sc_wait)
        total = jnp.sum(scal[...], axis=0)
        dl = jnp.where(ids == r0, total[0:1, :], 0.0) + jnp.where(ids == r1, total[1:2, :], 0.0)
        dl = dl * (1.0 - jax.nn.sigmoid(logits))
        sum_1 = total[2:3, :] + jnp.sum(dl * rg, axis=0, keepdims=True)
        sum_2 = total[3:4, :] + jnp.sum(dl * logits, axis=0, keepdims=True)
        sum_1 = jnp.transpose(jnp.broadcast_to(sum_1, (W, T))) * (1.0 / D)
        sum_2 = jnp.transpose(jnp.broadcast_to(sum_2, (W, T))) * (1.0 / D)
        dl_c = jnp.transpose(jnp.concatenate([dl, jnp.zeros((W - E, T), F32)], axis=0))
        router_cols = jnp.concatenate([routerT[:, cols], jnp.zeros((W - E, W), F32)], axis=0)
        second = dot(dl_c.astype(BF16), router_cols.astype(BF16))
        values = frames[:, cols].astype(F32)
        inverse = stats[1]
        scaled = (values - stats[0]) * inverse

        def arrived_sum(a):
            total = part[a, s, :, :].astype(F32)
            for way in (0, 1):
                for d in (1, 2, 4):
                    if d <= reach[way]:
                        q = way * 3 + LAST[d]
                        landed = fin.at[a, q]
                        remote(landed, landed, up_s.at[a, s], fin_q.at[a, q], right).wait_recv()
                        total = total + fin[a, q, :, :].astype(F32)
            return total

        tail[0, :, :] = (values + arrived_sum(0)).astype(BF16)
        d_scaled = (arrived_sum(1) + second) * gain[:, cols]
        result = cotb[s, :, :].astype(F32) + inverse * (d_scaled - sum_1 - scaled * sum_2)
        tail[1, :, :] = result.astype(BF16)
        t_copy.start()

    pl.when(jnp.logical_not(own))(lambda: t_copy.wait_recv())

    @pl.when(c == 0)
    def _():
        mixed[...] = tail[0, :, 0 : W // 2]
        dfr[...] = tail[1, :, 0 : W // 2]

    @pl.when(c == 1)
    def _():
        mixed[...] = tail[0, :, W // 2 : W]
        dfr[...] = tail[1, :, W // 2 : W]

    @pl.when(own)
    def _():
        t_copy.wait_send()
        rt_copy.wait_send()
        pl.when(r == ZL - 1)(lambda: loop(0, ZL, lambda s: nrm(s, right).wait_send()))
        pl.when(r == 0)(lambda: loop(0, ZL, lambda s: nrm(s, left).wait_send()))
        cot_source(sent)

    @pl.when(jnp.logical_not(own))
    def _():
        cot_copy.wait_send()
        pl.when(r < ZL + ZL // 2 - 1)(lambda: loop(0, ZL, lambda s: nrm(s, right).wait_send()))
        pl.when(r > ZL + ZL // 2)(lambda: loop(0, ZL, lambda s: nrm(s, left).wait_send()))

    for d in (2, 4, 6):
        cot_relay(d, sent, wait=False)

    def last_xy(k):
        xy(0, send_n, rows_a, c * SL, k).wait_send()
        xy(1, send_c, rows_c, c * SL, k).wait_send()
        for h in (0, 1):
            give(0, h, prodb, got_p, k).wait_send()
            give(1, h, retb, got_r, k).wait_send()
        vp_send(k).wait_send()

    loop(1, NP, last_xy)
    loop(1, NZ, lambda k: v_send(k).wait_send())
    loop(0, ZL, lambda s: pl.when(s != r)(lambda: sc_copy(s).wait_send()))
    for d in range(1, ZL + 1):
        for a in (0, 1):
            up(a, d, 0, ZL, sent, run=False)
    sib(vp, vout.at[1 - c], 6).wait_recv()
    for copy in (a_copy, c_copy, p_copy, r_copy, v_copy, vp_copy):
        copy.wait_send()


def shards(dims, frames, norm_gain, router, routes, w_in, w_out, cotangent):
    X, Y, ZL = dims
    NP, NZ, W = X * Y, 2 * ZL, 128
    T, D = frames.shape
    E = router.shape[1]
    CAP = 4 * routes.shape[1] * T // (3 * E)
    SL = NP * CAP
    HS = w_in.shape[2]
    vmem = pl.BlockSpec(memory_space=pltpu.VMEM)
    dma = pltpu.SemaphoreType.DMA
    mixed, dfr, sums, gin, gout = pl.pallas_call(
        functools.partial(kernel, dims),
        out_shape=[
            jax.ShapeDtypeStruct((T, W // 2), BF16),
            jax.ShapeDtypeStruct((T, W // 2), BF16),
            jax.ShapeDtypeStruct((2, NP, 2, D // W, W), F32),
            jax.ShapeDtypeStruct((D, HS), BF16),
            jax.ShapeDtypeStruct((HS, D), BF16),
        ],
        in_specs=[vmem] * 7,
        out_specs=[vmem] * 5,
        scratch_shapes=[
            pltpu.VMEM((8, T), jnp.int32),
            pltpu.VMEM((ZL, T, W), BF16),
            pltpu.VMEM((ZL, T, W), BF16),
            pltpu.VMEM((T, W // 2), BF16),
            pltpu.VMEM((2, T, W), F32),
            pltpu.VMEM((SL, T), BF16),
            pltpu.VMEM((SL, T), BF16),
            pltpu.VMEM((T, SL), BF16),
            pltpu.VMEM((SL, D), BF16),
            pltpu.VMEM((SL, D), BF16),
            pltpu.VMEM((2 * SL, D), BF16),
            pltpu.VMEM((2 * SL, D), BF16),
            pltpu.VMEM((2 * SL, HS), F32),
            pltpu.VMEM((2 * SL, W), F32),
            pltpu.VMEM((HS, 2 * SL), BF16),
            pltpu.VMEM((HS, 2 * SL), BF16),
            pltpu.VMEM((2 * SL, D), BF16),
            pltpu.VMEM((2 * SL, D + W), BF16),
            pltpu.VMEM((SL, D), BF16),
            pltpu.VMEM((SL, D + W), BF16),
            pltpu.VMEM((SL, D), BF16),
            pltpu.VMEM((SL, D + W), BF16),
            pltpu.VMEM((2, ZL, T, W), BF16),
            pltpu.VMEM((2, ZL, 2, T, W), BF16),
            pltpu.VMEM((2, 6, T, W), BF16),
            pltpu.VMEM((NZ, 8, T), F32),
            pltpu.VMEM((2, D // W, W), F32),
            pltpu.VMEM((D // W, W), F32),
            pltpu.VMEM((NZ, D // W, W), F32),
            pltpu.VMEM((NP, 2, D // W, W), F32),
            pltpu.VMEM((2, T, W), BF16),
            dma((8,)),
            dma((8,)),
            dma((2,)),
            dma((ZL,)),
            dma((ZL,)),
            dma((6,)),
            dma((ZL, 2)),
            dma((ZL,)),
            dma((6, NP)),
            dma((6, NP)),
            dma((2, ZL)),
            dma((2, ZL, 2)),
            dma((2, 6)),
            dma((ZL,)),
            dma((NZ,)),
            dma((2, max(NP, NZ))),
            dma((2, max(NP, NZ))),
        ],
        compiler_params=pltpu.CompilerParams(
            collective_id=0, has_side_effects=True, vmem_limit_bytes=56 * 1024 * 1024
        ),
        name="experts",
    )(
        frames,
        norm_gain.reshape(1, D),
        router.T,
        jnp.pad(routes.T, ((0, 8 - routes.shape[1]), (0, 0))),
        w_in.reshape(D, HS),
        w_out.reshape(HS, D),
        cotangent,
    )
    column = lax.axis_index("expert")
    router_sum = sums[0].transpose(1, 0, 2, 3).reshape(E, D)
    d_router = router_sum.T * (1.0 / T)
    gain_sum = jnp.sum(sums[1, :, 0] + sums[1, :, 1], axis=0).reshape(D) * (1.0 / T)
    d_gain = (gain_sum + jnp.sum(router * d_router, axis=1)) / norm_gain
    d_gain = lax.dynamic_slice_in_dim(d_gain, column * (W // 2), W // 2, 0)
    return mixed, dfr, d_gain, d_router, gin.reshape(1, D, HS), gout.reshape(1, HS, D)


def plan(mesh):
    dp, ex = mesh.shape["dp"], mesh.shape["expert"]
    side = 4 if dp == 32 else 2
    return side, dp // 2 // side, ex // 2


def solution(mesh):
    placed = (
        P("dp", None),
        P(),
        P(),
        P("dp", None),
        P("dp", None, "expert"),
        P("dp", "expert", None),
        P("dp", "expert"),
    )
    return jax.shard_map(
        functools.partial(shards, plan(mesh)),
        mesh=mesh,
        in_specs=placed,
        out_specs=(
            P("dp", "expert"),
            P("dp", "expert"),
            P("expert"),
            P(),
            P("dp", None, "expert"),
            P("dp", "expert", None),
        ),
        check_vma=False,
    )
```

```python
import functools

import jax
import jax.numpy as jnp
from jax import lax
from jax.experimental import pallas as pl
from jax.experimental.pallas import tpu as pltpu
from jax.sharding import PartitionSpec as P

EPS = 1e-05
F32 = jnp.float32
BF16 = jnp.bfloat16
MESH = pl.DeviceIdType.MESH
NN = (((1,), (0,)), ((), ()))
NT = (((1,), (1,)), ((), ()))


def dot(a, b, dims=NN):
    return lax.dot_general(a, b, dims, preferred_element_type=F32)


def loop(lo, hi, body):
    def step(i, carry):
        body(i)
        return carry

    lax.fori_loop(lo, hi, step, 0)


PARENT = {1: 0, 2: 0, 3: 2, 4: 0, 5: 4, 6: 4, 7: 6, 8: 6}
LAST = {1: 0, 2: 1, 4: 2}


def kernel(
    dims,
    frames,
    gain,
    routerT,
    routesT,
    w_in,
    w_out,
    cot,
    mixed,
    dfr,
    vout,
    gin,
    gout,
    rt,
    nb,
    cotb,
    sibcot,
    stats,
    p0t,
    p1t,
    pcomb,
    send_n,
    send_c,
    rows_a,
    rows_c,
    hid,
    gates,
    ga_t,
    d_t,
    prodb,
    retb,
    sib_p,
    sib_r,
    got_p,
    got_r,
    part,
    relay,
    fin,
    scal,
    logits_t,
    vw,
    sibvw,
    vz,
    vp,
    tail,
    sib_s,
    sib_q,
    rt_sem,
    nrm_s,
    nrm_q,
    chain_s,
    cot_s0,
    cot_s1,
    cot_q,
    xy_s,
    xy_q,
    up_s,
    relay_q,
    fin_q,
    sc_s,
    sc_q,
    vz_s,
    vz_q,
):
    X, Y, ZL = dims
    NP = X * Y
    NZ = 2 * ZL
    T, D = frames.shape
    SL = send_n.shape[0]
    CAP = SL // NP
    E = routerT.shape[0]
    W = 128
    reach = (ZL, ZL - 1)
    dp = lax.axis_index("dp")
    ex = lax.axis_index("expert")
    p = lax.rem(dp, NP)
    zh = dp // NP
    zl = ex // 2
    c = lax.rem(ex, 2)
    z = zh * ZL + zl
    x = p // Y
    y = lax.rem(p, Y)
    r = lax.rem(z + NZ - ZL * c, NZ)
    own = r < ZL
    sib_id = (dp, zl * 2 + 1 - c)

    def z_id(to):
        return ((to // ZL) * NP + p, lax.rem(to, ZL) * 2 + c)

    def z_at(way, hops):
        return z_id(lax.rem(z + (hops if way == 0 else NZ - hops), NZ))

    right = z_at(0, 1)
    left = z_at(1, 1)

    def plane(k, sign):
        px = lax.rem(x + X + sign * (k // Y), X)
        py = lax.rem(y + Y + sign * lax.rem(k, Y), Y)
        return px * Y + py

    def plane_id(k):
        return (zh * NP + plane(k, 1), ex)

    def remote(src, dst, ssem, rsem, to):
        return pltpu.make_async_remote_copy(
            src_ref=src, dst_ref=dst, send_sem=ssem, recv_sem=rsem, device_id=to, device_id_type=MESH
        )

    def sib(src, dst, i):
        return remote(src, dst, sib_s.at[i], sib_q.at[i], sib_id)

    barrier = pltpu.get_barrier_semaphore()

    def greet(to):
        pl.semaphore_signal(barrier, inc=1, device_id=to, device_id_type=MESH)

    greet(sib_id)
    loop(1, NP, lambda k: greet(plane_id(k)))
    loop(1, NZ, lambda k: greet(z_id(lax.rem(z + k, NZ))))

    @pl.when(own)
    def _():
        step = T // 8

        def norm(i):
            at = pl.ds(pl.multiple_of(i * step, step), step)
            values = frames[at, :].astype(F32)
            mean = jnp.mean(values, axis=1, keepdims=True)
            centred = values - mean
            inverse = lax.rsqrt(jnp.mean(centred * centred, axis=1, keepdims=True) + EPS)
            normed = (centred * inverse * gain[...]).astype(BF16)
            for s in range(ZL):
                nb[s, at, :] = normed[:, s * W : (s + 1) * W]
            stats[0, at, :] = jnp.broadcast_to(mean, (step, W))
            stats[1, at, :] = jnp.broadcast_to(inverse, (step, W))

        loop(0, 8, norm)
        rt[...] = routesT[...]

    pl.semaphore_wait(barrier, NP + NZ - 1)

    cot_copy = sib(cot, sibcot, 0)
    rt_copy = remote(rt, rt, rt_sem.at[0], rt_sem.at[1], z_id(lax.rem(z + ZL, NZ)))

    def nrm(s, to):
        return remote(nb.at[s], nb.at[s], nrm_s.at[s], nrm_q.at[s], to)

    def pass_on(s, to):
        return remote(cotb.at[s], cotb.at[s], chain_s.at[s], cot_q.at[s], to)

    def cot_copy_to(s, sem, way, hops):
        return remote(cotb.at[s], cotb.at[s], sem, cot_q.at[s], z_at(way, hops))

    def inside(way, hops):
        return (r + hops < ZL) if way == 0 else (r >= hops)

    def to_other_block(s, act):
        pl.when(r == ZL - 1)(lambda: act(pass_on(s, right)))
        pl.when(r == 0)(lambda: act(pass_on(s, left)))

    def cot_source(act):
        s = lax.rem(r, ZL)
        for d in (4, 2, 1):
            for way in (0, 1):
                copy = cot_copy_to(s, cot_s0.at[way * 3 + LAST[d]], way, d)
                pl.when(inside(way, d))(functools.partial(act, copy))
        to_other_block(s, act)

    def cot_relay(d, act, wait=True):
        for way in (0, 1):

            @pl.when(inside(1 - way, d))
            def _():
                s = lax.rem(r + (NZ - d if way == 0 else d), NZ)
                if wait:
                    cot_copy_to(s, cot_s1.at[s, 0], way, 1).wait_recv()
                for far in (d + 2, d + 1):
                    if far < ZL and PARENT[far] == d:
                        copy = cot_copy_to(s, cot_s1.at[s, far - d - 1], way, far - d)
                        pl.when(inside(way, far - d))(functools.partial(act, copy))
                if way == 0:
                    pl.when(r == ZL - 1)(lambda: act(pass_on(s, right)))
                else:
                    pl.when(r == 0)(lambda: act(pass_on(s, left)))

    def start(copy):
        copy.start()

    def sent(copy):
        copy.wait_send()

    near = r < ZL + ZL // 2
    onward_r = near & (r >= ZL) & (r < ZL + ZL // 2 - 1)
    onward_l = r > ZL + ZL // 2

    def positions():
        r0 = rt[0:1, :].astype(F32)
        r1 = rt[1:2, :].astype(F32)
        lanes = lax.broadcasted_iota(jnp.int32, (E, T), 0).astype(F32)
        e0 = jnp.where(lanes == r0, 1.0, 0.0)
        e1 = jnp.where(lanes == r1, 1.0, 0.0)
        before = lax.broadcasted_iota(jnp.int32, (T, T), 0) < lax.broadcasted_iota(
            jnp.int32, (T, T), 1
        )
        counts = dot((e0 + e1).astype(BF16), jnp.where(before, 1.0, 0.0).astype(BF16))
        base = (zh * NP).astype(F32)
        for rk, ek, pt, first in ((r0, e0, p0t, True), (r1, e1, p1t, False)):
            slot = jnp.sum(ek * counts, axis=0, keepdims=True)
            pos = (rk - base) * CAP + slot
            posc = jnp.transpose(jnp.broadcast_to(pos, (W, T)))
            for b in range(SL // W):
                down = (lax.broadcasted_iota(jnp.int32, (W, T), 0) + b * W).astype(F32)
                pt[b * W : (b + 1) * W, :] = jnp.where(down == pos, 1.0, 0.0).astype(BF16)
                across = (lax.broadcasted_iota(jnp.int32, (T, W), 1) + b * W).astype(F32)
                hit = jnp.where(across == posc, 1.0, 0.0).astype(BF16)
                if first:
                    pcomb[:, b * W : (b + 1) * W] = hit
                else:
                    pcomb[:, b * W : (b + 1) * W] += hit

    def half_cols(h):
        return pl.ds(pl.multiple_of(h * (D // 2), D // 2), D // 2)

    def xy(a, h, src, dst, k):
        return remote(
            src.at[pl.ds(pl.multiple_of(plane(k, 1) * CAP, CAP), CAP), half_cols(h)],
            dst.at[pl.ds(pl.multiple_of(c * SL + p * CAP, CAP), CAP), half_cols(h)],
            xy_s.at[2 * a + h, k],
            xy_q.at[2 * a + h, k],
            plane_id(k),
        )

    def xy_arrival(a, h, dst, k):
        here = dst.at[
            pl.ds(pl.multiple_of(c * SL + plane(k, -1) * CAP, CAP), CAP), half_cols(h)
        ]
        return remote(here, here, xy_s.at[2 * a + h, k], xy_q.at[2 * a + h, k], plane_id(k))

    def to_slots(pieces, send, s):
        pt = p0t[...] + p1t[...]
        send[:, pl.ds(pl.multiple_of(s * W, W), W)] = dot(pt, pieces[s]).astype(BF16)

    def go(a, h, send, dst):
        loop(1, NP, lambda k: xy(a, h, send, dst, k).start())

    def keep(send, dst):
        mine = pl.ds(pl.multiple_of(p * CAP, CAP), CAP)
        dst[pl.ds(pl.multiple_of(c * SL + p * CAP, CAP), CAP), :] = send[mine, :]

    order = [d for d in (1, 2, 4, 3, 6, 5, 7) if d < ZL]
    chain_order = [0] + order
    enough = max(chain_order.index(d) for d in range(ZL // 2))

    @pl.when(own)
    def _():
        rt_copy.start()
        pl.when(r == ZL - 1)(lambda: loop(0, ZL, lambda i: nrm(ZL - 1 - i, right).start()))
        pl.when(r == 0)(lambda: loop(0, ZL, lambda s: nrm(s, left).start()))
        cot_copy.wait_recv()
        one, two = cot[...], sibcot[...]

        @pl.when(c == 0)
        def _():
            cotb[r, :, :] = jnp.concatenate([one, two], axis=1)

        @pl.when(c == 1)
        def _():
            cotb[r, :, :] = jnp.concatenate([two, one], axis=1)

        cot_source(start)
        positions()
        for h in (0, 1):
            loop(h * (ZL // 2), (h + 1) * (ZL // 2), lambda s: to_slots(nb, send_n, s))
            go(0, h, send_n, rows_a)
        for d in order:
            cot_relay(d, start)
        for h in (0, 1):
            loop(h * (ZL // 2), (h + 1) * (ZL // 2), lambda s: to_slots(cotb, send_c, s))
            go(1, h, send_c, rows_c)

    @pl.when(jnp.logical_not(own))
    def _():
        cot_copy.start()
        rt_copy.wait_recv()
        positions()
        first = jnp.where(near, 1, 0)

        def take(copy, i):
            s = jnp.where(near, ZL - 1 - i, i)
            copy(s, right).wait_recv()
            pl.when(onward_r)(lambda: copy(s, right).start())
            pl.when(onward_l)(lambda: copy(s, left).start())
            return s

        loop(0, ZL // 2, lambda i: to_slots(nb, send_n, take(nrm, i)))
        go(0, first, send_n, rows_a)
        loop(ZL // 2, ZL, lambda i: to_slots(nb, send_n, take(nrm, i)))
        go(0, 1 - first, send_n, rows_a)
        for n, i in enumerate(chain_order):
            to_slots(cotb, send_c, take(pass_on, i))
            if n == enough:
                go(1, first, send_c, rows_c)
        go(1, 1 - first, send_c, rows_c)

    keep(send_n, rows_a)
    keep(send_c, rows_c)

    half = pl.ds(pl.multiple_of(c * SL, SL), SL)
    away = pl.ds(pl.multiple_of((1 - c) * SL, SL), SL)
    RT = 128
    tiles = SL // RT
    mine_rows = pl.ds(pl.multiple_of(c * SL + p * CAP, CAP), CAP)
    here_rows = pl.ds(pl.multiple_of(p * CAP, CAP), CAP)

    a_copy = sib(rows_a.at[half], rows_a.at[half], 1)
    for h in (0, 1):
        loop(1, NP, lambda k: xy_arrival(0, h, rows_a, k).wait_recv())
    a_copy.start()
    weight_in = w_in[...]
    weight_out = w_out[...]
    router_row = routerT[pl.ds(dp, 1), :]
    router_hi = router_row.astype(BF16)
    router_lo = (router_row - router_hi.astype(F32)).astype(BF16)
    router_hi = jnp.broadcast_to(router_hi, (16, D))
    router_lo = jnp.broadcast_to(router_lo, (16, D))

    def forward(i):
        at = pl.ds(pl.multiple_of(i * RT, RT), RT)
        arrived = rows_a[at, :]
        hidden = dot(arrived, weight_in)
        logit = dot(arrived, router_hi, NT) + dot(arrived, router_lo, NT)
        gate = jax.nn.sigmoid(logit[:, 0:1])
        active = hidden * jax.nn.sigmoid(hidden)
        ga = active.astype(BF16).astype(F32) * (0.5 * gate)
        hid[at, :] = hidden
        gates[at, :] = jnp.broadcast_to(gate, (RT, W))
        ga_t[:, at] = jnp.transpose(ga).astype(BF16)
        prodb[at, :] = dot(ga.astype(BF16), weight_out).astype(BF16)

    def pair_sum(buf, other, i):
        at = pl.ds(pl.multiple_of(i * RT, RT), RT)
        mine = pl.ds(pl.multiple_of(c * SL + i * RT, RT), RT)
        buf[mine, :] = (buf[mine, :].astype(F32) + other[at, :].astype(F32)).astype(BF16)

    def give(a, h, src, dst, k):
        wide = src.shape[1]
        cut = wide - D // 2
        cols = pl.ds(0, cut) if h == 0 else pl.ds(cut, D // 2)
        return remote(
            src.at[pl.ds(pl.multiple_of(c * SL + plane(k, 1) * CAP, CAP), CAP), cols],
            dst.at[here_rows, cols],
            xy_s.at[4 + 2 * a + h, k],
            xy_q.at[4 + 2 * a + h, k],
            plane_id(k),
        )

    def give_arrival(a, h, dst, k):
        wide = dst.shape[1]
        cut = wide - D // 2
        cols = pl.ds(0, cut) if h == 0 else pl.ds(cut, D // 2)
        here = dst.at[pl.ds(pl.multiple_of(plane(k, -1) * CAP, CAP), CAP), cols]
        return remote(here, here, xy_s.at[4 + 2 * a + h, k], xy_q.at[4 + 2 * a + h, k], plane_id(k))

    p_copy = sib(prodb.at[away], sib_p, 3)
    sib(rows_a.at[away], rows_a.at[away], 1).wait_recv()
    loop(0, tiles, lambda i: forward((1 - c) * tiles + i))
    p_copy.start()
    loop(0, tiles, lambda i: forward(c * tiles + i))
    p_copy.wait_recv()
    loop(0, tiles, lambda i: pair_sum(prodb, sib_p, i))
    for h in (0, 1):
        loop(1, NP, lambda k: give(0, h, prodb, got_p, k).start())
    got_p[here_rows, :] = prodb[mine_rows, :]

    c_copy = sib(rows_c.at[half], rows_c.at[half], 2)
    for h in (0, 1):
        loop(1, NP, lambda k: xy_arrival(1, h, rows_c, k).wait_recv())
    c_copy.start()
    gain_hi = gain[...].astype(BF16)
    gain_lo = (gain[...] - gain_hi.astype(F32)).astype(BF16)
    gw = (
        dot(jnp.broadcast_to(gain_hi, (16, D)), weight_in)
        + dot(jnp.broadcast_to(gain_lo, (16, D)), weight_in)
    )[0:1, :]
    vw[...] = jnp.zeros_like(vw)
    lane = lax.broadcasted_iota(jnp.int32, (RT, W), 1)

    def backward(i):
        at = pl.ds(pl.multiple_of(i * RT, RT), RT)
        hidden = hid[at, :]
        gate = gates[at, 0:1]
        sig = jax.nn.sigmoid(hidden)
        up = dot(rows_c[at, :], weight_out, NT) * (0.5 * gate)
        dh = up * (sig * (1.0 + hidden * (1.0 - sig)))
        d_t[:, at] = jnp.transpose(dh).astype(BF16)
        dgg = jnp.sum(up * (hidden * sig), axis=1, keepdims=True)
        s1 = jnp.sum(dh * gw, axis=1, keepdims=True)
        s2 = jnp.sum(dh * hidden, axis=1, keepdims=True)
        back = dot(dh.astype(BF16), weight_in, NT)
        retb[at, W : W + D] = back.astype(BF16)
        retb[at, 0:W] = jnp.where(
            lane == 0, dgg, jnp.where(lane == 1, s1, jnp.where(lane == 2, s2, 0.0))
        ).astype(BF16)
        wide = rows_a[at, :].astype(F32)
        v = jnp.sum(wide * (dgg * (1.0 - gate)), axis=0, keepdims=True)
        w = jnp.sum(wide * back, axis=0, keepdims=True)
        for b in range(D // W):
            vw[0, b : b + 1, :] += v[:, b * W : (b + 1) * W]
            vw[1, b : b + 1, :] += w[:, b * W : (b + 1) * W]

    r_copy = sib(retb.at[away], sib_r, 4)
    sib(rows_c.at[away], rows_c.at[away], 2).wait_recv()
    loop(0, tiles, lambda i: backward((1 - c) * tiles + i))
    r_copy.start()
    loop(0, tiles, lambda i: backward(c * tiles + i))
    v_copy = sib(vw.at[1 - c], sibvw, 5)
    v_copy.start()
    r_copy.wait_recv()
    loop(0, tiles, lambda i: pair_sum(retb, sib_r, i))
    for h in (0, 1):
        loop(1, NP, lambda k: give(1, h, retb, got_r, k).start())
    got_r[here_rows, :] = retb[mine_rows, :]

    v_copy.wait_recv()
    vz[z, :, :] = vw[c, :, :] + sibvw[...]

    def v_send(k):
        return remote(vz.at[z], vz.at[z], vz_s.at[0, k], vz_q.at[0, k], z_id(lax.rem(z + k, NZ)))

    def v_arrival(k):
        here = vz.at[lax.rem(z + NZ - k, NZ)]
        return remote(here, here, vz_s.at[0, k], vz_q.at[0, k], z_id(lax.rem(z + k, NZ)))

    loop(1, NZ, lambda k: v_send(k).start())

    def up(a, d, lo, hi, act, run=True):
        for way in (0, 1):
            if d > reach[way]:
                continue
            to = lax.rem(r + (d if way == 0 else NZ - d), NZ)

            @pl.when((to >= lo) & (to < hi))
            def _():
                s = lax.rem(to, ZL)
                pd = PARENT[d]
                if pd == 0:
                    dst, sem = fin.at[a, way * 3 + LAST[d]], fin_q.at[a, way * 3 + LAST[d]]
                else:
                    dst, sem = relay.at[a, s, 1 - d % 2], relay_q.at[a, s, 1 - d % 2]
                if run:
                    kids = [k for k in (d + 1, d + 2) if k <= reach[way] and PARENT[k] == d]
                    total = None
                    for kid in kids:
                        q = 1 - kid % 2
                        landed = relay.at[a, s, q]
                        remote(landed, landed, up_s.at[a, s], relay_q.at[a, s, q], right).wait_recv()
                        if total is None:
                            total = part[a, s, :, :].astype(F32)
                        total = total + relay[a, s, q, :, :].astype(F32)
                    if kids:
                        part[a, s, :, :] = total.astype(BF16)
                act(remote(part.at[a, s], dst, up_s.at[a, s], sem, z_at(way, d - pd)))

    def combine(a, h, got):
        first = h * (ZL // 2)
        off = got.shape[1] - D

        def one(i):
            s = first + i
            at = pl.ds(pl.multiple_of(off + s * W, W), W)
            part[a, s, :, :] = dot(pcomb[...], got[:, at]).astype(BF16)

        loop(1, NP, lambda k: give_arrival(a, h, got, k).wait_recv())
        loop(0, ZL // 2, one)
        for d in (7, 8, 5, 3, 1):
            up(a, d, first, first + ZL // 2, start)

    def relays(a, ds, lo, hi):
        for d in ds:
            up(a, d, lo, hi, start)

    combine(0, 0, got_p)
    combine(0, 1, got_p)

    def grads(i):
        at = pl.ds(pl.multiple_of(i * W, W), W)
        gout[:, at] = dot(ga_t[...], rows_c[:, at]).astype(BF16)
        gin[at, :] = jnp.transpose(dot(d_t[...], rows_a[:, at])).astype(BF16)

    loop(0, D // W // 2, grads)

    def vp_send(k):
        return remote(vp.at[p], vp.at[p], vz_s.at[1, k], vz_q.at[1, k], plane_id(k))

    def vp_arrival(k):
        here = vp.at[plane(k, -1)]
        return remote(here, here, vz_s.at[1, k], vz_q.at[1, k], plane_id(k))

    router_all = routerT[...]

    @pl.when(own)
    def _():
        router_h = router_all.astype(BF16)
        router_l = (router_all - router_h.astype(F32)).astype(BF16)
        logits = jnp.zeros((E, T), F32)
        for b in range(ZL):
            at = slice(b * W, (b + 1) * W)
            logits += dot(router_h[:, at], nb[b], NT) + dot(router_l[:, at], nb[b], NT)
        logits_t[...] = logits

    relays(0, (6, 2), 0, ZL)
    loop(D // W // 2, D // W, grads)

    combine(1, 0, got_r)
    extra = jnp.transpose(got_r[:, 0:W].astype(F32)).astype(BF16)
    t0 = dot(extra, p0t[...])
    t1 = dot(extra, p1t[...])
    scal[z, 0:1, :] = t0[0:1, :]
    scal[z, 1:2, :] = t1[0:1, :]
    scal[z, 2:4, :] = t0[1:3, :] + t1[1:3, :]

    def sc_copy(s):
        to = lax.rem(s + ZL * c, NZ)
        return remote(scal.at[z], scal.at[z], sc_s.at[s], sc_q.at[z], z_id(to))

    def sc_arrival(k):
        here = scal.at[k]
        return remote(here, here, sc_s.at[0], sc_q.at[k], right)

    loop(0, ZL, lambda s: pl.when(s != r)(lambda: sc_copy(s).start()))
    relays(0, (4,), 0, ZL)
    relays(1, (6, 2), 0, ZL // 2)
    combine(1, 1, got_r)
    relays(1, (4,), 0, ZL // 2)
    relays(1, (6, 2), ZL // 2, ZL)

    loop(1, NZ, lambda k: v_arrival(k).wait_recv())
    vp[p, 0, :, :] = jnp.sum(vz[0:ZL], axis=0)
    vp[p, 1, :, :] = jnp.sum(vz[ZL:NZ], axis=0)
    loop(1, NP, lambda k: vp_send(k).start())
    relays(1, (4,), ZL // 2, ZL)

    loop(1, NP, lambda k: vp_arrival(k).wait_recv())
    vp_copy = sib(vp, vout.at[c], 6)
    vp_copy.start()
    vout[c, :, :, :, :] = vp[...]

    t_copy = sib(tail, tail, 7)

    @pl.when(own)
    def _():
        s = lax.rem(r, ZL)
        cols = pl.ds(pl.multiple_of(zl * W, W), W)
        logits = logits_t[...]
        r0 = rt[0:1, :].astype(F32)
        r1 = rt[1:2, :].astype(F32)
        ids = lax.broadcasted_iota(jnp.int32, (E, T), 0).astype(F32)
        rg = jnp.sum(router_all * gain[...], axis=1, keepdims=True)

        def sc_wait(k):
            pl.when(k != z)(lambda: sc_arrival(k).wait_recv())

        loop(0, NZ, sc_wait)
        total = jnp.sum(scal[...], axis=0)
        dl = jnp.where(ids == r0, total[0:1, :], 0.0) + jnp.where(ids == r1, total[1:2, :], 0.0)
        dl = dl * (1.0 - jax.nn.sigmoid(logits))
        sum_1 = total[2:3, :] + jnp.sum(dl * rg, axis=0, keepdims=True)
        sum_2 = total[3:4, :] + jnp.sum(dl * logits, axis=0, keepdims=True)
        sum_1 = jnp.transpose(jnp.broadcast_to(sum_1, (W, T))) * (1.0 / D)
        sum_2 = jnp.transpose(jnp.broadcast_to(sum_2, (W, T))) * (1.0 / D)
        dl_c = jnp.transpose(jnp.concatenate([dl, jnp.zeros((W - E, T), F32)], axis=0))
        router_cols = jnp.concatenate([routerT[:, cols], jnp.zeros((W - E, W), F32)], axis=0)
        second = dot(dl_c.astype(BF16), router_cols.astype(BF16))
        values = frames[:, cols].astype(F32)
        inverse = stats[1]
        scaled = (values - stats[0]) * inverse

        def arrived_sum(a):
            total = part[a, s, :, :].astype(F32)
            for way in (0, 1):
                for d in (1, 2, 4):
                    if d <= reach[way]:
                        q = way * 3 + LAST[d]
                        landed = fin.at[a, q]
                        remote(landed, landed, up_s.at[a, s], fin_q.at[a, q], right).wait_recv()
                        total = total + fin[a, q, :, :].astype(F32)
            return total

        tail[0, :, :] = (values + arrived_sum(0)).astype(BF16)
        d_scaled = (arrived_sum(1) + second) * gain[:, cols]
        result = cotb[s, :, :].astype(F32) + inverse * (d_scaled - sum_1 - scaled * sum_2)
        tail[1, :, :] = result.astype(BF16)
        t_copy.start()

    pl.when(jnp.logical_not(own))(lambda: t_copy.wait_recv())

    @pl.when(c == 0)
    def _():
        mixed[...] = tail[0, :, 0 : W // 2]
        dfr[...] = tail[1, :, 0 : W // 2]

    @pl.when(c == 1)
    def _():
        mixed[...] = tail[0, :, W // 2 : W]
        dfr[...] = tail[1, :, W // 2 : W]

    @pl.when(own)
    def _():
        t_copy.wait_send()
        rt_copy.wait_send()
        pl.when(r == ZL - 1)(lambda: loop(0, ZL, lambda s: nrm(s, right).wait_send()))
        pl.when(r == 0)(lambda: loop(0, ZL, lambda s: nrm(s, left).wait_send()))
        cot_source(sent)
        for d in order:
            cot_relay(d, sent, wait=False)

    @pl.when(jnp.logical_not(own))
    def _():
        cot_copy.wait_send()
        pl.when(onward_r | onward_l)(
            lambda: loop(0, ZL, lambda s: (nrm(s, right).wait_send(), pass_on(s, right).wait_send()))
        )

    def last_xy(k):
        for h in (0, 1):
            xy(0, h, send_n, rows_a, k).wait_send()
            xy(1, h, send_c, rows_c, k).wait_send()
            give(0, h, prodb, got_p, k).wait_send()
            give(1, h, retb, got_r, k).wait_send()
        vp_send(k).wait_send()

    loop(1, NP, last_xy)
    loop(1, NZ, lambda k: v_send(k).wait_send())
    loop(0, ZL, lambda s: pl.when(s != r)(lambda: sc_copy(s).wait_send()))
    for d in range(1, ZL + 1):
        for a in (0, 1):
            up(a, d, 0, ZL, sent, run=False)
    sib(vp, vout.at[1 - c], 6).wait_recv()
    for copy in (a_copy, c_copy, p_copy, r_copy, v_copy, vp_copy):
        copy.wait_send()


def shards(dims, frames, norm_gain, router, routes, w_in, w_out, cotangent):
    X, Y, ZL = dims
    NP, NZ, W = X * Y, 2 * ZL, 128
    T, D = frames.shape
    E = router.shape[1]
    CAP = 4 * routes.shape[1] * T // (3 * E)
    SL = NP * CAP
    HS = w_in.shape[2]
    vmem = pl.BlockSpec(memory_space=pltpu.VMEM)
    dma = pltpu.SemaphoreType.DMA
    mixed, dfr, sums, gin, gout = pl.pallas_call(
        functools.partial(kernel, dims),
        out_shape=[
            jax.ShapeDtypeStruct((T, W // 2), BF16),
            jax.ShapeDtypeStruct((T, W // 2), BF16),
            jax.ShapeDtypeStruct((2, NP, 2, D // W, W), F32),
            jax.ShapeDtypeStruct((D, HS), BF16),
            jax.ShapeDtypeStruct((HS, D), BF16),
        ],
        in_specs=[vmem] * 7,
        out_specs=[vmem] * 5,
        scratch_shapes=[
            pltpu.VMEM((8, T), jnp.int32),
            pltpu.VMEM((ZL, T, W), BF16),
            pltpu.VMEM((ZL, T, W), BF16),
            pltpu.VMEM((T, W // 2), BF16),
            pltpu.VMEM((2, T, W), F32),
            pltpu.VMEM((SL, T), BF16),
            pltpu.VMEM((SL, T), BF16),
            pltpu.VMEM((T, SL), BF16),
            pltpu.VMEM((SL, D), BF16),
            pltpu.VMEM((SL, D), BF16),
            pltpu.VMEM((2 * SL, D), BF16),
            pltpu.VMEM((2 * SL, D), BF16),
            pltpu.VMEM((2 * SL, HS), F32),
            pltpu.VMEM((2 * SL, W), F32),
            pltpu.VMEM((HS, 2 * SL), BF16),
            pltpu.VMEM((HS, 2 * SL), BF16),
            pltpu.VMEM((2 * SL, D), BF16),
            pltpu.VMEM((2 * SL, D + W), BF16),
            pltpu.VMEM((SL, D), BF16),
            pltpu.VMEM((SL, D + W), BF16),
            pltpu.VMEM((SL, D), BF16),
            pltpu.VMEM((SL, D + W), BF16),
            pltpu.VMEM((2, ZL, T, W), BF16),
            pltpu.VMEM((2, ZL, 2, T, W), BF16),
            pltpu.VMEM((2, 6, T, W), BF16),
            pltpu.VMEM((NZ, 4, T), F32),
            pltpu.VMEM((E, T), F32),
            pltpu.VMEM((2, D // W, W), F32),
            pltpu.VMEM((D // W, W), F32),
            pltpu.VMEM((NZ, D // W, W), F32),
            pltpu.VMEM((NP, 2, D // W, W), F32),
            pltpu.VMEM((2, T, W), BF16),
            dma((8,)),
            dma((8,)),
            dma((2,)),
            dma((ZL,)),
            dma((ZL,)),
            dma((ZL,)),
            dma((6,)),
            dma((ZL, 2)),
            dma((ZL,)),
            dma((8, NP)),
            dma((8, NP)),
            dma((2, ZL)),
            dma((2, ZL, 2)),
            dma((2, 6)),
            dma((ZL,)),
            dma((NZ,)),
            dma((2, max(NP, NZ))),
            dma((2, max(NP, NZ))),
        ],
        compiler_params=pltpu.CompilerParams(
            collective_id=0, has_side_effects=True, vmem_limit_bytes=56 * 1024 * 1024
        ),
        name="experts",
    )(
        frames,
        norm_gain.reshape(1, D),
        router.T,
        jnp.pad(routes.T, ((0, 8 - routes.shape[1]), (0, 0))),
        w_in.reshape(D, HS),
        w_out.reshape(HS, D),
        cotangent,
    )
    column = lax.axis_index("expert")
    router_sum = sums[0].transpose(1, 0, 2, 3).reshape(E, D)
    d_router = router_sum.T * (1.0 / T)
    gain_sum = jnp.sum(sums[1, :, 0] + sums[1, :, 1], axis=0).reshape(D) * (1.0 / T)
    d_gain = (gain_sum + jnp.sum(router * d_router, axis=1)) / norm_gain
    d_gain = lax.dynamic_slice_in_dim(d_gain, column * (W // 2), W // 2, 0)
    return mixed, dfr, d_gain, d_router, gin.reshape(1, D, HS), gout.reshape(1, HS, D)


def plan(mesh):
    dp, ex = mesh.shape["dp"], mesh.shape["expert"]
    side = 4 if dp == 32 else 2
    return side, dp // 2 // side, ex // 2


def solution(mesh):
    placed = (
        P("dp", None),
        P(),
        P(),
        P("dp", None),
        P("dp", None, "expert"),
        P("dp", "expert", None),
        P("dp", "expert"),
    )
    return jax.shard_map(
        functools.partial(shards, plan(mesh)),
        mesh=mesh,
        in_specs=placed,
        out_specs=(
            P("dp", "expert"),
            P("dp", "expert"),
            P("expert"),
            P(),
            P("dp", None, "expert"),
            P("dp", "expert", None),
        ),
        check_vma=False,
    )
```

```python
import functools

import jax
import jax.numpy as jnp
from jax import lax
from jax.experimental import pallas as pl
from jax.experimental.pallas import tpu as pltpu
from jax.sharding import PartitionSpec as P

EPS = 1e-05
F32 = jnp.float32
BF16 = jnp.bfloat16
MESH = pl.DeviceIdType.MESH
NN = (((1,), (0,)), ((), ()))
NT = (((1,), (1,)), ((), ()))


def dot(a, b, dims=NN):
    return lax.dot_general(a, b, dims, preferred_element_type=F32)


def loop(lo, hi, body):
    def step(i, carry):
        body(i)
        return carry

    lax.fori_loop(lo, hi, step, 0)


PARENT = {1: 0, 2: 0, 3: 2, 4: 0, 5: 4, 6: 4, 7: 6, 8: 6}
LAST = {1: 0, 2: 1, 4: 2}
FLAT = {1: 0, 2: 0, 3: 2, 4: 2, 5: 0, 6: 5, 7: 5, 8: 5}
TREES = (PARENT, FLAT)
PARTS = (2, 4)


def children(tree, d, most):
    return [k for k in range(1, most + 1) if tree[k] == d]


def kernel(
    dims,
    frames,
    gain,
    routerT,
    routesT,
    w_in,
    w_out,
    cot,
    mixed,
    dfr,
    dgain,
    drouter,
    gin,
    gout,
    rt,
    nb,
    cotb,
    sibcot,
    stats,
    p0t,
    p1t,
    pcomb,
    send_n,
    send_c,
    rows_a,
    rows_c,
    hid,
    gates,
    ga_t,
    d_t,
    prodb,
    retb,
    sib_p,
    sib_r,
    got_p,
    got_r,
    part,
    relay,
    fin,
    scal,
    logits_t,
    vw,
    sibvw,
    vz,
    vp,
    vout,
    tail,
    sib_s,
    sib_q,
    rt_sem,
    nrm_s,
    nrm_q,
    chain_s,
    cot_s0,
    cot_s1,
    cot_q,
    xy_s,
    xy_q,
    up_s,
    relay_q,
    fin_q,
    sc_s,
    sc_q,
    vz_s,
    vz_q,
):
    X, Y, ZL = dims
    NP = X * Y
    NZ = 2 * ZL
    T, D = frames.shape
    SL = send_n.shape[0]
    CAP = SL // NP
    E = routerT.shape[0]
    W = 128
    reach = (ZL, ZL - 1)
    dp = lax.axis_index("dp")
    ex = lax.axis_index("expert")
    p = lax.rem(dp, NP)
    zh = dp // NP
    zl = ex // 2
    c = lax.rem(ex, 2)
    z = zh * ZL + zl
    x = p // Y
    y = lax.rem(p, Y)
    r = lax.rem(z + NZ - ZL * c, NZ)
    own = r < ZL
    sib_id = (dp, zl * 2 + 1 - c)

    def z_id(to):
        return ((to // ZL) * NP + p, lax.rem(to, ZL) * 2 + c)

    def z_at(way, hops):
        return z_id(lax.rem(z + (hops if way == 0 else NZ - hops), NZ))

    right = z_at(0, 1)
    left = z_at(1, 1)

    def plane(k, sign):
        px = lax.rem(x + X + sign * (k // Y), X)
        py = lax.rem(y + Y + sign * lax.rem(k, Y), Y)
        return px * Y + py

    def plane_id(k):
        return (zh * NP + plane(k, 1), ex)

    def remote(src, dst, ssem, rsem, to):
        return pltpu.make_async_remote_copy(
            src_ref=src, dst_ref=dst, send_sem=ssem, recv_sem=rsem, device_id=to, device_id_type=MESH
        )

    def sib(src, dst, i):
        return remote(src, dst, sib_s.at[i], sib_q.at[i], sib_id)

    barrier = pltpu.get_barrier_semaphore()

    def greet(to):
        pl.semaphore_signal(barrier, inc=1, device_id=to, device_id_type=MESH)

    greet(sib_id)
    loop(1, NP, lambda k: greet(plane_id(k)))
    loop(1, NZ, lambda k: greet(z_id(lax.rem(z + k, NZ))))

    @pl.when(own)
    def _():
        step = T // 8

        def norm(i):
            at = pl.ds(pl.multiple_of(i * step, step), step)
            values = frames[at, :].astype(F32)
            mean = jnp.mean(values, axis=1, keepdims=True)
            centred = values - mean
            inverse = lax.rsqrt(jnp.mean(centred * centred, axis=1, keepdims=True) + EPS)
            normed = (centred * inverse * gain[...]).astype(BF16)
            for s in range(ZL):
                nb[s, at, :] = normed[:, s * W : (s + 1) * W]
            stats[0, at, :] = jnp.broadcast_to(mean, (step, W))
            stats[1, at, :] = jnp.broadcast_to(inverse, (step, W))

        loop(0, 8, norm)
        rt[...] = routesT[...]

    pl.semaphore_wait(barrier, NP + NZ - 1)

    cot_copy = sib(cot, sibcot, 0)
    rt_copy = remote(rt, rt, rt_sem.at[0], rt_sem.at[1], z_id(lax.rem(z + ZL, NZ)))

    def nrm(s, to):
        return remote(nb.at[s], nb.at[s], nrm_s.at[s], nrm_q.at[s], to)

    def pass_on(s, to):
        return remote(cotb.at[s], cotb.at[s], chain_s.at[s], cot_q.at[s], to)

    def cot_copy_to(s, sem, way, hops):
        return remote(cotb.at[s], cotb.at[s], sem, cot_q.at[s], z_at(way, hops))

    def inside(way, hops):
        return (r + hops < ZL) if way == 0 else (r >= hops)

    def to_other_block(s, act):
        pl.when(r == ZL - 1)(lambda: act(pass_on(s, right)))
        pl.when(r == 0)(lambda: act(pass_on(s, left)))

    def cot_source(act):
        s = lax.rem(r, ZL)
        for d in (4, 2, 1):
            for way in (0, 1):
                copy = cot_copy_to(s, cot_s0.at[way * 3 + LAST[d]], way, d)
                pl.when(inside(way, d))(functools.partial(act, copy))
        to_other_block(s, act)

    def cot_relay(d, act, wait=True):
        for way in (0, 1):

            @pl.when(inside(1 - way, d))
            def _():
                s = lax.rem(r + (NZ - d if way == 0 else d), NZ)
                if wait:
                    cot_copy_to(s, cot_s1.at[s, 0], way, 1).wait_recv()
                for far in (d + 2, d + 1):
                    if far < ZL and PARENT[far] == d:
                        copy = cot_copy_to(s, cot_s1.at[s, far - d - 1], way, far - d)
                        pl.when(inside(way, far - d))(functools.partial(act, copy))
                if way == 0:
                    pl.when(r == ZL - 1)(lambda: act(pass_on(s, right)))
                else:
                    pl.when(r == 0)(lambda: act(pass_on(s, left)))

    def start(copy):
        copy.start()

    def sent(copy):
        copy.wait_send()

    near = r < ZL + ZL // 2
    onward_r = near & (r >= ZL) & (r < ZL + ZL // 2 - 1)
    onward_l = r > ZL + ZL // 2

    def positions():
        r0 = rt[0:1, :].astype(F32)
        r1 = rt[1:2, :].astype(F32)
        lanes = lax.broadcasted_iota(jnp.int32, (E, T), 0).astype(F32)
        e0 = jnp.where(lanes == r0, 1.0, 0.0)
        e1 = jnp.where(lanes == r1, 1.0, 0.0)
        before = lax.broadcasted_iota(jnp.int32, (T, T), 0) < lax.broadcasted_iota(
            jnp.int32, (T, T), 1
        )
        counts = dot((e0 + e1).astype(BF16), jnp.where(before, 1.0, 0.0).astype(BF16))
        base = (zh * NP).astype(F32)
        for rk, ek, pt, first in ((r0, e0, p0t, True), (r1, e1, p1t, False)):
            slot = jnp.sum(ek * counts, axis=0, keepdims=True)
            pos = (rk - base) * CAP + slot
            posc = jnp.transpose(jnp.broadcast_to(pos, (W, T)))
            for b in range(SL // W):
                down = (lax.broadcasted_iota(jnp.int32, (W, T), 0) + b * W).astype(F32)
                pt[b * W : (b + 1) * W, :] = jnp.where(down == pos, 1.0, 0.0).astype(BF16)
                across = (lax.broadcasted_iota(jnp.int32, (T, W), 1) + b * W).astype(F32)
                hit = jnp.where(across == posc, 1.0, 0.0).astype(BF16)
                if first:
                    pcomb[:, b * W : (b + 1) * W] = hit
                else:
                    pcomb[:, b * W : (b + 1) * W] += hit

    def half_cols(h):
        return pl.ds(pl.multiple_of(h * (D // 2), D // 2), D // 2)

    def xy(a, h, src, dst, k):
        return remote(
            src.at[pl.ds(pl.multiple_of(plane(k, 1) * CAP, CAP), CAP), half_cols(h)],
            dst.at[pl.ds(pl.multiple_of(c * SL + p * CAP, CAP), CAP), half_cols(h)],
            xy_s.at[2 * a + h, k],
            xy_q.at[2 * a + h, k],
            plane_id(k),
        )

    def xy_arrival(a, h, dst, k):
        here = dst.at[
            pl.ds(pl.multiple_of(c * SL + plane(k, -1) * CAP, CAP), CAP), half_cols(h)
        ]
        return remote(here, here, xy_s.at[2 * a + h, k], xy_q.at[2 * a + h, k], plane_id(k))

    def to_slots(pieces, send, s):
        pt = p0t[...] + p1t[...]
        send[:, pl.ds(pl.multiple_of(s * W, W), W)] = dot(pt, pieces[s]).astype(BF16)

    def go(a, h, send, dst):
        loop(1, NP, lambda k: xy(a, h, send, dst, k).start())

    def keep(send, dst):
        mine = pl.ds(pl.multiple_of(p * CAP, CAP), CAP)
        dst[pl.ds(pl.multiple_of(c * SL + p * CAP, CAP), CAP), :] = send[mine, :]

    order = [d for d in (1, 2, 4, 3, 6, 5, 7) if d < ZL]
    chain_order = [0] + order
    enough = max(chain_order.index(d) for d in range(ZL // 2))

    @pl.when(own)
    def _():
        rt_copy.start()
        pl.when(r == ZL - 1)(lambda: loop(0, ZL, lambda i: nrm(ZL - 1 - i, right).start()))
        pl.when(r == 0)(lambda: loop(0, ZL, lambda s: nrm(s, left).start()))
        cot_copy.wait_recv()
        one, two = cot[...].astype(F32), sibcot[...].astype(F32)

        @pl.when(c == 0)
        def _():
            cotb[r, :, :] = jnp.transpose(jnp.concatenate([one, two], axis=0)).astype(BF16)

        @pl.when(c == 1)
        def _():
            cotb[r, :, :] = jnp.transpose(jnp.concatenate([two, one], axis=0)).astype(BF16)

        cot_source(start)
        positions()
        for h in (0, 1):
            loop(h * (ZL // 2), (h + 1) * (ZL // 2), lambda s: to_slots(nb, send_n, s))
            go(0, h, send_n, rows_a)
        for d in order:
            cot_relay(d, start)
        for h in (0, 1):
            loop(h * (ZL // 2), (h + 1) * (ZL // 2), lambda s: to_slots(cotb, send_c, s))
            go(1, h, send_c, rows_c)

    @pl.when(jnp.logical_not(own))
    def _():
        cot_copy.start()
        rt_copy.wait_recv()
        positions()
        first = jnp.where(near, 1, 0)

        def take(copy, i):
            s = jnp.where(near, ZL - 1 - i, i)
            copy(s, right).wait_recv()
            pl.when(onward_r)(lambda: copy(s, right).start())
            pl.when(onward_l)(lambda: copy(s, left).start())
            return s

        loop(0, ZL // 2, lambda i: to_slots(nb, send_n, take(nrm, i)))
        go(0, first, send_n, rows_a)
        loop(ZL // 2, ZL, lambda i: to_slots(nb, send_n, take(nrm, i)))
        go(0, 1 - first, send_n, rows_a)
        for n, i in enumerate(chain_order):
            to_slots(cotb, send_c, take(pass_on, i))
            if n == enough:
                go(1, first, send_c, rows_c)
        go(1, 1 - first, send_c, rows_c)

    keep(send_n, rows_a)
    keep(send_c, rows_c)

    half = pl.ds(pl.multiple_of(c * SL, SL), SL)
    away = pl.ds(pl.multiple_of((1 - c) * SL, SL), SL)
    RT = 128
    tiles = SL // RT
    mine_rows = pl.ds(pl.multiple_of(c * SL + p * CAP, CAP), CAP)
    here_rows = pl.ds(pl.multiple_of(p * CAP, CAP), CAP)

    a_copy = sib(rows_a.at[half], rows_a.at[half], 1)
    for h in (0, 1):
        loop(1, NP, lambda k: xy_arrival(0, h, rows_a, k).wait_recv())
    a_copy.start()
    weight_in = w_in[...]
    weight_out = w_out[...]
    router_row = routerT[pl.ds(dp, 1), :]
    router_hi = router_row.astype(BF16)
    router_lo = (router_row - router_hi.astype(F32)).astype(BF16)
    router_hi = jnp.broadcast_to(router_hi, (16, D))
    router_lo = jnp.broadcast_to(router_lo, (16, D))

    def forward(i):
        at = pl.ds(pl.multiple_of(i * RT, RT), RT)
        arrived = rows_a[at, :]
        hidden = dot(arrived, weight_in)
        logit = dot(arrived, router_hi, NT) + dot(arrived, router_lo, NT)
        gate = jax.nn.sigmoid(logit[:, 0:1])
        active = hidden * jax.nn.sigmoid(hidden)
        ga = active.astype(BF16).astype(F32) * (0.5 * gate)
        hid[at, :] = hidden
        gates[at, :] = jnp.broadcast_to(gate, (RT, W))
        ga_t[:, at] = jnp.transpose(ga).astype(BF16)
        prodb[at, :] = dot(ga.astype(BF16), weight_out).astype(BF16)

    def pair_sum(buf, other, i):
        at = pl.ds(pl.multiple_of(i * RT, RT), RT)
        mine = pl.ds(pl.multiple_of(c * SL + i * RT, RT), RT)
        buf[mine, :] = (buf[mine, :].astype(F32) + other[at, :].astype(F32)).astype(BF16)

    def part_cols(a, h):
        off = a * W
        step = D // PARTS[a]
        return pl.ds(off + h * step, step) if h else pl.ds(0, off + step)

    def give(a, h, src, dst, k):
        cols = part_cols(a, h)
        return remote(
            src.at[pl.ds(pl.multiple_of(c * SL + plane(k, 1) * CAP, CAP), CAP), cols],
            dst.at[here_rows, cols],
            xy_s.at[4 + 2 * a + h, k],
            xy_q.at[4 + 2 * a + h, k],
            plane_id(k),
        )

    def give_arrival(a, h, dst, k):
        here = dst.at[pl.ds(pl.multiple_of(plane(k, -1) * CAP, CAP), CAP), part_cols(a, h)]
        return remote(here, here, xy_s.at[4 + 2 * a + h, k], xy_q.at[4 + 2 * a + h, k], plane_id(k))

    p_copy = sib(prodb.at[away], sib_p, 3)
    sib(rows_a.at[away], rows_a.at[away], 1).wait_recv()
    loop(0, tiles, lambda i: forward((1 - c) * tiles + i))
    p_copy.start()
    loop(0, tiles, lambda i: forward(c * tiles + i))
    p_copy.wait_recv()
    loop(0, tiles, lambda i: pair_sum(prodb, sib_p, i))
    for h in (0, 1):
        loop(1, NP, lambda k: give(0, h, prodb, got_p, k).start())
    got_p[here_rows, :] = prodb[mine_rows, :]

    c_copy = sib(rows_c.at[half], rows_c.at[half], 2)
    for h in (0, 1):
        loop(1, NP, lambda k: xy_arrival(1, h, rows_c, k).wait_recv())
    c_copy.start()
    gain_hi = gain[...].astype(BF16)
    gain_lo = (gain[...] - gain_hi.astype(F32)).astype(BF16)
    gw = (
        dot(jnp.broadcast_to(gain_hi, (16, D)), weight_in)
        + dot(jnp.broadcast_to(gain_lo, (16, D)), weight_in)
    )[0:1, :]
    vw[...] = jnp.zeros_like(vw)
    lane = lax.broadcasted_iota(jnp.int32, (RT, W), 1)

    def backward(i):
        at = pl.ds(pl.multiple_of(i * RT, RT), RT)
        hidden = hid[at, :]
        gate = gates[at, 0:1]
        sig = jax.nn.sigmoid(hidden)
        up = dot(rows_c[at, :], weight_out, NT) * (0.5 * gate)
        dh = up * (sig * (1.0 + hidden * (1.0 - sig)))
        d_t[:, at] = jnp.transpose(dh).astype(BF16)
        dgg = jnp.sum(up * (hidden * sig), axis=1, keepdims=True)
        s1 = jnp.sum(dh * gw, axis=1, keepdims=True)
        s2 = jnp.sum(dh * hidden, axis=1, keepdims=True)
        back = dot(dh.astype(BF16), weight_in, NT)
        retb[at, W : W + D] = back.astype(BF16)
        retb[at, 0:W] = jnp.where(
            lane == 0, dgg, jnp.where(lane == 1, s1, jnp.where(lane == 2, s2, 0.0))
        ).astype(BF16)
        wide = rows_a[at, :].astype(F32)
        v = jnp.sum(wide * (dgg * (1.0 - gate)), axis=0, keepdims=True)
        w = jnp.sum(wide * back, axis=0, keepdims=True)
        for b in range(D // W):
            vw[0, b : b + 1, :] += v[:, b * W : (b + 1) * W]
            vw[1, b : b + 1, :] += w[:, b * W : (b + 1) * W]

    r_copy = sib(retb.at[away], sib_r, 4)
    sib(rows_c.at[away], rows_c.at[away], 2).wait_recv()
    loop(0, tiles, lambda i: backward((1 - c) * tiles + i))
    r_copy.start()
    loop(0, tiles, lambda i: backward(c * tiles + i))
    v_copy = sib(vw.at[1 - c], sibvw, 5)
    v_copy.start()
    r_copy.wait_recv()
    loop(0, tiles, lambda i: pair_sum(retb, sib_r, i))
    for h in range(PARTS[1]):
        loop(1, NP, lambda k: give(1, h, retb, got_r, k).start())
    got_r[here_rows, :] = retb[mine_rows, :]

    v_copy.wait_recv()
    vz[z, :, :] = vw[c, :, :] + sibvw[...]

    def v_send(k):
        return remote(vz.at[z], vz.at[z], vz_s.at[0, k], vz_q.at[0, k], z_id(lax.rem(z + k, NZ)))

    def v_arrival(k):
        here = vz.at[lax.rem(z + NZ - k, NZ)]
        return remote(here, here, vz_s.at[0, k], vz_q.at[0, k], z_id(lax.rem(z + k, NZ)))

    loop(1, NZ, lambda k: v_send(k).start())

    def up(a, d, lo, hi, act, run=True):
        tree = TREES[a]
        for way in (0, 1):
            if d > reach[way]:
                continue
            to = lax.rem(r + (d if way == 0 else NZ - d), NZ)

            @pl.when((to >= lo) & (to < hi))
            def _():
                s = lax.rem(to, ZL)
                pd = tree[d]
                q = children(tree, pd, reach[way]).index(d)
                if pd == 0:
                    dst, sem = fin.at[a, way * 3 + q], fin_q.at[a, way * 3 + q]
                else:
                    dst, sem = relay.at[a, s, q], relay_q.at[a, s, q]
                if run:
                    kids = children(tree, d, reach[way])
                    total = None
                    for n in range(len(kids)):
                        landed = relay.at[a, s, n]
                        remote(landed, landed, up_s.at[a, s], relay_q.at[a, s, n], right).wait_recv()
                        if total is None:
                            total = part[a, s, :, :].astype(F32)
                        total = total + relay[a, s, n, :, :].astype(F32)
                    if kids:
                        part[a, s, :, :] = total.astype(BF16)
                act(remote(part.at[a, s], dst, up_s.at[a, s], sem, z_at(way, d - pd)))

    def combine(a, h, got):
        count = ZL // PARTS[a]
        first = h * count

        def one(i):
            s = first + i
            at = pl.ds(pl.multiple_of(a * W + s * W, W), W)
            part[a, s, :, :] = dot(pcomb[...], got[:, at]).astype(BF16)

        loop(1, NP, lambda k: give_arrival(a, h, got, k).wait_recv())
        loop(0, count, one)
        for d in (8, 7, 6, 5, 4, 3, 1, 2):
            if d <= ZL and not children(TREES[a], d, 8):
                up(a, d, first, first + count, start)

    def relays(a, ds, lo, hi):
        for d in ds:
            if d <= ZL:
                up(a, d, lo, hi, start)

    combine(0, 0, got_p)
    combine(0, 1, got_p)

    def grads(i):
        at = pl.ds(pl.multiple_of(i * W, W), W)
        gout[:, at] = dot(ga_t[...], rows_c[:, at]).astype(BF16)
        gin[at, :] = jnp.transpose(dot(d_t[...], rows_a[:, at])).astype(BF16)

    loop(0, D // W // 2, grads)

    def vp_send(k):
        return remote(vp.at[p], vp.at[p], vz_s.at[1, k], vz_q.at[1, k], plane_id(k))

    def vp_arrival(k):
        here = vp.at[plane(k, -1)]
        return remote(here, here, vz_s.at[1, k], vz_q.at[1, k], plane_id(k))

    router_all = routerT[...]

    @pl.when(own)
    def _():
        router_h = router_all.astype(BF16)
        router_l = (router_all - router_h.astype(F32)).astype(BF16)
        logits = jnp.zeros((E, T), F32)
        for b in range(ZL):
            at = slice(b * W, (b + 1) * W)
            logits += dot(router_h[:, at], nb[b], NT) + dot(router_l[:, at], nb[b], NT)
        logits_t[...] = logits

    relays(0, (6, 2), 0, ZL)
    loop(D // W // 2, D // W, grads)

    combine(1, 0, got_r)
    extra = jnp.transpose(got_r[:, 0:W].astype(F32)).astype(BF16)
    t0 = dot(extra, p0t[...])
    t1 = dot(extra, p1t[...])
    scal[z, 0:1, :] = t0[0:1, :]
    scal[z, 1:2, :] = t1[0:1, :]
    scal[z, 2:4, :] = t0[1:3, :] + t1[1:3, :]

    def sc_copy(s):
        to = lax.rem(s + ZL * c, NZ)
        return remote(scal.at[z], scal.at[z], sc_s.at[s], sc_q.at[z], z_id(to))

    def sc_arrival(k):
        here = scal.at[k]
        return remote(here, here, sc_s.at[0], sc_q.at[k], right)

    loop(0, ZL, lambda s: pl.when(s != r)(lambda: sc_copy(s).start()))
    relays(0, (4,), 0, ZL)
    loop(1, NZ, lambda k: v_arrival(k).wait_recv())
    vp[p, 0, :, :] = jnp.sum(vz[0:ZL], axis=0)
    vp[p, 1, :, :] = jnp.sum(vz[ZL:NZ], axis=0)
    loop(1, NP, lambda k: vp_send(k).start())
    quarter = ZL // PARTS[1]

    def relays_q(h):
        relays(1, (5, 2), h * quarter, (h + 1) * quarter)

    combine(1, 1, got_r)
    relays_q(0)
    combine(1, 2, got_r)
    relays_q(1)

    loop(1, NP, lambda k: vp_arrival(k).wait_recv())
    vp_copy = sib(vp, vout.at[c], 6)
    vp_copy.start()
    vout[c, :, :, :, :] = vp[...]

    combine(1, 3, got_r)
    relays_q(2)

    cols = pl.ds(pl.multiple_of(zl * W, W), W)
    sib(vp, vout.at[1 - c], 6).wait_recv()
    for q in range(NP):
        for up_half in (0, 1):
            e = up_half * NP + q
            for b in range(D // W):
                drouter[e : e + 1, b * W : (b + 1) * W] = vout[0, q, up_half, b : b + 1, :] * (1.0 / T)
    sibvw[...] = jnp.sum(jnp.sum(vout[1], axis=0), axis=0) * (1.0 / T)
    d_gain = sibvw[pl.ds(zl, 1), :] + jnp.sum(
        routerT[:, cols] * drouter[:, cols], axis=0, keepdims=True
    )
    d_gain = d_gain / gain[:, cols]

    @pl.when(c == 0)
    def _():
        dgain[...] = d_gain[:, 0 : W // 2]

    @pl.when(c == 1)
    def _():
        dgain[...] = d_gain[:, W // 2 : W]

    relays_q(3)

    t_copy = sib(tail, tail, 7)

    @pl.when(own)
    def _():
        s = lax.rem(r, ZL)
        logits = logits_t[...]
        r0 = rt[0:1, :].astype(F32)
        r1 = rt[1:2, :].astype(F32)
        ids = lax.broadcasted_iota(jnp.int32, (E, T), 0).astype(F32)
        rg = jnp.sum(router_all * gain[...], axis=1, keepdims=True)

        def sc_wait(k):
            pl.when(k != z)(lambda: sc_arrival(k).wait_recv())

        loop(0, NZ, sc_wait)
        total = jnp.sum(scal[...], axis=0)
        dl = jnp.where(ids == r0, total[0:1, :], 0.0) + jnp.where(ids == r1, total[1:2, :], 0.0)
        dl = dl * (1.0 - jax.nn.sigmoid(logits))
        sum_1 = total[2:3, :] + jnp.sum(dl * rg, axis=0, keepdims=True)
        sum_2 = total[3:4, :] + jnp.sum(dl * logits, axis=0, keepdims=True)
        sum_1 = jnp.transpose(jnp.broadcast_to(sum_1, (W, T))) * (1.0 / D)
        sum_2 = jnp.transpose(jnp.broadcast_to(sum_2, (W, T))) * (1.0 / D)
        dl_c = jnp.transpose(jnp.concatenate([dl, jnp.zeros((W - E, T), F32)], axis=0))
        router_cols = jnp.concatenate([routerT[:, cols], jnp.zeros((W - E, W), F32)], axis=0)
        second = dot(dl_c.astype(BF16), router_cols.astype(BF16))
        values = frames[:, cols].astype(F32)
        inverse = stats[1]
        scaled = (values - stats[0]) * inverse

        def arrived_sum(a):
            total = part[a, s, :, :].astype(F32)
            for way in (0, 1):
                for q in range(len(children(TREES[a], 0, reach[way]))):
                    landed = fin.at[a, way * 3 + q]
                    sem = fin_q.at[a, way * 3 + q]
                    remote(landed, landed, up_s.at[a, s], sem, right).wait_recv()
                    total = total + fin[a, way * 3 + q, :, :].astype(F32)
            return total

        out_m = jnp.transpose(values + arrived_sum(0)).astype(BF16)
        d_scaled = (arrived_sum(1) + second) * gain[:, cols]
        result = cotb[s, :, :].astype(F32) + inverse * (d_scaled - sum_1 - scaled * sum_2)
        out_d = jnp.transpose(result).astype(BF16)

        @pl.when(c == 0)
        def _():
            tail[0, :, :] = out_m[W // 2 : W, :]
            tail[1, :, :] = out_d[W // 2 : W, :]
            mixed[...] = out_m[0 : W // 2, :]
            dfr[...] = out_d[0 : W // 2, :]

        @pl.when(c == 1)
        def _():
            tail[0, :, :] = out_m[0 : W // 2, :]
            tail[1, :, :] = out_d[0 : W // 2, :]
            mixed[...] = out_m[W // 2 : W, :]
            dfr[...] = out_d[W // 2 : W, :]

        t_copy.start()

    @pl.when(jnp.logical_not(own))
    def _():
        t_copy.wait_recv()
        mixed[...] = tail[0, :, :]
        dfr[...] = tail[1, :, :]

    @pl.when(own)
    def _():
        t_copy.wait_send()
        rt_copy.wait_send()
        pl.when(r == ZL - 1)(lambda: loop(0, ZL, lambda s: nrm(s, right).wait_send()))
        pl.when(r == 0)(lambda: loop(0, ZL, lambda s: nrm(s, left).wait_send()))
        cot_source(sent)
        for d in order:
            cot_relay(d, sent, wait=False)

    @pl.when(jnp.logical_not(own))
    def _():
        cot_copy.wait_send()
        pl.when(onward_r | onward_l)(
            lambda: loop(0, ZL, lambda s: (nrm(s, right).wait_send(), pass_on(s, right).wait_send()))
        )

    def last_xy(k):
        for h in (0, 1):
            xy(0, h, send_n, rows_a, k).wait_send()
            xy(1, h, send_c, rows_c, k).wait_send()
            give(0, h, prodb, got_p, k).wait_send()
        for h in range(PARTS[1]):
            give(1, h, retb, got_r, k).wait_send()
        vp_send(k).wait_send()

    loop(1, NP, last_xy)
    loop(1, NZ, lambda k: v_send(k).wait_send())
    loop(0, ZL, lambda s: pl.when(s != r)(lambda: sc_copy(s).wait_send()))
    for d in range(1, ZL + 1):
        for a in (0, 1):
            up(a, d, 0, ZL, sent, run=False)
    for copy in (a_copy, c_copy, p_copy, r_copy, v_copy, vp_copy):
        copy.wait_send()


def shards(dims, frames, norm_gain, router, routes, w_in, w_out, cotangent):
    X, Y, ZL = dims
    NP, NZ, W = X * Y, 2 * ZL, 128
    T, D = frames.shape
    E = router.shape[1]
    CAP = 4 * routes.shape[1] * T // (3 * E)
    SL = NP * CAP
    HS = w_in.shape[2]
    vmem = pl.BlockSpec(memory_space=pltpu.VMEM)
    dma = pltpu.SemaphoreType.DMA
    mixed, dfr, d_gain, d_router, gin, gout = pl.pallas_call(
        functools.partial(kernel, dims),
        out_shape=[
            jax.ShapeDtypeStruct((W // 2, T), BF16),
            jax.ShapeDtypeStruct((W // 2, T), BF16),
            jax.ShapeDtypeStruct((1, W // 2), F32),
            jax.ShapeDtypeStruct((E, D), F32),
            jax.ShapeDtypeStruct((D, HS), BF16),
            jax.ShapeDtypeStruct((HS, D), BF16),
        ],
        in_specs=[vmem] * 7,
        out_specs=[vmem] * 6,
        scratch_shapes=[
            pltpu.VMEM((8, T), jnp.int32),
            pltpu.VMEM((ZL, T, W), BF16),
            pltpu.VMEM((ZL, T, W), BF16),
            pltpu.VMEM((W // 2, T), BF16),
            pltpu.VMEM((2, T, W), F32),
            pltpu.VMEM((SL, T), BF16),
            pltpu.VMEM((SL, T), BF16),
            pltpu.VMEM((T, SL), BF16),
            pltpu.VMEM((SL, D), BF16),
            pltpu.VMEM((SL, D), BF16),
            pltpu.VMEM((2 * SL, D), BF16),
            pltpu.VMEM((2 * SL, D), BF16),
            pltpu.VMEM((2 * SL, HS), F32),
            pltpu.VMEM((2 * SL, W), F32),
            pltpu.VMEM((HS, 2 * SL), BF16),
            pltpu.VMEM((HS, 2 * SL), BF16),
            pltpu.VMEM((2 * SL, D), BF16),
            pltpu.VMEM((2 * SL, D + W), BF16),
            pltpu.VMEM((SL, D), BF16),
            pltpu.VMEM((SL, D + W), BF16),
            pltpu.VMEM((SL, D), BF16),
            pltpu.VMEM((SL, D + W), BF16),
            pltpu.VMEM((2, ZL, T, W), BF16),
            pltpu.VMEM((2, ZL, 3, T, W), BF16),
            pltpu.VMEM((2, 6, T, W), BF16),
            pltpu.VMEM((NZ, 4, T), F32),
            pltpu.VMEM((E, T), F32),
            pltpu.VMEM((2, D // W, W), F32),
            pltpu.VMEM((D // W, W), F32),
            pltpu.VMEM((NZ, D // W, W), F32),
            pltpu.VMEM((NP, 2, D // W, W), F32),
            pltpu.VMEM((2, NP, 2, D // W, W), F32),
            pltpu.VMEM((2, W // 2, T), BF16),
            dma((8,)),
            dma((8,)),
            dma((2,)),
            dma((ZL,)),
            dma((ZL,)),
            dma((ZL,)),
            dma((6,)),
            dma((ZL, 2)),
            dma((ZL,)),
            dma((10, NP)),
            dma((10, NP)),
            dma((2, ZL)),
            dma((2, ZL, 3)),
            dma((2, 6)),
            dma((ZL,)),
            dma((NZ,)),
            dma((2, max(NP, NZ))),
            dma((2, max(NP, NZ))),
        ],
        compiler_params=pltpu.CompilerParams(
            collective_id=0, has_side_effects=True, vmem_limit_bytes=56 * 1024 * 1024
        ),
        name="experts",
    )(
        frames,
        norm_gain.reshape(1, D),
        router.T,
        jnp.pad(routes.T, ((0, 8 - routes.shape[1]), (0, 0))),
        w_in.reshape(D, HS),
        w_out.reshape(HS, D),
        cotangent.T,
    )
    d_gain = d_gain.reshape(W // 2)
    return mixed.T, dfr.T, d_gain, d_router.T, gin.reshape(1, D, HS), gout.reshape(1, HS, D)


def plan(mesh):
    dp, ex = mesh.shape["dp"], mesh.shape["expert"]
    side = 4 if dp == 32 else 2
    return side, dp // 2 // side, ex // 2


def solution(mesh):
    placed = (
        P("dp", None),
        P(),
        P(),
        P("dp", None),
        P("dp", None, "expert"),
        P("dp", "expert", None),
        P("dp", "expert"),
    )
    return jax.shard_map(
        functools.partial(shards, plan(mesh)),
        mesh=mesh,
        in_specs=placed,
        out_specs=(
            P("dp", "expert"),
            P("dp", "expert"),
            P("expert"),
            P(),
            P("dp", None, "expert"),
            P("dp", "expert", None),
        ),
        check_vma=False,
    )
```

```python
import functools

import jax
import jax.numpy as jnp
from jax import lax
from jax.experimental import pallas as pl
from jax.experimental.pallas import tpu as pltpu
from jax.sharding import PartitionSpec as P

EPS = 1e-05
F32 = jnp.float32
BF16 = jnp.bfloat16
MESH = pl.DeviceIdType.MESH
NN = (((1,), (0,)), ((), ()))
NT = (((1,), (1,)), ((), ()))


def dot(a, b, dims=NN):
    return lax.dot_general(a, b, dims, preferred_element_type=F32)


def loop(lo, hi, body):
    def step(i, carry):
        body(i)
        return carry

    lax.fori_loop(lo, hi, step, 0)


PARENT = {1: 0, 2: 0, 3: 2, 4: 0, 5: 4, 6: 4, 7: 6, 8: 6}
LAST = {1: 0, 2: 1, 4: 2}
SUM_TREE = {1: 0, 2: 1, 3: 2, 4: 0, 5: 4, 6: 5, 7: 4, 8: 7}


def children(tree, d, most):
    return [k for k in range(1, most + 1) if tree[k] == d]


def height(tree, d, most):
    return max([1 + height(tree, k, most) for k in children(tree, d, most)], default=0)


def kernel(
    dims,
    frames,
    gain,
    routerT,
    routesT,
    w_in,
    w_out,
    cot,
    mixed,
    dfr,
    dgain,
    drouter,
    gin,
    gout,
    rt,
    nb,
    cotb,
    sibcot,
    stats,
    p0t,
    p1t,
    pcomb,
    send_n,
    send_c,
    rows_a,
    rows_c,
    hid,
    gates,
    ga_t,
    d_t,
    prodb,
    retb,
    sib_p,
    sib_r,
    got_p,
    got_r,
    part,
    relay,
    fin,
    scal,
    logits_t,
    vw,
    sibvw,
    vz,
    vp,
    vout,
    tail,
    sib_s,
    sib_q,
    rt_sem,
    nrm_s,
    nrm_q,
    chain_s,
    cot_s0,
    cot_s1,
    cot_q,
    xy_s,
    xy_q,
    up_s,
    relay_q,
    fin_q,
    sc_s,
    sc_q,
    vz_s,
    vz_q,
):
    X, Y, ZL = dims
    NP = X * Y
    NZ = 2 * ZL
    T, D = frames.shape
    SL = send_n.shape[0]
    CAP = SL // NP
    E = routerT.shape[0]
    W = 128
    reach = (ZL, ZL - 1)
    dp = lax.axis_index("dp")
    ex = lax.axis_index("expert")
    p = lax.rem(dp, NP)
    zh = dp // NP
    zl = ex // 2
    c = lax.rem(ex, 2)
    z = zh * ZL + zl
    x = p // Y
    y = lax.rem(p, Y)
    r = lax.rem(z + NZ - ZL * c, NZ)
    own = r < ZL
    sib_id = (dp, zl * 2 + 1 - c)

    def z_id(to):
        return ((to // ZL) * NP + p, lax.rem(to, ZL) * 2 + c)

    def z_at(way, hops):
        return z_id(lax.rem(z + (hops if way == 0 else NZ - hops), NZ))

    right = z_at(0, 1)
    left = z_at(1, 1)

    def plane(k, sign):
        px = lax.rem(x + X + sign * (k // Y), X)
        py = lax.rem(y + Y + sign * lax.rem(k, Y), Y)
        return px * Y + py

    def plane_id(k):
        return (zh * NP + plane(k, 1), ex)

    def remote(src, dst, ssem, rsem, to):
        return pltpu.make_async_remote_copy(
            src_ref=src, dst_ref=dst, send_sem=ssem, recv_sem=rsem, device_id=to, device_id_type=MESH
        )

    def sib(src, dst, i):
        return remote(src, dst, sib_s.at[i], sib_q.at[i], sib_id)

    barrier = pltpu.get_barrier_semaphore()

    def greet(to):
        pl.semaphore_signal(barrier, inc=1, device_id=to, device_id_type=MESH)

    greet(sib_id)
    loop(1, NP, lambda k: greet(plane_id(k)))
    loop(1, NZ, lambda k: greet(z_id(lax.rem(z + k, NZ))))

    @pl.when(own)
    def _():
        step = T // 8

        def norm(i):
            at = pl.ds(pl.multiple_of(i * step, step), step)
            values = frames[at, :].astype(F32)
            mean = jnp.mean(values, axis=1, keepdims=True)
            centred = values - mean
            inverse = lax.rsqrt(jnp.mean(centred * centred, axis=1, keepdims=True) + EPS)
            normed = (centred * inverse * gain[...]).astype(BF16)
            for s in range(ZL):
                nb[s, at, :] = normed[:, s * W : (s + 1) * W]
            stats[0, at, :] = jnp.broadcast_to(mean, (step, W))
            stats[1, at, :] = jnp.broadcast_to(inverse, (step, W))

        loop(0, 8, norm)
        rt[...] = routesT[...]

    pl.semaphore_wait(barrier, NP + NZ - 1)

    cot_copy = sib(cot, sibcot, 0)
    rt_copy = remote(rt, rt, rt_sem.at[0], rt_sem.at[1], z_id(lax.rem(z + ZL, NZ)))

    def nrm(s, to):
        return remote(nb.at[s], nb.at[s], nrm_s.at[s], nrm_q.at[s], to)

    def pass_on(s, to):
        return remote(cotb.at[s], cotb.at[s], chain_s.at[s], cot_q.at[s], to)

    def cot_copy_to(s, sem, way, hops):
        return remote(cotb.at[s], cotb.at[s], sem, cot_q.at[s], z_at(way, hops))

    def inside(way, hops):
        return (r + hops < ZL) if way == 0 else (r >= hops)

    def to_other_block(s, act):
        pl.when(r == ZL - 1)(lambda: act(pass_on(s, right)))
        pl.when(r == 0)(lambda: act(pass_on(s, left)))

    def cot_source(act):
        s = lax.rem(r, ZL)
        for d in (4, 2, 1):
            for way in (0, 1):
                copy = cot_copy_to(s, cot_s0.at[way * 3 + LAST[d]], way, d)
                pl.when(inside(way, d))(functools.partial(act, copy))
        to_other_block(s, act)

    def cot_relay(d, act, wait=True):
        for way in (0, 1):

            @pl.when(inside(1 - way, d))
            def _():
                s = lax.rem(r + (NZ - d if way == 0 else d), NZ)
                if wait:
                    cot_copy_to(s, cot_s1.at[s, 0], way, 1).wait_recv()
                for far in (d + 2, d + 1):
                    if far < ZL and PARENT[far] == d:
                        copy = cot_copy_to(s, cot_s1.at[s, far - d - 1], way, far - d)
                        pl.when(inside(way, far - d))(functools.partial(act, copy))
                if way == 0:
                    pl.when(r == ZL - 1)(lambda: act(pass_on(s, right)))
                else:
                    pl.when(r == 0)(lambda: act(pass_on(s, left)))

    def start(copy):
        copy.start()

    def sent(copy):
        copy.wait_send()

    near = r < ZL + ZL // 2
    onward_r = near & (r >= ZL) & (r < ZL + ZL // 2 - 1)
    onward_l = r > ZL + ZL // 2

    def positions():
        r0 = rt[0:1, :].astype(F32)
        r1 = rt[1:2, :].astype(F32)
        lanes = lax.broadcasted_iota(jnp.int32, (E, T), 0).astype(F32)
        e0 = jnp.where(lanes == r0, 1.0, 0.0)
        e1 = jnp.where(lanes == r1, 1.0, 0.0)
        before = lax.broadcasted_iota(jnp.int32, (T, T), 0) < lax.broadcasted_iota(
            jnp.int32, (T, T), 1
        )
        counts = dot((e0 + e1).astype(BF16), jnp.where(before, 1.0, 0.0).astype(BF16))
        base = (zh * NP).astype(F32)
        for rk, ek, pt, first in ((r0, e0, p0t, True), (r1, e1, p1t, False)):
            slot = jnp.sum(ek * counts, axis=0, keepdims=True)
            pos = (rk - base) * CAP + slot
            posc = jnp.transpose(jnp.broadcast_to(pos, (W, T)))
            for b in range(SL // W):
                down = (lax.broadcasted_iota(jnp.int32, (W, T), 0) + b * W).astype(F32)
                pt[b * W : (b + 1) * W, :] = jnp.where(down == pos, 1.0, 0.0).astype(BF16)
                across = (lax.broadcasted_iota(jnp.int32, (T, W), 1) + b * W).astype(F32)
                hit = jnp.where(across == posc, 1.0, 0.0).astype(BF16)
                if first:
                    pcomb[:, b * W : (b + 1) * W] = hit
                else:
                    pcomb[:, b * W : (b + 1) * W] += hit

    def half_cols(h):
        return pl.ds(pl.multiple_of(h * (D // 2), D // 2), D // 2)

    def xy(a, h, src, dst, k):
        return remote(
            src.at[pl.ds(pl.multiple_of(plane(k, 1) * CAP, CAP), CAP), half_cols(h)],
            dst.at[pl.ds(pl.multiple_of(c * SL + p * CAP, CAP), CAP), half_cols(h)],
            xy_s.at[2 * a + h, k],
            xy_q.at[2 * a + h, k],
            plane_id(k),
        )

    def xy_arrival(a, h, dst, k):
        here = dst.at[
            pl.ds(pl.multiple_of(c * SL + plane(k, -1) * CAP, CAP), CAP), half_cols(h)
        ]
        return remote(here, here, xy_s.at[2 * a + h, k], xy_q.at[2 * a + h, k], plane_id(k))

    def to_slots(pieces, send, s):
        pt = p0t[...] + p1t[...]
        send[:, pl.ds(pl.multiple_of(s * W, W), W)] = dot(pt, pieces[s]).astype(BF16)

    def go(a, h, send, dst):
        loop(1, NP, lambda k: xy(a, h, send, dst, k).start())

    def keep(send, dst):
        mine = pl.ds(pl.multiple_of(p * CAP, CAP), CAP)
        dst[pl.ds(pl.multiple_of(c * SL + p * CAP, CAP), CAP), :] = send[mine, :]

    order = [d for d in (1, 2, 4, 3, 6, 5, 7) if d < ZL]
    chain_order = [0] + order
    enough = max(chain_order.index(d) for d in range(ZL // 2))

    @pl.when(own)
    def _():
        rt_copy.start()
        pl.when(r == ZL - 1)(lambda: loop(0, ZL, lambda i: nrm(ZL - 1 - i, right).start()))
        pl.when(r == 0)(lambda: loop(0, ZL, lambda s: nrm(s, left).start()))
        cot_copy.wait_recv()
        one, two = cot[...].astype(F32), sibcot[...].astype(F32)

        @pl.when(c == 0)
        def _():
            cotb[r, :, :] = jnp.transpose(jnp.concatenate([one, two], axis=0)).astype(BF16)

        @pl.when(c == 1)
        def _():
            cotb[r, :, :] = jnp.transpose(jnp.concatenate([two, one], axis=0)).astype(BF16)

        cot_source(start)
        positions()
        for h in (0, 1):
            loop(h * (ZL // 2), (h + 1) * (ZL // 2), lambda s: to_slots(nb, send_n, s))
            go(0, h, send_n, rows_a)
        for d in order:
            cot_relay(d, start)
        for h in (0, 1):
            loop(h * (ZL // 2), (h + 1) * (ZL // 2), lambda s: to_slots(cotb, send_c, s))
            go(1, h, send_c, rows_c)

    @pl.when(jnp.logical_not(own))
    def _():
        cot_copy.start()
        rt_copy.wait_recv()
        positions()
        first = jnp.where(near, 1, 0)

        def take(copy, i):
            s = jnp.where(near, ZL - 1 - i, i)
            copy(s, right).wait_recv()
            pl.when(onward_r)(lambda: copy(s, right).start())
            pl.when(onward_l)(lambda: copy(s, left).start())
            return s

        loop(0, ZL // 2, lambda i: to_slots(nb, send_n, take(nrm, i)))
        go(0, first, send_n, rows_a)
        loop(ZL // 2, ZL, lambda i: to_slots(nb, send_n, take(nrm, i)))
        go(0, 1 - first, send_n, rows_a)
        for n, i in enumerate(chain_order):
            to_slots(cotb, send_c, take(pass_on, i))
            if n == enough:
                go(1, first, send_c, rows_c)
        go(1, 1 - first, send_c, rows_c)

    keep(send_n, rows_a)
    keep(send_c, rows_c)

    half = pl.ds(pl.multiple_of(c * SL, SL), SL)
    away = pl.ds(pl.multiple_of((1 - c) * SL, SL), SL)
    RT = 128
    tiles = SL // RT
    mine_rows = pl.ds(pl.multiple_of(c * SL + p * CAP, CAP), CAP)
    here_rows = pl.ds(pl.multiple_of(p * CAP, CAP), CAP)

    a_copy = sib(rows_a.at[half], rows_a.at[half], 1)
    for h in (0, 1):
        loop(1, NP, lambda k: xy_arrival(0, h, rows_a, k).wait_recv())
    a_copy.start()
    weight_in = w_in[...]
    weight_out = w_out[...]
    router_row = routerT[pl.ds(dp, 1), :]
    router_hi = router_row.astype(BF16)
    router_lo = (router_row - router_hi.astype(F32)).astype(BF16)
    router_hi = jnp.broadcast_to(router_hi, (16, D))
    router_lo = jnp.broadcast_to(router_lo, (16, D))

    def forward(i):
        at = pl.ds(pl.multiple_of(i * RT, RT), RT)
        arrived = rows_a[at, :]
        hidden = dot(arrived, weight_in)
        logit = dot(arrived, router_hi, NT) + dot(arrived, router_lo, NT)
        gate = jax.nn.sigmoid(logit[:, 0:1])
        active = hidden * jax.nn.sigmoid(hidden)
        ga = active.astype(BF16).astype(F32) * (0.5 * gate)
        hid[at, :] = hidden
        gates[at, :] = jnp.broadcast_to(gate, (RT, W))
        ga_t[:, at] = jnp.transpose(ga).astype(BF16)
        prodb[at, :] = dot(ga.astype(BF16), weight_out).astype(BF16)

    def pair_sum(buf, other, i):
        at = pl.ds(pl.multiple_of(i * RT, RT), RT)
        mine = pl.ds(pl.multiple_of(c * SL + i * RT, RT), RT)
        buf[mine, :] = (buf[mine, :].astype(F32) + other[at, :].astype(F32)).astype(BF16)

    def give(a, src, dst, k):
        return remote(
            src.at[pl.ds(pl.multiple_of(c * SL + plane(k, 1) * CAP, CAP), CAP)],
            dst.at[here_rows],
            xy_s.at[4 + a, k],
            xy_q.at[4 + a, k],
            plane_id(k),
        )

    def give_arrival(a, dst, k):
        here = dst.at[pl.ds(pl.multiple_of(plane(k, -1) * CAP, CAP), CAP)]
        return remote(here, here, xy_s.at[4 + a, k], xy_q.at[4 + a, k], plane_id(k))

    p_copy = sib(prodb.at[away], sib_p, 3)
    sib(rows_a.at[away], rows_a.at[away], 1).wait_recv()
    loop(0, tiles, lambda i: forward((1 - c) * tiles + i))
    p_copy.start()
    loop(0, tiles, lambda i: forward(c * tiles + i))
    p_copy.wait_recv()
    loop(0, tiles, lambda i: pair_sum(prodb, sib_p, i))
    loop(1, NP, lambda k: give(0, prodb, got_p, k).start())
    got_p[here_rows, :] = prodb[mine_rows, :]

    c_copy = sib(rows_c.at[half], rows_c.at[half], 2)
    for h in (0, 1):
        loop(1, NP, lambda k: xy_arrival(1, h, rows_c, k).wait_recv())
    c_copy.start()
    gain_hi = gain[...].astype(BF16)
    gain_lo = (gain[...] - gain_hi.astype(F32)).astype(BF16)
    gw = (
        dot(jnp.broadcast_to(gain_hi, (16, D)), weight_in)
        + dot(jnp.broadcast_to(gain_lo, (16, D)), weight_in)
    )[0:1, :]
    vw[...] = jnp.zeros_like(vw)
    lane = lax.broadcasted_iota(jnp.int32, (RT, W), 1)

    def backward(i):
        at = pl.ds(pl.multiple_of(i * RT, RT), RT)
        hidden = hid[at, :]
        gate = gates[at, 0:1]
        sig = jax.nn.sigmoid(hidden)
        up = dot(rows_c[at, :], weight_out, NT) * (0.5 * gate)
        dh = up * (sig * (1.0 + hidden * (1.0 - sig)))
        d_t[:, at] = jnp.transpose(dh).astype(BF16)
        dgg = jnp.sum(up * (hidden * sig), axis=1, keepdims=True)
        s1 = jnp.sum(dh * gw, axis=1, keepdims=True)
        s2 = jnp.sum(dh * hidden, axis=1, keepdims=True)
        back = dot(dh.astype(BF16), weight_in, NT)
        retb[at, W : W + D] = back.astype(BF16)
        retb[at, 0:W] = jnp.where(
            lane == 0, dgg, jnp.where(lane == 1, s1, jnp.where(lane == 2, s2, 0.0))
        ).astype(BF16)
        wide = rows_a[at, :].astype(F32)
        v = jnp.sum(wide * (dgg * (1.0 - gate)), axis=0, keepdims=True)
        w = jnp.sum(wide * back, axis=0, keepdims=True)
        for b in range(D // W):
            vw[0, b : b + 1, :] += v[:, b * W : (b + 1) * W]
            vw[1, b : b + 1, :] += w[:, b * W : (b + 1) * W]

    r_copy = sib(retb.at[away], sib_r, 4)
    sib(rows_c.at[away], rows_c.at[away], 2).wait_recv()
    loop(0, tiles, lambda i: backward((1 - c) * tiles + i))
    r_copy.start()
    loop(0, tiles, lambda i: backward(c * tiles + i))
    v_copy = sib(vw.at[1 - c], sibvw, 5)
    v_copy.start()
    r_copy.wait_recv()
    loop(0, tiles, lambda i: pair_sum(retb, sib_r, i))
    loop(1, NP, lambda k: give(1, retb, got_r, k).start())
    got_r[here_rows, :] = retb[mine_rows, :]

    v_copy.wait_recv()
    vz[z, :, :] = vw[c, :, :] + sibvw[...]

    def v_send(k):
        return remote(vz.at[z], vz.at[z], vz_s.at[0, k], vz_q.at[0, k], z_id(lax.rem(z + k, NZ)))

    def v_arrival(k):
        here = vz.at[lax.rem(z + NZ - k, NZ)]
        return remote(here, here, vz_s.at[0, k], vz_q.at[0, k], z_id(lax.rem(z + k, NZ)))

    loop(1, NZ, lambda k: v_send(k).start())

    def up(a, d, way, act, run=True):
        to = lax.rem(r + (d if way == 0 else NZ - d), NZ)

        @pl.when(to < ZL)
        def _():
            s = lax.rem(to, ZL)
            pd = SUM_TREE[d]
            q = children(SUM_TREE, pd, reach[way]).index(d)
            if pd == 0:
                dst, sem = fin.at[a, way * 3 + q], fin_q.at[a, way * 3 + q]
            else:
                dst, sem = relay.at[a, s, q], relay_q.at[a, s, q]
            kids = children(SUM_TREE, d, reach[way])
            if run and kids:
                total = part[a, s, :, :].astype(F32)
                for n in range(len(kids)):
                    landed = relay.at[a, s, n]
                    remote(landed, landed, up_s.at[a, s], relay_q.at[a, s, n], right).wait_recv()
                    total = total + relay[a, s, n, :, :].astype(F32)
                part[a, s, :, :] = total.astype(BF16)
            act(remote(part.at[a, s], dst, up_s.at[a, s], sem, z_at(way, d - pd)))

    def stage(a, level):
        for d in range(ZL, 0, -1):
            for way in (0, 1):
                if d <= reach[way] and height(SUM_TREE, d, reach[way]) == level:
                    up(a, d, way, start)

    def combine(a, got):
        def one(s):
            at = pl.ds(pl.multiple_of(a * W + s * W, W), W)
            part[a, s, :, :] = dot(pcomb[...], got[:, at]).astype(BF16)

        loop(1, NP, lambda k: give_arrival(a, got, k).wait_recv())
        loop(0, ZL, one)
        stage(a, 0)

    combine(0, got_p)

    def grads(i):
        at = pl.ds(pl.multiple_of(i * W, W), W)
        gout[:, at] = dot(ga_t[...], rows_c[:, at]).astype(BF16)
        gin[at, :] = jnp.transpose(dot(d_t[...], rows_a[:, at])).astype(BF16)

    loop(0, D // W // 2, grads)

    def vp_send(k):
        return remote(vp.at[p], vp.at[p], vz_s.at[1, k], vz_q.at[1, k], plane_id(k))

    def vp_arrival(k):
        here = vp.at[plane(k, -1)]
        return remote(here, here, vz_s.at[1, k], vz_q.at[1, k], plane_id(k))

    router_all = routerT[...]

    @pl.when(own)
    def _():
        router_h = router_all.astype(BF16)
        router_l = (router_all - router_h.astype(F32)).astype(BF16)
        logits = jnp.zeros((E, T), F32)
        for b in range(ZL):
            at = slice(b * W, (b + 1) * W)
            logits += dot(router_h[:, at], nb[b], NT) + dot(router_l[:, at], nb[b], NT)
        logits_t[...] = logits

    stage(0, 1)
    loop(D // W // 2, D // W, grads)
    loop(1, NZ, lambda k: v_arrival(k).wait_recv())
    vp[p, 0, :, :] = jnp.sum(vz[0:ZL], axis=0)
    vp[p, 1, :, :] = jnp.sum(vz[ZL:NZ], axis=0)
    loop(1, NP, lambda k: vp_send(k).start())
    stage(0, 2)

    combine(1, got_r)
    extra = jnp.transpose(got_r[:, 0:W].astype(F32)).astype(BF16)
    t0 = dot(extra, p0t[...])
    t1 = dot(extra, p1t[...])
    scal[z, 0:1, :] = t0[0:1, :]
    scal[z, 1:2, :] = t1[0:1, :]
    scal[z, 2:4, :] = t0[1:3, :] + t1[1:3, :]

    def sc_copy(s):
        to = lax.rem(s + ZL * c, NZ)
        return remote(scal.at[z], scal.at[z], sc_s.at[s], sc_q.at[z], z_id(to))

    def sc_arrival(k):
        here = scal.at[k]
        return remote(here, here, sc_s.at[0], sc_q.at[k], right)

    loop(0, ZL, lambda s: pl.when(s != r)(lambda: sc_copy(s).start()))
    loop(1, NP, lambda k: vp_arrival(k).wait_recv())
    vp_copy = sib(vp, vout.at[c], 6)
    vp_copy.start()
    vout[c, :, :, :, :] = vp[...]

    stage(1, 1)

    cols = pl.ds(pl.multiple_of(zl * W, W), W)
    sib(vp, vout.at[1 - c], 6).wait_recv()
    for q in range(NP):
        for up_half in (0, 1):
            e = up_half * NP + q
            for b in range(D // W):
                drouter[e : e + 1, b * W : (b + 1) * W] = vout[0, q, up_half, b : b + 1, :] * (1.0 / T)
    sibvw[...] = jnp.sum(jnp.sum(vout[1], axis=0), axis=0) * (1.0 / T)
    d_gain = sibvw[pl.ds(zl, 1), :] + jnp.sum(
        routerT[:, cols] * drouter[:, cols], axis=0, keepdims=True
    )
    d_gain = d_gain / gain[:, cols]

    @pl.when(c == 0)
    def _():
        dgain[...] = d_gain[:, 0 : W // 2]

    @pl.when(c == 1)
    def _():
        dgain[...] = d_gain[:, W // 2 : W]

    stage(1, 2)

    t_copy = sib(tail, tail, 7)

    @pl.when(own)
    def _():
        s = lax.rem(r, ZL)
        logits = logits_t[...]
        r0 = rt[0:1, :].astype(F32)
        r1 = rt[1:2, :].astype(F32)
        ids = lax.broadcasted_iota(jnp.int32, (E, T), 0).astype(F32)
        rg = jnp.sum(router_all * gain[...], axis=1, keepdims=True)

        def sc_wait(k):
            pl.when(k != z)(lambda: sc_arrival(k).wait_recv())

        loop(0, NZ, sc_wait)
        total = jnp.sum(scal[...], axis=0)
        dl = jnp.where(ids == r0, total[0:1, :], 0.0) + jnp.where(ids == r1, total[1:2, :], 0.0)
        dl = dl * (1.0 - jax.nn.sigmoid(logits))
        sum_1 = total[2:3, :] + jnp.sum(dl * rg, axis=0, keepdims=True)
        sum_2 = total[3:4, :] + jnp.sum(dl * logits, axis=0, keepdims=True)
        sum_1 = jnp.transpose(jnp.broadcast_to(sum_1, (W, T))) * (1.0 / D)
        sum_2 = jnp.transpose(jnp.broadcast_to(sum_2, (W, T))) * (1.0 / D)
        dl_c = jnp.transpose(jnp.concatenate([dl, jnp.zeros((W - E, T), F32)], axis=0))
        router_cols = jnp.concatenate([routerT[:, cols], jnp.zeros((W - E, W), F32)], axis=0)
        second = dot(dl_c.astype(BF16), router_cols.astype(BF16))
        values = frames[:, cols].astype(F32)
        inverse = stats[1]
        scaled = (values - stats[0]) * inverse

        def arrived_sum(a):
            total = part[a, s, :, :].astype(F32)
            for way in (0, 1):
                for q in range(len(children(SUM_TREE, 0, reach[way]))):
                    landed = fin.at[a, way * 3 + q]
                    sem = fin_q.at[a, way * 3 + q]
                    remote(landed, landed, up_s.at[a, s], sem, right).wait_recv()
                    total = total + fin[a, way * 3 + q, :, :].astype(F32)
            return total

        out_m = jnp.transpose(values + arrived_sum(0)).astype(BF16)
        d_scaled = (arrived_sum(1) + second) * gain[:, cols]
        result = cotb[s, :, :].astype(F32) + inverse * (d_scaled - sum_1 - scaled * sum_2)
        out_d = jnp.transpose(result).astype(BF16)

        @pl.when(c == 0)
        def _():
            tail[0, :, :] = out_m[W // 2 : W, :]
            tail[1, :, :] = out_d[W // 2 : W, :]
            mixed[...] = out_m[0 : W // 2, :]
            dfr[...] = out_d[0 : W // 2, :]

        @pl.when(c == 1)
        def _():
            tail[0, :, :] = out_m[0 : W // 2, :]
            tail[1, :, :] = out_d[0 : W // 2, :]
            mixed[...] = out_m[W // 2 : W, :]
            dfr[...] = out_d[W // 2 : W, :]

        t_copy.start()

    @pl.when(jnp.logical_not(own))
    def _():
        t_copy.wait_recv()
        mixed[...] = tail[0, :, :]
        dfr[...] = tail[1, :, :]

    @pl.when(own)
    def _():
        t_copy.wait_send()
        rt_copy.wait_send()
        pl.when(r == ZL - 1)(lambda: loop(0, ZL, lambda s: nrm(s, right).wait_send()))
        pl.when(r == 0)(lambda: loop(0, ZL, lambda s: nrm(s, left).wait_send()))
        cot_source(sent)
        for d in order:
            cot_relay(d, sent, wait=False)

    @pl.when(jnp.logical_not(own))
    def _():
        cot_copy.wait_send()
        pl.when(onward_r | onward_l)(
            lambda: loop(0, ZL, lambda s: (nrm(s, right).wait_send(), pass_on(s, right).wait_send()))
        )

    def last_xy(k):
        for h in (0, 1):
            xy(0, h, send_n, rows_a, k).wait_send()
            xy(1, h, send_c, rows_c, k).wait_send()
        give(0, prodb, got_p, k).wait_send()
        give(1, retb, got_r, k).wait_send()
        vp_send(k).wait_send()

    loop(1, NP, last_xy)
    loop(1, NZ, lambda k: v_send(k).wait_send())
    loop(0, ZL, lambda s: pl.when(s != r)(lambda: sc_copy(s).wait_send()))
    for d in range(1, ZL + 1):
        for a in (0, 1):
            for way in (0, 1):
                if d <= reach[way]:
                    up(a, d, way, sent, run=False)
    for copy in (a_copy, c_copy, p_copy, r_copy, v_copy, vp_copy):
        copy.wait_send()


def shards(dims, frames, norm_gain, router, routes, w_in, w_out, cotangent):
    X, Y, ZL = dims
    NP, NZ, W = X * Y, 2 * ZL, 128
    T, D = frames.shape
    E = router.shape[1]
    CAP = 4 * routes.shape[1] * T // (3 * E)
    SL = NP * CAP
    HS = w_in.shape[2]
    vmem = pl.BlockSpec(memory_space=pltpu.VMEM)
    dma = pltpu.SemaphoreType.DMA
    mixed, dfr, d_gain, d_router, gin, gout = pl.pallas_call(
        functools.partial(kernel, dims),
        out_shape=[
            jax.ShapeDtypeStruct((W // 2, T), BF16),
            jax.ShapeDtypeStruct((W // 2, T), BF16),
            jax.ShapeDtypeStruct((1, W // 2), F32),
            jax.ShapeDtypeStruct((E, D), F32),
            jax.ShapeDtypeStruct((D, HS), BF16),
            jax.ShapeDtypeStruct((HS, D), BF16),
        ],
        in_specs=[vmem] * 7,
        out_specs=[vmem] * 6,
        scratch_shapes=[
            pltpu.VMEM((8, T), jnp.int32),
            pltpu.VMEM((ZL, T, W), BF16),
            pltpu.VMEM((ZL, T, W), BF16),
            pltpu.VMEM((W // 2, T), BF16),
            pltpu.VMEM((2, T, W), F32),
            pltpu.VMEM((SL, T), BF16),
            pltpu.VMEM((SL, T), BF16),
            pltpu.VMEM((T, SL), BF16),
            pltpu.VMEM((SL, D), BF16),
            pltpu.VMEM((SL, D), BF16),
            pltpu.VMEM((2 * SL, D), BF16),
            pltpu.VMEM((2 * SL, D), BF16),
            pltpu.VMEM((2 * SL, HS), F32),
            pltpu.VMEM((2 * SL, W), F32),
            pltpu.VMEM((HS, 2 * SL), BF16),
            pltpu.VMEM((HS, 2 * SL), BF16),
            pltpu.VMEM((2 * SL, D), BF16),
            pltpu.VMEM((2 * SL, D + W), BF16),
            pltpu.VMEM((SL, D), BF16),
            pltpu.VMEM((SL, D + W), BF16),
            pltpu.VMEM((SL, D), BF16),
            pltpu.VMEM((SL, D + W), BF16),
            pltpu.VMEM((2, ZL, T, W), BF16),
            pltpu.VMEM((2, ZL, 3, T, W), BF16),
            pltpu.VMEM((2, 6, T, W), BF16),
            pltpu.VMEM((NZ, 4, T), F32),
            pltpu.VMEM((E, T), F32),
            pltpu.VMEM((2, D // W, W), F32),
            pltpu.VMEM((D // W, W), F32),
            pltpu.VMEM((NZ, D // W, W), F32),
            pltpu.VMEM((NP, 2, D // W, W), F32),
            pltpu.VMEM((2, NP, 2, D // W, W), F32),
            pltpu.VMEM((2, W // 2, T), BF16),
            dma((8,)),
            dma((8,)),
            dma((2,)),
            dma((ZL,)),
            dma((ZL,)),
            dma((ZL,)),
            dma((6,)),
            dma((ZL, 2)),
            dma((ZL,)),
            dma((6, NP)),
            dma((6, NP)),
            dma((2, ZL)),
            dma((2, ZL, 3)),
            dma((2, 6)),
            dma((ZL,)),
            dma((NZ,)),
            dma((2, max(NP, NZ))),
            dma((2, max(NP, NZ))),
        ],
        compiler_params=pltpu.CompilerParams(
            collective_id=0, has_side_effects=True, vmem_limit_bytes=56 * 1024 * 1024
        ),
        name="experts",
    )(
        frames,
        norm_gain.reshape(1, D),
        router.T,
        jnp.pad(routes.T, ((0, 8 - routes.shape[1]), (0, 0))),
        w_in.reshape(D, HS),
        w_out.reshape(HS, D),
        cotangent.T,
    )
    d_gain = d_gain.reshape(W // 2)
    return mixed.T, dfr.T, d_gain, d_router.T, gin.reshape(1, D, HS), gout.reshape(1, HS, D)


def plan(mesh):
    dp, ex = mesh.shape["dp"], mesh.shape["expert"]
    side = 4 if dp == 32 else 2
    return side, dp // 2 // side, ex // 2


def solution(mesh):
    placed = (
        P("dp", None),
        P(),
        P(),
        P("dp", None),
        P("dp", None, "expert"),
        P("dp", "expert", None),
        P("dp", "expert"),
    )
    return jax.shard_map(
        functools.partial(shards, plan(mesh)),
        mesh=mesh,
        in_specs=placed,
        out_specs=(
            P("dp", "expert"),
            P("dp", "expert"),
            P("expert"),
            P(),
            P("dp", None, "expert"),
            P("dp", "expert", None),
        ),
        check_vma=False,
    )
```

```python
import functools

import jax
import jax.numpy as jnp
from jax import lax
from jax.experimental import pallas as pl
from jax.experimental.pallas import tpu as pltpu
from jax.sharding import PartitionSpec as P

EPS = 1e-05
F32 = jnp.float32
BF16 = jnp.bfloat16
MESH = pl.DeviceIdType.MESH
NN = (((1,), (0,)), ((), ()))
NT = (((1,), (1,)), ((), ()))


def dot(a, b, dims=NN):
    return lax.dot_general(a, b, dims, preferred_element_type=F32)


def loop(lo, hi, body):
    def step(i, carry):
        body(i)
        return carry

    lax.fori_loop(lo, hi, step, 0)


PARENT = {1: 0, 2: 0, 3: 2, 4: 0, 5: 4, 6: 4, 7: 6, 8: 6}
LAST = {1: 0, 2: 1, 4: 2}
FLAT = {1: 0, 2: 0, 3: 2, 4: 2, 5: 0, 6: 5, 7: 5, 8: 5}
TREES = (PARENT, FLAT)
PARTS = (2, 4)


def children(tree, d, most):
    return [k for k in range(1, most + 1) if tree[k] == d]


def kernel(
    dims,
    frames,
    gain,
    routerT,
    routesT,
    w_in,
    w_out,
    cot,
    mixed,
    dfr,
    dgain,
    drouter,
    gin,
    gout,
    rt,
    nb,
    cotb,
    sibcot,
    stats,
    p0t,
    p1t,
    pcomb,
    send_n,
    send_c,
    rows_a,
    rows_c,
    hid,
    gates,
    ga_t,
    d_t,
    prodb,
    retb,
    sib_p,
    sib_r,
    got_p,
    got_r,
    part,
    relay,
    fin,
    scal,
    logits_t,
    vw,
    sibvw,
    vz,
    vp,
    vout,
    tail,
    sib_s,
    sib_q,
    rt_sem,
    nrm_s,
    nrm_q,
    chain_s,
    cot_s0,
    cot_s1,
    cot_q,
    xy_s,
    xy_q,
    up_s,
    relay_q,
    fin_q,
    sc_s,
    sc_q,
    vz_s,
    vz_q,
):
    X, Y, ZL = dims
    NP = X * Y
    NZ = 2 * ZL
    T, D = frames.shape
    SL = send_n.shape[0]
    CAP = SL // NP
    E = routerT.shape[0]
    W = 128
    reach = (ZL, ZL - 1)
    dp = lax.axis_index("dp")
    ex = lax.axis_index("expert")
    p = lax.rem(dp, NP)
    zh = dp // NP
    zl = ex // 2
    c = lax.rem(ex, 2)
    z = zh * ZL + zl
    x = p // Y
    y = lax.rem(p, Y)
    r = lax.rem(z + NZ - ZL * c, NZ)
    own = r < ZL
    sib_id = (dp, zl * 2 + 1 - c)

    def z_id(to):
        return ((to // ZL) * NP + p, lax.rem(to, ZL) * 2 + c)

    def z_at(way, hops):
        return z_id(lax.rem(z + (hops if way == 0 else NZ - hops), NZ))

    right = z_at(0, 1)
    left = z_at(1, 1)

    def plane(k, sign):
        px = lax.rem(x + X + sign * (k // Y), X)
        py = lax.rem(y + Y + sign * lax.rem(k, Y), Y)
        return px * Y + py

    def plane_id(k):
        return (zh * NP + plane(k, 1), ex)

    def remote(src, dst, ssem, rsem, to):
        return pltpu.make_async_remote_copy(
            src_ref=src, dst_ref=dst, send_sem=ssem, recv_sem=rsem, device_id=to, device_id_type=MESH
        )

    def sib(src, dst, i):
        return remote(src, dst, sib_s.at[i], sib_q.at[i], sib_id)

    barrier = pltpu.get_barrier_semaphore()

    def greet(to):
        pl.semaphore_signal(barrier, inc=1, device_id=to, device_id_type=MESH)

    greet(sib_id)
    loop(1, NP, lambda k: greet(plane_id(k)))
    loop(1, NZ, lambda k: greet(z_id(lax.rem(z + k, NZ))))

    @pl.when(own)
    def _():
        step = T // 8

        def norm(i):
            at = pl.ds(pl.multiple_of(i * step, step), step)
            values = frames[at, :].astype(F32)
            mean = jnp.mean(values, axis=1, keepdims=True)
            centred = values - mean
            inverse = lax.rsqrt(jnp.mean(centred * centred, axis=1, keepdims=True) + EPS)
            normed = (centred * inverse * gain[...]).astype(BF16)
            for s in range(ZL):
                nb[s, at, :] = normed[:, s * W : (s + 1) * W]
            stats[0, at, :] = jnp.broadcast_to(mean, (step, W))
            stats[1, at, :] = jnp.broadcast_to(inverse, (step, W))

        loop(0, 8, norm)
        rt[...] = routesT[...]

    pl.semaphore_wait(barrier, NP + NZ - 1)

    cot_copy = sib(cot, sibcot, 0)
    rt_copy = remote(rt, rt, rt_sem.at[0], rt_sem.at[1], z_id(lax.rem(z + ZL, NZ)))

    def nrm(s, to):
        return remote(nb.at[s], nb.at[s], nrm_s.at[s], nrm_q.at[s], to)

    def pass_on(s, to):
        return remote(cotb.at[s], cotb.at[s], chain_s.at[s], cot_q.at[s], to)

    def cot_copy_to(s, sem, way, hops):
        return remote(cotb.at[s], cotb.at[s], sem, cot_q.at[s], z_at(way, hops))

    def inside(way, hops):
        return (r + hops < ZL) if way == 0 else (r >= hops)

    def to_other_block(s, act):
        pl.when(r == ZL - 1)(lambda: act(pass_on(s, right)))
        pl.when(r == 0)(lambda: act(pass_on(s, left)))

    def cot_source(act):
        s = lax.rem(r, ZL)
        for d in (4, 2, 1):
            for way in (0, 1):
                copy = cot_copy_to(s, cot_s0.at[way * 3 + LAST[d]], way, d)
                pl.when(inside(way, d))(functools.partial(act, copy))
        to_other_block(s, act)

    def cot_relay(d, act, wait=True):
        for way in (0, 1):

            @pl.when(inside(1 - way, d))
            def _():
                s = lax.rem(r + (NZ - d if way == 0 else d), NZ)
                if wait:
                    cot_copy_to(s, cot_s1.at[s, 0], way, 1).wait_recv()
                for far in (d + 2, d + 1):
                    if far < ZL and PARENT[far] == d:
                        copy = cot_copy_to(s, cot_s1.at[s, far - d - 1], way, far - d)
                        pl.when(inside(way, far - d))(functools.partial(act, copy))
                if way == 0:
                    pl.when(r == ZL - 1)(lambda: act(pass_on(s, right)))
                else:
                    pl.when(r == 0)(lambda: act(pass_on(s, left)))

    def start(copy):
        copy.start()

    def sent(copy):
        copy.wait_send()

    near = r < ZL + ZL // 2
    onward_r = near & (r >= ZL) & (r < ZL + ZL // 2 - 1)
    onward_l = r > ZL + ZL // 2

    def positions():
        r0 = rt[0:1, :].astype(F32)
        r1 = rt[1:2, :].astype(F32)
        lanes = lax.broadcasted_iota(jnp.int32, (E, T), 0).astype(F32)
        e0 = jnp.where(lanes == r0, 1.0, 0.0)
        e1 = jnp.where(lanes == r1, 1.0, 0.0)
        before = lax.broadcasted_iota(jnp.int32, (T, T), 0) < lax.broadcasted_iota(
            jnp.int32, (T, T), 1
        )
        counts = dot((e0 + e1).astype(BF16), jnp.where(before, 1.0, 0.0).astype(BF16))
        base = (zh * NP).astype(F32)
        for rk, ek, pt, first in ((r0, e0, p0t, True), (r1, e1, p1t, False)):
            slot = jnp.sum(ek * counts, axis=0, keepdims=True)
            pos = (rk - base) * CAP + slot
            posc = jnp.transpose(jnp.broadcast_to(pos, (W, T)))
            for b in range(SL // W):
                down = (lax.broadcasted_iota(jnp.int32, (W, T), 0) + b * W).astype(F32)
                pt[b * W : (b + 1) * W, :] = jnp.where(down == pos, 1.0, 0.0).astype(BF16)
                across = (lax.broadcasted_iota(jnp.int32, (T, W), 1) + b * W).astype(F32)
                hit = jnp.where(across == posc, 1.0, 0.0).astype(BF16)
                if first:
                    pcomb[:, b * W : (b + 1) * W] = hit
                else:
                    pcomb[:, b * W : (b + 1) * W] += hit

    def half_cols(h):
        return pl.ds(pl.multiple_of(h * (D // 2), D // 2), D // 2)

    def xy(a, h, src, dst, k):
        return remote(
            src.at[pl.ds(pl.multiple_of(plane(k, 1) * CAP, CAP), CAP), half_cols(h)],
            dst.at[pl.ds(pl.multiple_of(c * SL + p * CAP, CAP), CAP), half_cols(h)],
            xy_s.at[2 * a + h, k],
            xy_q.at[2 * a + h, k],
            plane_id(k),
        )

    def xy_arrival(a, h, dst, k):
        here = dst.at[
            pl.ds(pl.multiple_of(c * SL + plane(k, -1) * CAP, CAP), CAP), half_cols(h)
        ]
        return remote(here, here, xy_s.at[2 * a + h, k], xy_q.at[2 * a + h, k], plane_id(k))

    def to_slots(pieces, send, s):
        pt = p0t[...] + p1t[...]
        send[:, pl.ds(pl.multiple_of(s * W, W), W)] = dot(pt, pieces[s]).astype(BF16)

    def go(a, h, send, dst):
        loop(1, NP, lambda k: xy(a, h, send, dst, k).start())

    def keep(send, dst):
        mine = pl.ds(pl.multiple_of(p * CAP, CAP), CAP)
        dst[pl.ds(pl.multiple_of(c * SL + p * CAP, CAP), CAP), :] = send[mine, :]

    order = [d for d in (1, 2, 4, 3, 6, 5, 7) if d < ZL]
    chain_order = [0] + order
    enough = max(chain_order.index(d) for d in range(ZL // 2))

    @pl.when(own)
    def _():
        rt_copy.start()
        pl.when(r == ZL - 1)(lambda: loop(0, ZL, lambda i: nrm(ZL - 1 - i, right).start()))
        pl.when(r == 0)(lambda: loop(0, ZL, lambda s: nrm(s, left).start()))
        cot_copy.wait_recv()
        one, two = cot[...].astype(F32), sibcot[...].astype(F32)

        @pl.when(c == 0)
        def _():
            cotb[r, :, :] = jnp.transpose(jnp.concatenate([one, two], axis=0)).astype(BF16)

        @pl.when(c == 1)
        def _():
            cotb[r, :, :] = jnp.transpose(jnp.concatenate([two, one], axis=0)).astype(BF16)

        cot_source(start)
        positions()
        for h in (0, 1):
            loop(h * (ZL // 2), (h + 1) * (ZL // 2), lambda s: to_slots(nb, send_n, s))
            go(0, h, send_n, rows_a)
        for d in order:
            cot_relay(d, start)
        for h in (0, 1):
            loop(h * (ZL // 2), (h + 1) * (ZL // 2), lambda s: to_slots(cotb, send_c, s))
            go(1, h, send_c, rows_c)

    @pl.when(jnp.logical_not(own))
    def _():
        cot_copy.start()
        rt_copy.wait_recv()
        positions()
        first = jnp.where(near, 1, 0)

        def take(copy, i):
            s = jnp.where(near, ZL - 1 - i, i)
            copy(s, right).wait_recv()
            pl.when(onward_r)(lambda: copy(s, right).start())
            pl.when(onward_l)(lambda: copy(s, left).start())
            return s

        loop(0, ZL // 2, lambda i: to_slots(nb, send_n, take(nrm, i)))
        go(0, first, send_n, rows_a)
        loop(ZL // 2, ZL, lambda i: to_slots(nb, send_n, take(nrm, i)))
        go(0, 1 - first, send_n, rows_a)
        for n, i in enumerate(chain_order):
            to_slots(cotb, send_c, take(pass_on, i))
            if n == enough:
                go(1, first, send_c, rows_c)
        go(1, 1 - first, send_c, rows_c)

    keep(send_n, rows_a)
    keep(send_c, rows_c)

    half = pl.ds(pl.multiple_of(c * SL, SL), SL)
    away = pl.ds(pl.multiple_of((1 - c) * SL, SL), SL)
    RT = 128
    tiles = SL // RT
    mine_rows = pl.ds(pl.multiple_of(c * SL + p * CAP, CAP), CAP)
    here_rows = pl.ds(pl.multiple_of(p * CAP, CAP), CAP)

    a_copy = sib(rows_a.at[half], rows_a.at[half], 1)
    for h in (0, 1):
        loop(1, NP, lambda k: xy_arrival(0, h, rows_a, k).wait_recv())
    a_copy.start()
    weight_in = w_in[...]
    weight_out = w_out[...]
    router_row = routerT[pl.ds(dp, 1), :]
    router_hi = router_row.astype(BF16)
    router_lo = (router_row - router_hi.astype(F32)).astype(BF16)
    router_hi = jnp.broadcast_to(router_hi, (16, D))
    router_lo = jnp.broadcast_to(router_lo, (16, D))

    def forward(i):
        at = pl.ds(pl.multiple_of(i * RT, RT), RT)
        arrived = rows_a[at, :]
        hidden = dot(arrived, weight_in)
        logit = dot(arrived, router_hi, NT) + dot(arrived, router_lo, NT)
        gate = jax.nn.sigmoid(logit[:, 0:1])
        active = hidden * jax.nn.sigmoid(hidden)
        ga = active.astype(BF16).astype(F32) * (0.5 * gate)
        hid[at, :] = hidden
        gates[at, :] = jnp.broadcast_to(gate, (RT, W))
        ga_t[:, at] = jnp.transpose(ga).astype(BF16)
        prodb[at, :] = dot(ga.astype(BF16), weight_out).astype(BF16)

    def pair_sum(buf, other, i):
        at = pl.ds(pl.multiple_of(i * RT, RT), RT)
        mine = pl.ds(pl.multiple_of(c * SL + i * RT, RT), RT)
        buf[mine, :] = (buf[mine, :].astype(F32) + other[at, :].astype(F32)).astype(BF16)

    def part_cols(a, h):
        off = a * W
        step = D // PARTS[a]
        return pl.ds(off + h * step, step) if h else pl.ds(0, off + step)

    def give(a, h, src, dst, k):
        cols = part_cols(a, h)
        return remote(
            src.at[pl.ds(pl.multiple_of(c * SL + plane(k, 1) * CAP, CAP), CAP), cols],
            dst.at[here_rows, cols],
            xy_s.at[4 + 2 * a + h, k],
            xy_q.at[4 + 2 * a + h, k],
            plane_id(k),
        )

    def give_arrival(a, h, dst, k):
        here = dst.at[pl.ds(pl.multiple_of(plane(k, -1) * CAP, CAP), CAP), part_cols(a, h)]
        return remote(here, here, xy_s.at[4 + 2 * a + h, k], xy_q.at[4 + 2 * a + h, k], plane_id(k))

    p_copy = sib(prodb.at[away], sib_p, 3)
    sib(rows_a.at[away], rows_a.at[away], 1).wait_recv()
    loop(0, tiles, lambda i: forward((1 - c) * tiles + i))
    p_copy.start()
    loop(0, tiles, lambda i: forward(c * tiles + i))
    p_copy.wait_recv()
    loop(0, tiles, lambda i: pair_sum(prodb, sib_p, i))
    for h in (0, 1):
        loop(1, NP, lambda k: give(0, h, prodb, got_p, k).start())
    got_p[here_rows, :] = prodb[mine_rows, :]

    c_copy = sib(rows_c.at[half], rows_c.at[half], 2)
    for h in (0, 1):
        loop(1, NP, lambda k: xy_arrival(1, h, rows_c, k).wait_recv())
    c_copy.start()
    gain_hi = gain[...].astype(BF16)
    gain_lo = (gain[...] - gain_hi.astype(F32)).astype(BF16)
    gw = (
        dot(jnp.broadcast_to(gain_hi, (16, D)), weight_in)
        + dot(jnp.broadcast_to(gain_lo, (16, D)), weight_in)
    )[0:1, :]
    vw[...] = jnp.zeros_like(vw)
    lane = lax.broadcasted_iota(jnp.int32, (RT, W), 1)

    def backward(i):
        at = pl.ds(pl.multiple_of(i * RT, RT), RT)
        hidden = hid[at, :]
        gate = gates[at, 0:1]
        sig = jax.nn.sigmoid(hidden)
        up = dot(rows_c[at, :], weight_out, NT) * (0.5 * gate)
        dh = up * (sig * (1.0 + hidden * (1.0 - sig)))
        d_t[:, at] = jnp.transpose(dh).astype(BF16)
        dgg = jnp.sum(up * (hidden * sig), axis=1, keepdims=True)
        s1 = jnp.sum(dh * gw, axis=1, keepdims=True)
        s2 = jnp.sum(dh * hidden, axis=1, keepdims=True)
        back = dot(dh.astype(BF16), weight_in, NT)
        retb[at, W : W + D] = back.astype(BF16)
        retb[at, 0:W] = jnp.where(
            lane == 0, dgg, jnp.where(lane == 1, s1, jnp.where(lane == 2, s2, 0.0))
        ).astype(BF16)
        wide = rows_a[at, :].astype(F32)
        v = jnp.sum(wide * (dgg * (1.0 - gate)), axis=0, keepdims=True)
        w = jnp.sum(wide * back, axis=0, keepdims=True)
        for b in range(D // W):
            vw[0, b : b + 1, :] += v[:, b * W : (b + 1) * W]
            vw[1, b : b + 1, :] += w[:, b * W : (b + 1) * W]

    r_copy = sib(retb.at[away], sib_r, 4)
    sib(rows_c.at[away], rows_c.at[away], 2).wait_recv()
    loop(0, tiles, lambda i: backward((1 - c) * tiles + i))
    r_copy.start()
    loop(0, tiles, lambda i: backward(c * tiles + i))
    v_copy = sib(vw.at[1 - c], sibvw, 5)
    v_copy.start()
    r_copy.wait_recv()
    loop(0, tiles, lambda i: pair_sum(retb, sib_r, i))
    for h in range(PARTS[1]):
        loop(1, NP, lambda k: give(1, h, retb, got_r, k).start())
    got_r[here_rows, :] = retb[mine_rows, :]

    v_copy.wait_recv()
    vz[z, :, :] = vw[c, :, :] + sibvw[...]

    def v_send(k):
        return remote(vz.at[z], vz.at[z], vz_s.at[0, k], vz_q.at[0, k], z_id(lax.rem(z + k, NZ)))

    def v_arrival(k):
        here = vz.at[lax.rem(z + NZ - k, NZ)]
        return remote(here, here, vz_s.at[0, k], vz_q.at[0, k], z_id(lax.rem(z + k, NZ)))

    loop(1, NZ, lambda k: v_send(k).start())

    def up(a, d, lo, hi, act, run=True):
        tree = TREES[a]
        for way in (0, 1):
            if d > reach[way]:
                continue
            to = lax.rem(r + (d if way == 0 else NZ - d), NZ)

            @pl.when((to >= lo) & (to < hi))
            def _():
                s = lax.rem(to, ZL)
                pd = tree[d]
                q = children(tree, pd, reach[way]).index(d)
                if pd == 0:
                    dst, sem = fin.at[a, way * 3 + q], fin_q.at[a, way * 3 + q]
                else:
                    dst, sem = relay.at[a, s, q], relay_q.at[a, s, q]
                if run:
                    kids = children(tree, d, reach[way])
                    total = None
                    for n in range(len(kids)):
                        landed = relay.at[a, s, n]
                        remote(landed, landed, up_s.at[a, s], relay_q.at[a, s, n], right).wait_recv()
                        if total is None:
                            total = part[a, s, :, :].astype(F32)
                        total = total + relay[a, s, n, :, :].astype(F32)
                    if kids:
                        part[a, s, :, :] = total.astype(BF16)
                act(remote(part.at[a, s], dst, up_s.at[a, s], sem, z_at(way, d - pd)))

    def combine(a, h, got):
        count = ZL // PARTS[a]
        first = h * count

        def one(i):
            s = first + i
            at = pl.ds(pl.multiple_of(a * W + s * W, W), W)
            part[a, s, :, :] = dot(pcomb[...], got[:, at]).astype(BF16)

        loop(1, NP, lambda k: give_arrival(a, h, got, k).wait_recv())
        loop(0, count, one)
        for d in (8, 7, 6, 5, 4, 3, 1, 2):
            if d <= ZL and not children(TREES[a], d, 8):
                up(a, d, first, first + count, start)

    def relays(a, ds, lo, hi):
        for d in ds:
            if d <= ZL:
                up(a, d, lo, hi, start)

    combine(0, 0, got_p)
    combine(0, 1, got_p)

    def grads(i):
        at = pl.ds(pl.multiple_of(i * W, W), W)
        gout[:, at] = dot(ga_t[...], rows_c[:, at]).astype(BF16)
        gin[at, :] = jnp.transpose(dot(d_t[...], rows_a[:, at])).astype(BF16)

    loop(0, D // W // 2, grads)

    def vp_send(k):
        return remote(vp.at[p], vp.at[p], vz_s.at[1, k], vz_q.at[1, k], plane_id(k))

    def vp_arrival(k):
        here = vp.at[plane(k, -1)]
        return remote(here, here, vz_s.at[1, k], vz_q.at[1, k], plane_id(k))

    router_all = routerT[...]

    @pl.when(own)
    def _():
        router_h = router_all.astype(BF16)
        router_l = (router_all - router_h.astype(F32)).astype(BF16)
        logits = jnp.zeros((E, T), F32)
        for b in range(ZL):
            at = slice(b * W, (b + 1) * W)
            logits += dot(router_h[:, at], nb[b], NT) + dot(router_l[:, at], nb[b], NT)
        logits_t[...] = logits

    relays(0, (6, 2), 0, ZL)
    loop(D // W // 2, D // W, grads)

    combine(1, 0, got_r)
    extra = jnp.transpose(got_r[:, 0:W].astype(F32)).astype(BF16)
    t0 = dot(extra, p0t[...])
    t1 = dot(extra, p1t[...])
    scal[z, 0:1, :] = t0[0:1, :]
    scal[z, 1:2, :] = t1[0:1, :]
    scal[z, 2:4, :] = t0[1:3, :] + t1[1:3, :]

    def sc_copy(s):
        to = lax.rem(s + ZL * c, NZ)
        return remote(scal.at[z], scal.at[z], sc_s.at[s], sc_q.at[z], z_id(to))

    def sc_arrival(k):
        here = scal.at[k]
        return remote(here, here, sc_s.at[0], sc_q.at[k], right)

    loop(0, ZL, lambda s: pl.when(s != r)(lambda: sc_copy(s).start()))
    relays(0, (4,), 0, ZL)
    loop(1, NZ, lambda k: v_arrival(k).wait_recv())
    vp[p, 0, :, :] = jnp.sum(vz[0:ZL], axis=0)
    vp[p, 1, :, :] = jnp.sum(vz[ZL:NZ], axis=0)
    loop(1, NP, lambda k: vp_send(k).start())
    quarter = ZL // PARTS[1]

    def relays_q(h):
        relays(1, (5, 2), h * quarter, (h + 1) * quarter)

    combine(1, 1, got_r)
    combine(1, 2, got_r)
    relays_q(0)

    loop(1, NP, lambda k: vp_arrival(k).wait_recv())
    vp_copy = sib(vp, vout.at[c], 6)
    vp_copy.start()
    vout[c, :, :, :, :] = vp[...]

    combine(1, 3, got_r)
    relays_q(1)

    cols = pl.ds(pl.multiple_of(zl * W, W), W)
    sib(vp, vout.at[1 - c], 6).wait_recv()
    for q in range(NP):
        for up_half in (0, 1):
            e = up_half * NP + q
            for b in range(D // W):
                drouter[e : e + 1, b * W : (b + 1) * W] = vout[0, q, up_half, b : b + 1, :] * (1.0 / T)
    sibvw[...] = jnp.sum(jnp.sum(vout[1], axis=0), axis=0) * (1.0 / T)
    d_gain = sibvw[pl.ds(zl, 1), :] + jnp.sum(
        routerT[:, cols] * drouter[:, cols], axis=0, keepdims=True
    )
    d_gain = d_gain / gain[:, cols]

    @pl.when(c == 0)
    def _():
        dgain[...] = d_gain[:, 0 : W // 2]

    @pl.when(c == 1)
    def _():
        dgain[...] = d_gain[:, W // 2 : W]

    relays_q(2)
    relays_q(3)

    t_copy = sib(tail, tail, 7)

    @pl.when(own)
    def _():
        s = lax.rem(r, ZL)
        logits = logits_t[...]
        r0 = rt[0:1, :].astype(F32)
        r1 = rt[1:2, :].astype(F32)
        ids = lax.broadcasted_iota(jnp.int32, (E, T), 0).astype(F32)
        rg = jnp.sum(router_all * gain[...], axis=1, keepdims=True)

        def sc_wait(k):
            pl.when(k != z)(lambda: sc_arrival(k).wait_recv())

        loop(0, NZ, sc_wait)
        total = jnp.sum(scal[...], axis=0)
        dl = jnp.where(ids == r0, total[0:1, :], 0.0) + jnp.where(ids == r1, total[1:2, :], 0.0)
        dl = dl * (1.0 - jax.nn.sigmoid(logits))
        sum_1 = total[2:3, :] + jnp.sum(dl * rg, axis=0, keepdims=True)
        sum_2 = total[3:4, :] + jnp.sum(dl * logits, axis=0, keepdims=True)
        sum_1 = jnp.transpose(jnp.broadcast_to(sum_1, (W, T))) * (1.0 / D)
        sum_2 = jnp.transpose(jnp.broadcast_to(sum_2, (W, T))) * (1.0 / D)
        dl_c = jnp.transpose(jnp.concatenate([dl, jnp.zeros((W - E, T), F32)], axis=0))
        router_cols = jnp.concatenate([routerT[:, cols], jnp.zeros((W - E, W), F32)], axis=0)
        second = dot(dl_c.astype(BF16), router_cols.astype(BF16))
        values = frames[:, cols].astype(F32)
        inverse = stats[1]
        scaled = (values - stats[0]) * inverse

        def arrived_sum(a):
            total = part[a, s, :, :].astype(F32)
            for way in (0, 1):
                for q in range(len(children(TREES[a], 0, reach[way]))):
                    landed = fin.at[a, way * 3 + q]
                    sem = fin_q.at[a, way * 3 + q]
                    remote(landed, landed, up_s.at[a, s], sem, right).wait_recv()
                    total = total + fin[a, way * 3 + q, :, :].astype(F32)
            return total

        out_m = jnp.transpose(values + arrived_sum(0)).astype(BF16)
        d_scaled = (arrived_sum(1) + second) * gain[:, cols]
        result = cotb[s, :, :].astype(F32) + inverse * (d_scaled - sum_1 - scaled * sum_2)
        out_d = jnp.transpose(result).astype(BF16)

        @pl.when(c == 0)
        def _():
            tail[0, :, :] = out_m[W // 2 : W, :]
            tail[1, :, :] = out_d[W // 2 : W, :]
            mixed[...] = out_m[0 : W // 2, :]
            dfr[...] = out_d[0 : W // 2, :]

        @pl.when(c == 1)
        def _():
            tail[0, :, :] = out_m[0 : W // 2, :]
            tail[1, :, :] = out_d[0 : W // 2, :]
            mixed[...] = out_m[W // 2 : W, :]
            dfr[...] = out_d[W // 2 : W, :]

        t_copy.start()

    @pl.when(jnp.logical_not(own))
    def _():
        t_copy.wait_recv()
        mixed[...] = tail[0, :, :]
        dfr[...] = tail[1, :, :]

    @pl.when(own)
    def _():
        t_copy.wait_send()
        rt_copy.wait_send()
        pl.when(r == ZL - 1)(lambda: loop(0, ZL, lambda s: nrm(s, right).wait_send()))
        pl.when(r == 0)(lambda: loop(0, ZL, lambda s: nrm(s, left).wait_send()))
        cot_source(sent)
        for d in order:
            cot_relay(d, sent, wait=False)

    @pl.when(jnp.logical_not(own))
    def _():
        cot_copy.wait_send()
        pl.when(onward_r | onward_l)(
            lambda: loop(0, ZL, lambda s: (nrm(s, right).wait_send(), pass_on(s, right).wait_send()))
        )

    def last_xy(k):
        for h in (0, 1):
            xy(0, h, send_n, rows_a, k).wait_send()
            xy(1, h, send_c, rows_c, k).wait_send()
            give(0, h, prodb, got_p, k).wait_send()
        for h in range(PARTS[1]):
            give(1, h, retb, got_r, k).wait_send()
        vp_send(k).wait_send()

    loop(1, NP, last_xy)
    loop(1, NZ, lambda k: v_send(k).wait_send())
    loop(0, ZL, lambda s: pl.when(s != r)(lambda: sc_copy(s).wait_send()))
    for d in range(1, ZL + 1):
        for a in (0, 1):
            up(a, d, 0, ZL, sent, run=False)
    for copy in (a_copy, c_copy, p_copy, r_copy, v_copy, vp_copy):
        copy.wait_send()


def shards(dims, frames, norm_gain, router, routes, w_in, w_out, cotangent):
    X, Y, ZL = dims
    NP, NZ, W = X * Y, 2 * ZL, 128
    T, D = frames.shape
    E = router.shape[1]
    CAP = 4 * routes.shape[1] * T // (3 * E)
    SL = NP * CAP
    HS = w_in.shape[2]
    vmem = pl.BlockSpec(memory_space=pltpu.VMEM)
    dma = pltpu.SemaphoreType.DMA
    mixed, dfr, d_gain, d_router, gin, gout = pl.pallas_call(
        functools.partial(kernel, dims),
        out_shape=[
            jax.ShapeDtypeStruct((W // 2, T), BF16),
            jax.ShapeDtypeStruct((W // 2, T), BF16),
            jax.ShapeDtypeStruct((1, W // 2), F32),
            jax.ShapeDtypeStruct((E, D), F32),
            jax.ShapeDtypeStruct((D, HS), BF16),
            jax.ShapeDtypeStruct((HS, D), BF16),
        ],
        in_specs=[vmem] * 7,
        out_specs=[vmem] * 6,
        scratch_shapes=[
            pltpu.VMEM((routes.shape[1], T), jnp.int32),
            pltpu.VMEM((ZL, T, W), BF16),
            pltpu.VMEM((ZL, T, W), BF16),
            pltpu.VMEM((W // 2, T), BF16),
            pltpu.VMEM((2, T, W), F32),
            pltpu.VMEM((SL, T), BF16),
            pltpu.VMEM((SL, T), BF16),
            pltpu.VMEM((T, SL), BF16),
            pltpu.VMEM((SL, D), BF16),
            pltpu.VMEM((SL, D), BF16),
            pltpu.VMEM((2 * SL, D), BF16),
            pltpu.VMEM((2 * SL, D), BF16),
            pltpu.VMEM((2 * SL, HS), F32),
            pltpu.VMEM((2 * SL, W), F32),
            pltpu.VMEM((HS, 2 * SL), BF16),
            pltpu.VMEM((HS, 2 * SL), BF16),
            pltpu.VMEM((2 * SL, D), BF16),
            pltpu.VMEM((2 * SL, D + W), BF16),
            pltpu.VMEM((SL, D), BF16),
            pltpu.VMEM((SL, D + W), BF16),
            pltpu.VMEM((SL, D), BF16),
            pltpu.VMEM((SL, D + W), BF16),
            pltpu.VMEM((2, ZL, T, W), BF16),
            pltpu.VMEM((2, ZL, 3, T, W), BF16),
            pltpu.VMEM((2, 6, T, W), BF16),
            pltpu.VMEM((NZ, 4, T), F32),
            pltpu.VMEM((E, T), F32),
            pltpu.VMEM((2, D // W, W), F32),
            pltpu.VMEM((D // W, W), F32),
            pltpu.VMEM((NZ, D // W, W), F32),
            pltpu.VMEM((NP, 2, D // W, W), F32),
            pltpu.VMEM((2, NP, 2, D // W, W), F32),
            pltpu.VMEM((2, W // 2, T), BF16),
            dma((8,)),
            dma((8,)),
            dma((2,)),
            dma((ZL,)),
            dma((ZL,)),
            dma((ZL,)),
            dma((6,)),
            dma((ZL, 2)),
            dma((ZL,)),
            dma((10, NP)),
            dma((10, NP)),
            dma((2, ZL)),
            dma((2, ZL, 3)),
            dma((2, 6)),
            dma((ZL,)),
            dma((NZ,)),
            dma((2, max(NP, NZ))),
            dma((2, max(NP, NZ))),
        ],
        compiler_params=pltpu.CompilerParams(
            collective_id=0, has_side_effects=True, vmem_limit_bytes=56 * 1024 * 1024
        ),
        name="experts",
    )(
        frames,
        norm_gain.reshape(1, D),
        router.T,
        routes.T,
        w_in.reshape(D, HS),
        w_out.reshape(HS, D),
        cotangent.T,
    )
    d_gain = d_gain.reshape(W // 2)
    return mixed.T, dfr.T, d_gain, d_router.T, gin.reshape(1, D, HS), gout.reshape(1, HS, D)


def plan(mesh):
    dp, ex = mesh.shape["dp"], mesh.shape["expert"]
    side = 4 if dp == 32 else 2
    return side, dp // 2 // side, ex // 2


def solution(mesh):
    placed = (
        P("dp", None),
        P(),
        P(),
        P("dp", None),
        P("dp", None, "expert"),
        P("dp", "expert", None),
        P("dp", "expert"),
    )
    return jax.shard_map(
        functools.partial(shards, plan(mesh)),
        mesh=mesh,
        in_specs=placed,
        out_specs=(
            P("dp", "expert"),
            P("dp", "expert"),
            P("expert"),
            P(),
            P("dp", None, "expert"),
            P("dp", "expert", None),
        ),
        check_vma=False,
    )
```
